32 devices in a mesh: fsdp: 16 (over z, y, x), tp: 2 (over core).
Axes of the slice: x: 2, y: 2, z: 4, core: 2. Of those that a mesh axis runs over, the one named last changes fastest.
Arguments:
- hidden: bfloat16 [8192, 1536], P(('fsdp', 'tp')), may hold values from -6 to 6
- document_index: int32 [8192], replicated, may hold values from 0 to 8192, as said below
- attn_gain: bfloat16 [1, 1536], P(None, 'fsdp'), may hold values from 0.25 to 1.75
- q_weight: bfloat16 [1, 1536, 1536], P(None, 'fsdp', 'tp'), may hold values from -0.21875 to 0.21875
- key_matrix: bfloat16 [1, 1536, 768], P(None, 'fsdp', 'tp'), may hold values from -0.21875 to 0.21875
- value_matrix: bfloat16 [1, 1536, 768], P(None, 'fsdp', 'tp'), may hold values from -0.15625 to 0.15625
- out_weight: bfloat16 [1, 1536, 1536], P(None, 'fsdp', 'tp'), may hold values from -0.625 to 0.625
- mlp_gain: bfloat16 [1, 1536], P(None, 'fsdp'), may hold values from 0.25 to 1.75
- gate_weight: bfloat16 [1, 1536, 4096], P(None, 'fsdp', 'tp'), may hold values from -0.15625 to 0.15625
- up_weight: bfloat16 [1, 1536, 4096], P(None, 'fsdp', 'tp'), may hold values from -0.15625 to 0.15625
- down_weight: bfloat16 [1, 1536, 4096], P(None, 'fsdp', 'tp'), may hold values from -0.125 to 0.125
- cotangent: bfloat16 [8192, 1536], P(('fsdp', 'tp')), may hold values from -6 to 6
Outputs:
- output: bfloat16 [8192, 1536], P(('fsdp', 'tp'))
- input_grad: float32 [8192, 1536], P(('fsdp', 'tp'))
- attn_gain_grad: float32 [1, 1536], P(None, 'fsdp')
- q_grad: float32 [1, 1536, 1536], P(None, 'fsdp', 'tp')
- k_grad: float32 [1, 1536, 768], P(None, 'fsdp', 'tp')
- v_grad: float32 [1, 1536, 768], P(None, 'fsdp', 'tp')
- out_grad: float32 [1, 1536, 1536], P(None, 'fsdp', 'tp')
- mlp_gain_grad: float32 [1, 1536], P(None, 'fsdp')
- gate_grad: float32 [1, 1536, 4096], P(None, 'fsdp', 'tp')
- up_grad: float32 [1, 1536, 4096], P(None, 'fsdp', 'tp')
- down_grad: float32 [1, 1536, 4096], P(None, 'fsdp', 'tp')
The draws below stay inside these ranges and needn't reach their ends.
Inputs may be any that keep to these rules, and one draw needn't show every extreme that they name: `document_index`: sequence s holds ids 0 and ids in (s * 4096, (s + 1) * 4096]; its last document has id (s + 1) * 4096. A document is a run of one nonzero id, and ids never fall inside a sequence except to 0. Every sequence ends with 1 to 128 padding tokens of id 0. In every sequence one document starts within its first 257 tokens and ends within its last 512 tokens; the others start at random places.
All inputs are finite; a program needn't handle non-finite values.
Results may differ from the reference program's by a relative error of at most 0.015.
The reference program's roundings to bfloat16 on the way count: a program that leaves them out, or rounds other values in their place, can miss the bound.
Values may be sent and summed in bfloat16 or wider, within the bound.
No kernel may reach another device: no remote copies, remote signals or barrier semaphores. Data moves between devices by JAX's collectives and lax.ppermute only.
A program may use at most 256 MiB of HBM per device.

```python
import jax
import jax.numpy as jnp
from jax import lax

MODEL_WIDTH = 1536
QUERY_HEADS = 16
KEY_VALUE_HEADS = 8
HEAD_SIZE = 96
FF = 4096
DECODER_LAYERS = 1
SPAN = 512
PACKED_LENGTH = 4096
TOKENS = 8192


def draw_document_index(key, part):
    key = jax.random.fold_in(key, 7)
    count = TOKENS // PACKED_LENGTH
    key_start, key_pad, key_tail, key_marks = jax.random.split(key, 4)
    begin = jax.random.randint(key_start, (count, 1), 1, SPAN // 2 + 1)
    padding = jax.random.randint(key_pad, (count, 1), 1, SPAN // 4 + 1)
    tail = jax.random.randint(key_tail, (count, 1), 2, SPAN // 2 + 1)
    finish = PACKED_LENGTH - padding - tail
    marks = jax.random.randint(key_marks, (count, PACKED_LENGTH), 0, 24) == 0
    index = jnp.arange(PACKED_LENGTH, dtype=jnp.int32)[None, :]
    inside = (index >= begin) & (index < finish)
    filled = index < PACKED_LENGTH - padding
    cuts = (index == 0) | (index == begin) | (index == finish) | marks & jnp.logical_not(inside)
    number = jnp.cumsum(cuts.astype(jnp.int32), axis=1)
    last = jnp.max(jnp.where(filled, number, 0), axis=1, keepdims=True)
    offset = jnp.arange(count, dtype=jnp.int32)[:, None] * PACKED_LENGTH
    return jnp.where(filled, number + offset + PACKED_LENGTH - last, 0).reshape(-1).astype(jnp.int32)


def strengthened(entries, key, source, target, parts, factor):
    def block_of(position):
        return (jnp.arange(entries.shape[position]) // (entries.shape[position] // parts)).reshape((-1,) + (1,) * (entries.ndim - 1 - position))

    first = jax.random.permutation(key, parts)[block_of(target)]
    far = (block_of(target) + parts // 2) % parts
    return jnp.where((block_of(source) == first) | (block_of(source) == far), factor * entries, entries)


def block_scale(key, extent, pieces, low, high):
    loudness = 1.0
    for dim, parts in pieces:
        heights = jax.random.uniform(jax.random.fold_in(jax.random.fold_in(key, 6), dim), (parts,), jnp.float32, low / len(pieces), high / len(pieces))
        loudness = loudness * jnp.repeat(jnp.exp(heights), extent[dim] // parts).reshape((-1,) + (1,) * (len(extent) - 1 - dim))
    return loudness


def centred(key, extent, deviation, reach, pieces=(), held_as=jnp.bfloat16):
    level = block_scale(key, extent, pieces, -0.22, 0.18) if pieces else 1.0
    entries = jax.random.normal(key, extent, jnp.float32) * deviation * level
    return jnp.minimum(jnp.maximum(entries, -reach), reach).astype(held_as)


def gaussian_with(key, dims, spread, reach, pieces, heavy, kind=jnp.bfloat16):
    drawn = spread * jax.random.normal(key, dims, jnp.float32)
    if pieces:
        drawn = drawn * block_scale(key, dims, pieces, -0.22, 0.18)
    return jnp.clip(strengthened(drawn, jax.random.fold_in(key, 3), *heavy), -reach, reach).astype(kind)


def setup_inputs(seed: int = 0) -> dict:
    key_of = jax.random.split(jax.random.key(seed), 13)
    hidden = gaussian_with(key_of[0], (TOKENS, MODEL_WIDTH), 1.0, 6.0, ((0, 32),), (0, 1, 32, 2.75))
    document_index = draw_document_index(jax.random.fold_in(key_of[12], 71), 0)
    attn_gain = jnp.clip(1.0 + 0.15 * jax.random.normal(key_of[2], (DECODER_LAYERS, MODEL_WIDTH), jnp.float32), 0.25, 1.75).astype(jnp.bfloat16)
    q_weight = centred(key_of[3], (DECODER_LAYERS, MODEL_WIDTH, QUERY_HEADS * HEAD_SIZE), (MODEL_WIDTH // 2) ** -0.5, 0.21875, ((1, 16), (2, 2)))
    key_matrix = centred(key_of[4], (DECODER_LAYERS, MODEL_WIDTH, KEY_VALUE_HEADS * HEAD_SIZE), (MODEL_WIDTH // 2) ** -0.5, 0.21875, ((1, 16), (2, 2)))
    value_matrix = centred(key_of[5], (DECODER_LAYERS, MODEL_WIDTH, KEY_VALUE_HEADS * HEAD_SIZE), MODEL_WIDTH ** -0.5, 0.15625, ((1, 16), (2, 2)))
    out_weight = centred(key_of[6], (DECODER_LAYERS, MODEL_WIDTH, QUERY_HEADS * HEAD_SIZE), (QUERY_HEADS * HEAD_SIZE // 16) ** -0.5, 0.625, ((1, 16), (2, 2)))
    mlp_gain = jnp.clip(1.0 + 0.15 * jax.random.normal(key_of[7], (DECODER_LAYERS, MODEL_WIDTH), jnp.float32), 0.25, 1.75).astype(jnp.bfloat16)
    gate_weight = centred(key_of[8], (DECODER_LAYERS, MODEL_WIDTH, FF), MODEL_WIDTH ** -0.5, 0.15625, ((1, 16), (2, 2)))
    up_weight = centred(key_of[9], (DECODER_LAYERS, MODEL_WIDTH, FF), MODEL_WIDTH ** -0.5, 0.15625, ((1, 16), (2, 2)))
    down_weight = centred(key_of[10], (DECODER_LAYERS, MODEL_WIDTH, FF), (FF // 2) ** -0.5, 0.125, ((1, 16), (2, 2)))
    cotangent = gaussian_with(key_of[11], (TOKENS, MODEL_WIDTH), 1.0, 6.0, ((0, 32),), (0, 1, 32, 2.75))
    return dict(hidden=hidden, document_index=document_index, attn_gain=attn_gain, q_weight=q_weight, key_matrix=key_matrix, value_matrix=value_matrix, out_weight=out_weight, mlp_gain=mlp_gain, gate_weight=gate_weight, up_weight=up_weight, down_weight=down_weight, cotangent=cotangent)


rope_base = 100000.0
norm_eps = 1e-05

@jax.custom_vjp
def low_precision(v):
    return lax.optimization_barrier(v.astype(jnp.bfloat16)).astype(jnp.float32)

@jax.custom_vjp
def low_precision_backward(v):
    return v

def low_keep(v):
    return (low_precision(v), None)

def low_pass(kept, grad):
    return (grad,)

def back_keep(v):
    return (v, None)

def back_low(kept, grad):
    return (low_precision(grad),)
low_precision.defvjp(low_keep, low_pass)
low_precision_backward.defvjp(back_keep, back_low)

def highest_precision(left, right):
    return jnp.dot(left, right, precision=lax.Precision.HIGHEST)

def rms_scaled(stream, gain):
    return stream * lax.rsqrt(lax.optimization_barrier(jnp.mean(stream * stream, axis=-1, keepdims=True)) + norm_eps) * gain

def apply_rotary(values_in, token_positions):
    half = values_in.shape[-1] // 2
    freq = rope_base ** (-2.0 * jnp.arange(half, dtype=jnp.float32) / values_in.shape[-1])
    angle = token_positions.astype(jnp.float32)[:, None] * freq[None, :]
    cosine = jnp.cos(angle)[:, None, :]
    sine = jnp.sin(angle)[:, None, :]
    first = values_in[..., :half]
    second = values_in[..., half:]
    return jnp.concatenate([first * cosine - second * sine, second * cosine + first * sine], axis=-1)

def positions_within(document_index):
    table = document_index.reshape(-1, PACKED_LENGTH)
    index = jnp.arange(PACKED_LENGTH, dtype=jnp.int32)
    before = jnp.concatenate([jnp.full((table.shape[0], 1), -1, jnp.int32), table[:, :-1]], axis=1)
    starts = lax.cummax(jnp.where(table != before, index[None, :], 0), axis=1)
    return (index[None, :] - starts).reshape(-1)

def attend_packed_sequence(packed):
    query_rows, every_key, every_value, seq_ids = packed
    block = min(512, PACKED_LENGTH)
    count = PACKED_LENGTH // block
    key_index = jnp.arange(PACKED_LENGTH, dtype=jnp.int32)
    scale = query_rows.shape[-1] ** (-0.5)

    @jax.checkpoint
    def one_block(start):
        rows_q = lax.dynamic_slice_in_dim(query_rows, start, block, 0)
        row_ids = lax.dynamic_slice_in_dim(seq_ids, start, block, 0)
        row_index = start + jnp.arange(block, dtype=jnp.int32)
        raw = jnp.einsum('qkgd,skd->kgqs', rows_q, every_key, precision=lax.Precision.HIGHEST)
        scores = low_precision_backward(raw * scale)
        allowed = (row_ids[:, None] == seq_ids[None, :]) & (key_index[None, :] <= row_index[:, None])
        scores = jnp.where(allowed[None, None], scores, -1000000000.0)
        largest = lax.optimization_barrier(jnp.max(scores, axis=-1, keepdims=True))
        weights = jnp.exp(scores - largest)
        probs = weights / lax.optimization_barrier(jnp.sum(weights, axis=-1, keepdims=True))
        return jnp.einsum('kgqs,skd->qkgd', low_precision(probs), every_value, precision=lax.Precision.HIGHEST)
    starts = jnp.arange(count, dtype=jnp.int32) * block
    result = lax.map(one_block, starts)
    return result.reshape(PACKED_LENGTH, -1)

def forward(stream, attn_gain, q_weight, key_matrix, value_matrix, out_weight, mlp_gain, gate_weight, up_weight, down_weight, token_positions, document_index):
    token_row_count = stream.shape[0]
    sequence_count = token_row_count // PACKED_LENGTH
    for decoder_layer_index in range(DECODER_LAYERS):
        normalized_input = low_precision(rms_scaled(stream, attn_gain[decoder_layer_index]))
        query_rows = low_precision(apply_rotary(low_precision_backward(highest_precision(normalized_input, q_weight[decoder_layer_index])).reshape(token_row_count, QUERY_HEADS, HEAD_SIZE), token_positions))
        every_key = low_precision(apply_rotary(low_precision_backward(highest_precision(normalized_input, key_matrix[decoder_layer_index])).reshape(token_row_count, KEY_VALUE_HEADS, HEAD_SIZE), token_positions))
        every_value = low_precision(low_precision_backward(highest_precision(normalized_input, value_matrix[decoder_layer_index]))).reshape(token_row_count, KEY_VALUE_HEADS, HEAD_SIZE)
        grouped_heads = query_rows.reshape(sequence_count, PACKED_LENGTH, KEY_VALUE_HEADS, QUERY_HEADS // KEY_VALUE_HEADS, HEAD_SIZE)
        mixed_heads = lax.map(attend_packed_sequence, (grouped_heads, every_key.reshape(sequence_count, PACKED_LENGTH, KEY_VALUE_HEADS, HEAD_SIZE), every_value.reshape(sequence_count, PACKED_LENGTH, KEY_VALUE_HEADS, HEAD_SIZE), document_index.reshape(sequence_count, PACKED_LENGTH)))
        attended = low_precision(low_precision_backward(mixed_heads.reshape(token_row_count, QUERY_HEADS * HEAD_SIZE)))
        stream = stream + low_precision_backward(highest_precision(attended, out_weight[decoder_layer_index].T))
        normed_m = low_precision(rms_scaled(stream, mlp_gain[decoder_layer_index]))
        gate = low_precision_backward(highest_precision(normed_m, gate_weight[decoder_layer_index]))
        up_part = low_precision_backward(highest_precision(normed_m, up_weight[decoder_layer_index]))
        act = low_precision(gate / (1.0 + jnp.exp(-gate)) * up_part)
        stream = stream + low_precision_backward(highest_precision(act, down_weight[decoder_layer_index].T))
    return stream

def reference(hidden, document_index, attn_gain, q_weight, key_matrix, value_matrix, out_weight, mlp_gain, gate_weight, up_weight, down_weight, cotangent):
    token_positions = positions_within(document_index)
    params = tuple((weight.astype(jnp.float32) for weight in (attn_gain, q_weight, key_matrix, value_matrix, out_weight, mlp_gain, gate_weight, up_weight, down_weight)))

    def run(stream, attn_g, q_w, k_w, v_w, o_w, mlp_g, gate_w, up_w, down_w):
        return forward(stream, attn_g, q_w, k_w, v_w, o_w, mlp_g, gate_w, up_w, down_w, token_positions, document_index)
    output, pullback = jax.vjp(run, hidden.astype(jnp.float32), *params)
    start_grad = cotangent.astype(jnp.float32) * (document_index != 0).astype(jnp.float32)[:, None]
    grads = pullback(start_grad)
    return (output.astype(jnp.bfloat16), grads[0], grads[1], grads[2], grads[3], grads[4], grads[5], grads[6], grads[7], grads[8], grads[9])
```

```python
import functools
import math

import jax
import jax.numpy as jnp
from jax import lax
from jax.experimental import pallas as pl
from jax.experimental.pallas import tpu as pltpu
from jax.sharding import PartitionSpec as P

HEAD_SIZE = 96
HALF = HEAD_SIZE // 2
SPANS = 8
PLANE = 4
PACKED_LENGTH = 4096
SPAN = PACKED_LENGTH // SPANS

rope_base = 100000.0
norm_eps = 1e-05
masked_score = -1000000000.0
scale = HEAD_SIZE ** (-0.5)
scale_log2 = scale * math.log2(math.e)
bf16 = jnp.bfloat16
f32 = jnp.float32


def dot(left, right, left_dim=1, right_dim=0):
    return lax.dot_general(
        left, right, (((left_dim,), (right_dim,)), ((), ())), preferred_element_type=f32
    )


def hop(value, distance):
    count = lax.axis_size("fsdp")
    return lax.ppermute(value, "fsdp", [(i, i ^ distance) for i in range(count)])


def swap(value):
    return lax.ppermute(value, "tp", [(0, 1), (1, 0)])


def groups_of(size):
    count = lax.axis_size("fsdp")
    return [list(range(first, first + size)) for first in range(0, count, size)]


def exchange(value, size):
    groups = None if size == lax.axis_size("fsdp") else groups_of(size)
    return lax.all_to_all(value, "fsdp", 0, 0, axis_index_groups=groups)


def project_kernel(place_ref, hidden_ref, gain_ref, weight_ref, cos_ref, sin_ref,
                   normed_ref, q_t_ref, k_t_ref, v_t_ref, q_ref, k_ref, v_ref):
    x = hidden_ref[0].astype(f32)
    factor = lax.rsqrt(jnp.mean(x * x, axis=-1, keepdims=True) + norm_eps)
    normed = (x * factor * gain_ref[...]).astype(bf16)
    normed_ref[0] = normed
    product = dot(normed, weight_ref[...]).T
    cosine, sine = cos_ref[...], sin_ref[...]
    for number, (t_ref, n_ref) in enumerate(((q_t_ref, q_ref), (k_t_ref, k_ref))):
        first = product[number * HEAD_SIZE:number * HEAD_SIZE + HALF]
        second = product[number * HEAD_SIZE + HALF:(number + 1) * HEAD_SIZE]
        turned = jnp.concatenate(
            [first * cosine - second * sine, second * cosine + first * sine], axis=0
        )
        t_ref[...] = turned.astype(bf16)
        n_ref[...] = turned.T.astype(bf16)
    value = product[2 * HEAD_SIZE:3 * HEAD_SIZE]
    v_t_ref[...] = value.astype(bf16)
    v_ref[...] = value.T.astype(bf16)


def project(pieces, gain, weight, places, cosine, sine):
    count, rows, width = pieces.shape
    tokens = count * rows
    wide = pl.BlockSpec((HEAD_SIZE, rows), lambda i, p: (0, p[i]))
    tall = pl.BlockSpec((rows, HEAD_SIZE), lambda i, p: (p[i], 0))
    table = pl.BlockSpec((HALF, rows), lambda i, p: (0, p[i]))
    return pl.pallas_call(
        project_kernel,
        grid_spec=pltpu.PrefetchScalarGridSpec(
            num_scalar_prefetch=1,
            grid=(count,),
            in_specs=[
                pl.BlockSpec((1, rows, width), lambda i, p: (i, 0, 0)),
                pl.BlockSpec((1, width), lambda i, p: (0, 0)),
                pl.BlockSpec(weight.shape, lambda i, p: (0, 0)),
                table,
                table,
            ],
            out_specs=[pl.BlockSpec((1, rows, width), lambda i, p: (i, 0, 0))]
            + [wide] * 3 + [tall] * 3,
        ),
        out_shape=[jax.ShapeDtypeStruct(pieces.shape, bf16)]
        + [jax.ShapeDtypeStruct((HEAD_SIZE, tokens), bf16)] * 3
        + [jax.ShapeDtypeStruct((tokens, HEAD_SIZE), bf16)] * 3,
        compiler_params=pltpu.CompilerParams(vmem_limit_bytes=32 * 2**20),
        cost_estimate=pl.CostEstimate(
            flops=2 * tokens * width * 3 * HEAD_SIZE,
            bytes_accessed=4 * tokens * width,
            transcendentals=0,
        ),
        name="project",
    )(places, pieces, gain, weight, cosine, sine)


def widened(column):
    return jnp.concatenate([column] * (SPAN // column.shape[1]), axis=1)


def causal_tile():
    key_at = lax.broadcasted_iota(jnp.int32, (SPAN, SPAN), 0)
    query_at = lax.broadcasted_iota(jnp.int32, (SPAN, SPAN), 1)
    return key_at <= query_at


def forward_kernel(q_t_ref, k_ref, v_t_ref, id_row_ref, id_col_ref, out_ref, out_full_ref, lse_ref):
    block = pl.program_id(0)
    query = q_t_ref[...]
    id_row = id_row_ref[...]

    def step(at, carry, diagonal):
        best, total, result = carry
        keys = pl.ds(pl.multiple_of(at * SPAN, SPAN), SPAN)
        scores = dot(k_ref[keys, :], query) * scale_log2
        allowed = widened(id_col_ref[keys, :]) == id_row
        if diagonal:
            allowed = allowed & causal_tile()
        scores = jnp.where(allowed, scores, masked_score)
        larger = jnp.maximum(best, jnp.max(scores, axis=0, keepdims=True))
        weights = jnp.exp2(scores - larger)
        faded = jnp.exp2(best - larger)
        total = total * faded + jnp.sum(weights, axis=0, keepdims=True)
        result = result * faded + dot(v_t_ref[:, keys], weights.astype(bf16))
        return larger, total, result

    carry = (
        jnp.full((1, SPAN), masked_score, f32),
        jnp.zeros((1, SPAN), f32),
        jnp.zeros((HEAD_SIZE, SPAN), f32),
    )
    carry = lax.fori_loop(0, block, lambda at, c: step(at, c, False), carry)
    best, total, result = step(block, carry, True)
    result = result / total
    out_full_ref[...] = result
    out_ref[0] = result.astype(bf16)
    lse_ref[...] = best + jnp.log2(total)


def attention_forward(q_t, k, v_t, id_row, id_col):
    tokens = k.shape[0]
    whole = lambda array: pl.BlockSpec(array.shape, lambda i: (0, 0))
    return pl.pallas_call(
        forward_kernel,
        grid=(SPANS,),
        in_specs=[
            pl.BlockSpec((HEAD_SIZE, SPAN), lambda i: (0, i)),
            whole(k),
            whole(v_t),
            pl.BlockSpec((1, SPAN), lambda i: (0, i)),
            whole(id_col),
        ],
        out_specs=[
            pl.BlockSpec((1, HEAD_SIZE, SPAN), lambda i: (i, 0, 0)),
            pl.BlockSpec((HEAD_SIZE, SPAN), lambda i: (0, i)),
            pl.BlockSpec((1, SPAN), lambda i: (0, i)),
        ],
        out_shape=[
            jax.ShapeDtypeStruct((SPANS, HEAD_SIZE, SPAN), bf16),
            jax.ShapeDtypeStruct((HEAD_SIZE, tokens), f32),
            jax.ShapeDtypeStruct((1, tokens), f32),
        ],
        compiler_params=pltpu.CompilerParams(vmem_limit_bytes=40 * 2**20),
        cost_estimate=pl.CostEstimate(
            flops=36 * SPAN * SPAN * 256 * 4 * 4, bytes_accessed=8 * 2**20, transcendentals=36 * SPAN * SPAN
        ),
        name="attention_forward",
    )(q_t, k, v_t, id_row, id_col)


def backward_kernel(q_t_ref, q_ref, k_t_ref, k_ref, v_ref, dout_ref, out_ref, lse_ref, id_row_ref, id_col_ref,
                    cos_ref, sin_ref, grad_ref, delta_ref, dout_n_ref, dq_ref):
    block = pl.program_id(0)

    @pl.when(block == 0)
    def _():
        for at in range(SPANS):
            dout = dout_ref[at]
            here = slice(at * SPAN, (at + 1) * SPAN)
            delta_ref[:, here] = jnp.sum(dout.astype(f32) * out_ref[:, here], axis=0, keepdims=True)
            dout_n_ref[here, :] = dout.astype(f32).T.astype(bf16)
        dq_ref[...] = jnp.zeros(dq_ref.shape, f32)

    key_t, key, value = k_t_ref[...], k_ref[...], v_ref[...]
    id_col = widened(id_col_ref[...])

    def step(at, carry, diagonal):
        dkey, dvalue = carry
        rows = pl.ds(pl.multiple_of(at * SPAN, SPAN), SPAN)
        scores = dot(key, q_t_ref[:, rows]) * scale_log2 - lse_ref[:, rows]
        allowed = id_col == id_row_ref[:, rows]
        if diagonal:
            allowed = allowed & causal_tile()
        probs = jnp.exp2(jnp.where(allowed, scores, masked_score))
        dprobs = dot(value, dout_ref[at])
        dscores = (probs * (dprobs - delta_ref[:, rows])).astype(bf16)
        dvalue = dvalue + dot(probs.astype(bf16), dout_n_ref[rows, :])
        dkey = dkey + dot(dscores, q_ref[rows, :])
        dq_ref[at] += dot(key_t, dscores)
        return dkey, dvalue

    zero = jnp.zeros((SPAN, HEAD_SIZE), f32)
    carry = step(block, (zero, zero), True)
    dkey, dvalue = lax.fori_loop(block + 1, SPANS, lambda at, c: step(at, c, False), carry)
    cosine, sine = cos_ref[...], sin_ref[...]
    for number, grad in enumerate((dq_ref[block], dkey.T)):
        first = grad[:HALF] * scale
        second = grad[HALF:] * scale
        turned = jnp.concatenate(
            [first * cosine + second * sine, second * cosine - first * sine], axis=0
        )
        grad_ref[0, number * HEAD_SIZE:(number + 1) * HEAD_SIZE, :] = turned.astype(bf16)
    grad_ref[0, 2 * HEAD_SIZE:, :] = dvalue.T.astype(bf16)


def attention_backward(q_t, q, k_t, k, v, dout, out, lse, id_row, id_col, cosine, sine):
    tokens = k.shape[0]
    whole = lambda array: pl.BlockSpec(array.shape, lambda i: (0,) * array.ndim)
    wide = pl.BlockSpec((HEAD_SIZE, SPAN), lambda i: (0, i))
    tall = pl.BlockSpec((SPAN, HEAD_SIZE), lambda i: (i, 0))
    table = pl.BlockSpec((HALF, SPAN), lambda i: (0, i))
    return pl.pallas_call(
        backward_kernel,
        grid=(SPANS,),
        in_specs=[
            whole(q_t), whole(q), wide, tall, tall, whole(dout), whole(out), whole(lse), whole(id_row),
            pl.BlockSpec((SPAN, id_col.shape[1]), lambda i: (i, 0)), table, table,
        ],
        out_specs=pl.BlockSpec((1, 3 * HEAD_SIZE, SPAN), lambda i: (i, 0, 0)),
        out_shape=jax.ShapeDtypeStruct((SPANS, 3 * HEAD_SIZE, SPAN), bf16),
        scratch_shapes=[
            pltpu.VMEM((1, tokens), f32),
            pltpu.VMEM((tokens, HEAD_SIZE), bf16),
            pltpu.VMEM((SPANS, HEAD_SIZE, SPAN), f32),
        ],
        compiler_params=pltpu.CompilerParams(vmem_limit_bytes=48 * 2**20),
        cost_estimate=pl.CostEstimate(
            flops=36 * SPAN * SPAN * 256 * 10 * 4, bytes_accessed=12 * 2**20, transcendentals=36 * SPAN * SPAN
        ),
        name="attention_backward",
    )(q_t, q, k_t, k, v, dout, out, lse, id_row, id_col, cosine, sine)


def head_grad_kernel(place_ref, normed_ref, grad_ref, out_ref, sum_ref):
    at = pl.program_id(0)
    product = dot(grad_ref[0], normed_ref[0])

    @pl.when(at == 0)
    def _():
        sum_ref[...] = product

    @pl.when(at > 0)
    def _():
        sum_ref[...] += product

    @pl.when(at == pl.num_programs(0) - 1)
    def _():
        out_ref[...] = sum_ref[...].T.astype(bf16)


def head_grads(normed, grads, places):
    count, rows, width = normed.shape
    return pl.pallas_call(
        head_grad_kernel,
        grid_spec=pltpu.PrefetchScalarGridSpec(
            num_scalar_prefetch=1,
            grid=(count,),
            in_specs=[
                pl.BlockSpec((1, rows, width), lambda i, p: (i, 0, 0)),
                pl.BlockSpec((1, 3 * HEAD_SIZE, rows), lambda i, p: (p[i] // 2, 0, p[i] % 2)),
            ],
            out_specs=pl.BlockSpec((width, 3 * HEAD_SIZE), lambda i, p: (0, 0)),
            scratch_shapes=[pltpu.VMEM((3 * HEAD_SIZE, width), f32)],
        ),
        out_shape=jax.ShapeDtypeStruct((width, 3 * HEAD_SIZE), bf16),
        compiler_params=pltpu.CompilerParams(vmem_limit_bytes=32 * 2**20),
        cost_estimate=pl.CostEstimate(
            flops=2 * count * rows * width * 3 * HEAD_SIZE, bytes_accessed=2 * count * rows * width, transcendentals=0
        ),
        name="head_grads",
    )(places, normed, grads)


def gather_block(own):
    rows = own.shape[0]
    cut_a, cut_b = rows // 128 * 48, rows // 128 * 88
    p1, p2, p4 = hop(own, 1), hop(own, 2), hop(own, 4)
    p3, p6, p5 = hop(p2, 1), hop(p4, 2), hop(p1, 4)
    p7 = jnp.concatenate([hop(p6[:cut_a], 1), hop(p5[cut_a:cut_b], 2), hop(p3[cut_b:], 4)], axis=0)
    pieces = []
    for piece in (own, p1, p2, p3, p4, p5, p6, p7):
        pieces += [piece, swap(piece)]
    return jnp.stack(pieces)


def gather_plane(own):
    pieces = []
    for piece in [own] + [hop(own, k) for k in range(1, PLANE)]:
        pieces += [piece, swap(piece)]
    return jnp.concatenate(pieces, axis=0)


def scatter_plane(parts, rows):
    table = parts.reshape(PLANE, 2, rows, -1)
    pair = table[:, 0] + swap(table[:, 1].astype(bf16)).astype(f32)
    low = pair.astype(bf16)
    total = pair[0]
    for k in range(1, PLANE):
        total = total + hop(low[k], k).astype(f32)
    return total


def reorder(rows, plane_at, planes):
    width = rows.shape[1] // planes
    return jnp.concatenate(
        [lax.dynamic_slice_in_dim(rows, (plane_at ^ k) * width, width, 1) for k in range(planes)], axis=1
    )


def rms_factor(stream):
    return lax.rsqrt(jnp.mean(stream * stream, axis=-1, keepdims=True) + norm_eps)


def norm_backward(stream, factor, gain, dnormed):
    scaled = dnormed * gain
    return factor * scaled - stream * factor**3 * jnp.mean(scaled * stream, axis=-1, keepdims=True)


def body(
    hidden,
    document_index,
    attn_gain,
    q_weight,
    key_matrix,
    value_matrix,
    out_weight,
    mlp_gain,
    gate_weight,
    up_weight,
    down_weight,
    cotangent,
):
    count = lax.axis_size("fsdp")
    planes = count // PLANE
    f = lax.axis_index("fsdp")
    t = lax.axis_index("tp")
    place = f % SPANS
    plane_at = f // PLANE
    own, width = hidden.shape
    shard = q_weight.shape[1]
    q_heads = q_weight.shape[2] // HEAD_SIZE
    kv_heads = key_matrix.shape[2] // HEAD_SIZE
    per_kv = q_heads // kv_heads
    units = gate_weight.shape[2] // PLANE

    def by_head(weight, heads, copies):
        cut = weight[0].reshape(shard, heads, HEAD_SIZE).transpose(1, 0, 2)
        return jnp.repeat(cut, copies, axis=0)

    gains_own = jnp.stack([attn_gain[0], mlp_gain[0]], axis=-1)
    sent = jnp.concatenate(
        [
            by_head(q_weight, q_heads, 1),
            by_head(key_matrix, kv_heads, per_kv),
            by_head(value_matrix, kv_heads, per_kv),
            jnp.broadcast_to(gains_own[None], (SPANS, shard, 2)),
        ],
        axis=-1,
    )
    sent = jnp.tile(sent, (count // SPANS, 1, 1))
    head_set = exchange(sent, count).reshape(width, -1)
    head_weight = head_set[:, :3 * HEAD_SIZE]
    gains = head_set[:, 3 * HEAD_SIZE:].T.astype(f32)
    gain_a, gain_m = gains[0:1], gains[1:2]

    pieces = gather_block(hidden)

    unit_set = jnp.concatenate(
        [w[0].reshape(shard, PLANE, units).transpose(1, 0, 2) for w in (gate_weight, up_weight, down_weight)],
        axis=-1,
    )
    unit_own = exchange(unit_set, PLANE).reshape(PLANE * shard, 3 * units)
    unit_weight = jnp.concatenate(
        [unit_own] + [hop(unit_own, PLANE * k) for k in range(1, planes)], axis=0
    )
    out_part = lax.all_gather(out_weight[0], "fsdp", axis=0, tiled=True)
    in_part = lax.all_gather(
        jnp.concatenate([q_weight[0], key_matrix[0], value_matrix[0]], axis=1), "fsdp", axis=0, tiled=True
    )

    seq_ids = lax.dynamic_slice_in_dim(document_index, f // SPANS * PACKED_LENGTH, PACKED_LENGTH)
    seq_index = jnp.arange(PACKED_LENGTH, dtype=jnp.int32)
    before = jnp.concatenate([jnp.full((1,), -1, jnp.int32), seq_ids[:-1]])
    starts = lax.cummax(jnp.where(seq_ids != before, seq_index, 0), axis=0)
    positions = (seq_index - starts).astype(f32)
    freq = rope_base ** (-2.0 * jnp.arange(HALF, dtype=f32) / HEAD_SIZE)
    angle = freq[:, None] * positions[None, :]
    cosine, sine = jnp.cos(angle), jnp.sin(angle)
    id_row = seq_ids[None, :]
    id_col = jnp.broadcast_to(seq_ids[:, None], (PACKED_LENGTH, 128))
    own_ids = lax.dynamic_slice_in_dim(seq_ids, place * SPAN + t * own, own)
    places = jnp.stack([(place ^ k) * 2 + (t ^ c) for k in range(SPANS) for c in range(2)]).astype(jnp.int32)

    dstream = cotangent.astype(f32) * (own_ids != 0).astype(f32)[:, None]
    dmlp = gather_plane(reorder(dstream.astype(bf16), plane_at, planes))

    normed, q_t, k_t, v_t, q, k, v = project(pieces, gain_a, head_weight, places, cosine, sine)
    out_t, out_full, lse = attention_forward(q_t, k, v_t, id_row, id_col)
    attended = exchange(out_t, SPANS).reshape(q_heads * HEAD_SIZE, SPAN)

    stream = hidden.astype(f32)
    mine = lax.dynamic_slice_in_dim(attended, t * own, own, 1)
    other = lax.dynamic_slice_in_dim(attended, (1 - t) * own, own, 1)
    mid = stream + dot(mine, out_part, 0, 1) + swap(dot(other, out_part, 0, 1))

    factor_m = rms_factor(mid)
    normed_m = gather_plane(reorder((mid * factor_m * gain_m).astype(bf16), plane_at, planes))
    gate = dot(normed_m, unit_weight[:, :units])
    up = dot(normed_m, unit_weight[:, units:2 * units])
    dact = dot(dmlp, unit_weight[:, 2 * units:])
    sigma = 1.0 / (1.0 + jnp.exp(-gate))
    act = (gate * sigma * up).astype(bf16)
    dgate = (dact * up * sigma * (1.0 + gate * (1.0 - sigma))).astype(bf16)
    dup = (dact * gate * sigma).astype(bf16)
    dgate_up = jnp.concatenate([dgate, dup], axis=1)
    dnormed_m = reorder(
        scatter_plane(dot(dgate_up, unit_weight[:, :2 * units], 1, 1), own), plane_at, planes
    )
    dmid = dstream + norm_backward(mid, factor_m, gain_m, dnormed_m)

    dattn = dmid.astype(bf16)
    dattn_other = swap(dattn)
    dattn = jnp.where(
        t == 0,
        jnp.concatenate([dattn, dattn_other], axis=0),
        jnp.concatenate([dattn_other, dattn], axis=0),
    )
    dout = exchange(
        dot(out_part, dattn, 0, 1).astype(bf16).reshape(SPANS, HEAD_SIZE, SPAN), SPANS
    )
    out_grad = lax.psum_scatter(
        dot(dattn, attended, 0, 1).astype(bf16), "fsdp", scatter_dimension=0, tiled=True
    ).astype(f32)
    grads = attention_backward(q_t, q, k_t, k, v, dout, out_full, lse, id_row, id_col, cosine, sine)

    back = exchange(grads, SPANS)
    dq = back[:, :HEAD_SIZE].reshape(q_heads * HEAD_SIZE, SPAN)
    dkv = back[:, HEAD_SIZE:].reshape(kv_heads, per_kv, 2, HEAD_SIZE, SPAN).astype(f32).sum(axis=1)
    dkv = dkv.astype(bf16).transpose(1, 0, 2, 3).reshape(2 * kv_heads * HEAD_SIZE, SPAN)
    din = jnp.concatenate([dq, dkv], axis=0)
    mine = lax.dynamic_slice_in_dim(din, t * own, own, 1)
    other = lax.dynamic_slice_in_dim(din, (1 - t) * own, own, 1)
    dnormed_a = dot(mine, in_part, 0, 1) + swap(dot(other, in_part, 0, 1))
    input_grad = dmid + norm_backward(stream, rms_factor(stream), gain_a, dnormed_a)

    head_sums = exchange(head_grads(normed, grads, places).reshape(count, shard, 3 * HEAD_SIZE), count)
    head_sums = head_sums.reshape(count // SPANS, SPANS, shard, 3 * HEAD_SIZE).astype(f32).sum(axis=0)
    q_grad = head_sums[..., :HEAD_SIZE].transpose(1, 0, 2).reshape(shard, -1)
    kv_sums = head_sums.reshape(kv_heads, per_kv, shard, 3 * HEAD_SIZE).sum(axis=1)
    k_grad = kv_sums[..., HEAD_SIZE:2 * HEAD_SIZE].transpose(1, 0, 2).reshape(shard, -1)
    v_grad = kv_sums[..., 2 * HEAD_SIZE:].transpose(1, 0, 2).reshape(shard, -1)

    output = (
        mid + reorder(scatter_plane(dot(act, unit_weight[:, 2 * units:], 1, 1), own), plane_at, planes)
    ).astype(bf16)
    unit_grad = jnp.concatenate([dot(normed_m, dgate_up, 0, 0), dot(dmlp, act, 0, 0)], axis=1)
    unit_grad = unit_grad.reshape(planes, PLANE * shard, 3 * units)
    low = unit_grad.astype(bf16)
    unit_sum = unit_grad[0]
    for step in range(1, planes):
        unit_sum = unit_sum + hop(low[step], PLANE * step).astype(f32)
    unit_back = exchange(unit_sum.astype(bf16).reshape(PLANE, shard, 3 * units), PLANE)
    unit_back = unit_back.transpose(1, 0, 2).astype(f32)
    gate_grad, up_grad, down_grad = (
        unit_back[..., part * units:(part + 1) * units].reshape(shard, -1) for part in range(3)
    )

    def row_products(pairs):
        return sum(jnp.sum(grad * weight[0].astype(f32), axis=1) for grad, weight in pairs)

    gain_parts = jnp.stack([
        row_products([(q_grad, q_weight), (k_grad, key_matrix), (v_grad, value_matrix)]),
        row_products([(gate_grad, gate_weight), (up_grad, up_weight)]),
    ])
    gain_grads = (gain_parts + swap(gain_parts)) / jnp.stack([attn_gain[0], mlp_gain[0]]).astype(f32)
    return (
        output,
        input_grad,
        gain_grads[0:1],
        q_grad[None],
        k_grad[None],
        v_grad[None],
        out_grad[None],
        gain_grads[1:2],
        gate_grad[None],
        up_grad[None],
        down_grad[None],
    )


def solution(mesh):
    rows = P(("fsdp", "tp"), None)
    gain = P(None, "fsdp")
    weight = P(None, "fsdp", "tp")
    return jax.shard_map(
        body,
        mesh=mesh,
        in_specs=(rows, P(), gain, weight, weight, weight, weight, gain, weight, weight, weight, rows),
        out_specs=(rows, rows, gain, weight, weight, weight, weight, gain, weight, weight, weight),
        check_vma=False,
    )
```

```python
import functools
import math

import jax
import jax.numpy as jnp
from jax import lax
from jax.experimental import pallas as pl
from jax.experimental.pallas import tpu as pltpu
from jax.sharding import PartitionSpec as P

HEAD_SIZE = 96
HALF = HEAD_SIZE // 2
SPANS = 8
PLANE = 4
PACKED_LENGTH = 4096
SPAN = PACKED_LENGTH // SPANS

rope_base = 100000.0
norm_eps = 1e-05
masked_score = -1000000000.0
scale = HEAD_SIZE ** (-0.5)
scale_log2 = scale * math.log2(math.e)
bf16 = jnp.bfloat16
f32 = jnp.float32


def dot(left, right, left_dim=1, right_dim=0):
    return lax.dot_general(
        left, right, (((left_dim,), (right_dim,)), ((), ())), preferred_element_type=f32
    )


def hop(value, distance):
    count = lax.axis_size("fsdp")
    return lax.ppermute(value, "fsdp", [(i, i ^ distance) for i in range(count)])


def swap(value):
    return lax.ppermute(value, "tp", [(0, 1), (1, 0)])


def groups_of(size):
    count = lax.axis_size("fsdp")
    return [list(range(first, first + size)) for first in range(0, count, size)]


def exchange(value, size):
    groups = None if size == lax.axis_size("fsdp") else groups_of(size)
    return lax.all_to_all(value, "fsdp", 0, 0, axis_index_groups=groups)


def project_kernel(*refs):
    pieces, (place_ref, head_ref, cos_ref, sin_ref) = refs[:2 * SPANS], refs[2 * SPANS:2 * SPANS + 4]
    normed_ref, gain_ref, q_t_ref, k_t_ref, v_t_ref, q_ref, k_ref, v_ref = refs[2 * SPANS + 4:2 * SPANS + 12]
    in_buf, out_buf, in_sem, out_sem = refs[2 * SPANS + 12:]
    rows = pieces[0].shape[0]
    place, core = place_ref[0], place_ref[1]

    def fetch(pair, part):
        return pltpu.make_async_copy(
            pieces[2 * pair + part],
            in_buf.at[pair % 3, pl.ds(pl.multiple_of((core ^ part) * rows, rows), rows)],
            in_sem.at[pair % 3, part],
        )

    def store(pair):
        return pltpu.make_async_copy(out_buf.at[pair % 2], normed_ref.at[place ^ pair], out_sem.at[pair % 2])

    for pair in range(2):
        for part in range(2):
            fetch(pair, part).start()
    row = lax.broadcasted_iota(jnp.int32, (8, head_ref.shape[1]), 0)
    column = lax.broadcasted_iota(jnp.int32, (8, head_ref.shape[1]), 1)
    pick = (column == row + 3 * HEAD_SIZE).astype(f32).astype(bf16)
    gains = dot(pick, head_ref[...], 1, 1)
    gain = gains[0:1]
    gain_ref[...] = gains
    for pair in range(SPANS):
        for part in range(2):
            fetch(pair, part).wait()
        if pair + 2 < SPANS:
            for part in range(2):
                fetch(pair + 2, part).start()
        if pair >= 2:
            store(pair - 2).wait()
        x = in_buf[pair % 3].astype(f32)
        factor = lax.rsqrt(jnp.mean(x * x, axis=-1, keepdims=True) + norm_eps)
        normed = (x * factor * gain).astype(bf16)
        out_buf[pair % 2] = normed
        store(pair).start()
        product = dot(normed, head_ref[:, :3 * HEAD_SIZE]).T
        here = pl.ds(pl.multiple_of((place ^ pair) * 2 * rows, 2 * rows), 2 * rows)
        cosine, sine = cos_ref[:, here], sin_ref[:, here]
        for number, (t_ref, n_ref) in enumerate(((q_t_ref, q_ref), (k_t_ref, k_ref))):
            first = product[number * HEAD_SIZE:number * HEAD_SIZE + HALF]
            second = product[number * HEAD_SIZE + HALF:(number + 1) * HEAD_SIZE]
            turned = jnp.concatenate(
                [first * cosine - second * sine, second * cosine + first * sine], axis=0
            )
            t_ref[:, here] = turned.astype(bf16)
            n_ref[here, :] = turned.T.astype(bf16)
        value = product[2 * HEAD_SIZE:3 * HEAD_SIZE]
        v_t_ref[:, here] = value.astype(bf16)
        v_ref[here, :] = value.T.astype(bf16)
    for pair in range(SPANS - 2, SPANS):
        store(pair).wait()


def project(pieces, head_set, places, cosine, sine):
    rows, width = pieces[0].shape
    tokens = 2 * SPANS * rows
    vmem = pl.BlockSpec(memory_space=pltpu.VMEM)
    anywhere = pl.BlockSpec(memory_space=pl.ANY)
    return pl.pallas_call(
        project_kernel,
        in_specs=[anywhere] * len(pieces) + [pl.BlockSpec(memory_space=pltpu.SMEM), vmem, vmem, vmem],
        out_specs=[anywhere] + [vmem] * 7,
        out_shape=[
            jax.ShapeDtypeStruct((SPANS, 2 * rows, width), bf16),
            jax.ShapeDtypeStruct((8, width), f32),
        ]
        + [jax.ShapeDtypeStruct((HEAD_SIZE, tokens), bf16)] * 3
        + [jax.ShapeDtypeStruct((tokens, HEAD_SIZE), bf16)] * 3,
        scratch_shapes=[
            pltpu.VMEM((3, 2 * rows, width), bf16),
            pltpu.VMEM((2, 2 * rows, width), bf16),
            pltpu.SemaphoreType.DMA((3, 2)),
            pltpu.SemaphoreType.DMA((2,)),
        ],
        compiler_params=pltpu.CompilerParams(vmem_limit_bytes=56 * 2**20),
        cost_estimate=pl.CostEstimate(
            flops=2 * tokens * width * 3 * HEAD_SIZE,
            bytes_accessed=4 * tokens * width,
            transcendentals=0,
        ),
        name="project",
    )(*pieces, places, head_set, cosine, sine)


def widened(column):
    return jnp.concatenate([column] * (SPAN // column.shape[1]), axis=1)


def causal_tile():
    key_at = lax.broadcasted_iota(jnp.int32, (SPAN, SPAN), 0)
    query_at = lax.broadcasted_iota(jnp.int32, (SPAN, SPAN), 1)
    return key_at <= query_at


def forward_kernel(q_t_ref, k_ref, v_t_ref, id_row_ref, id_col_ref, out_ref, out_full_ref, lse_ref):
    block = pl.program_id(0)
    query = q_t_ref[...]
    id_row = id_row_ref[...]

    def step(at, carry, diagonal):
        best, total, result = carry
        keys = pl.ds(pl.multiple_of(at * SPAN, SPAN), SPAN)
        scores = dot(k_ref[keys, :], query) * scale_log2
        allowed = widened(id_col_ref[keys, :]) == id_row
        if diagonal:
            allowed = allowed & causal_tile()
        scores = jnp.where(allowed, scores, masked_score)
        larger = jnp.maximum(best, jnp.max(scores, axis=0, keepdims=True))
        weights = jnp.exp2(scores - larger)
        faded = jnp.exp2(best - larger)
        total = total * faded + jnp.sum(weights, axis=0, keepdims=True)
        result = result * faded + dot(v_t_ref[:, keys], weights.astype(bf16))
        return larger, total, result

    carry = (
        jnp.full((1, SPAN), masked_score, f32),
        jnp.zeros((1, SPAN), f32),
        jnp.zeros((HEAD_SIZE, SPAN), f32),
    )
    carry = lax.fori_loop(0, block, lambda at, c: step(at, c, False), carry)
    best, total, result = step(block, carry, True)
    result = result / total
    out_full_ref[...] = result
    out_ref[0] = result.astype(bf16)
    lse_ref[...] = best + jnp.log2(total)


def attention_forward(q_t, k, v_t, id_row, id_col):
    tokens = k.shape[0]
    whole = lambda array: pl.BlockSpec(array.shape, lambda i: (0, 0))
    return pl.pallas_call(
        forward_kernel,
        grid=(SPANS,),
        in_specs=[
            pl.BlockSpec((HEAD_SIZE, SPAN), lambda i: (0, i)),
            whole(k),
            whole(v_t),
            pl.BlockSpec((1, SPAN), lambda i: (0, i)),
            whole(id_col),
        ],
        out_specs=[
            pl.BlockSpec((1, HEAD_SIZE, SPAN), lambda i: (i, 0, 0)),
            pl.BlockSpec((HEAD_SIZE, SPAN), lambda i: (0, i)),
            pl.BlockSpec((1, SPAN), lambda i: (0, i)),
        ],
        out_shape=[
            jax.ShapeDtypeStruct((SPANS, HEAD_SIZE, SPAN), bf16),
            jax.ShapeDtypeStruct((HEAD_SIZE, tokens), f32),
            jax.ShapeDtypeStruct((1, tokens), f32),
        ],
        compiler_params=pltpu.CompilerParams(vmem_limit_bytes=40 * 2**20),
        cost_estimate=pl.CostEstimate(
            flops=36 * SPAN * SPAN * 256 * 4 * 4, bytes_accessed=8 * 2**20, transcendentals=36 * SPAN * SPAN
        ),
        name="attention_forward",
    )(q_t, k, v_t, id_row, id_col)


def backward_kernel(cubes, q_t_ref, q_ref, k_t_ref, k_ref, v_ref, dout_ref, out_ref, lse_ref, id_row_ref, id_col_ref,
                    cos_ref, sin_ref, normed_ref, grad_ref, delta_ref, dout_n_ref, dq_ref, sum_ref):
    block = pl.program_id(0)

    @pl.when(block == 0)
    def _():
        for at in range(SPANS):
            dout = dout_ref[at]
            here = slice(at * SPAN, (at + 1) * SPAN)
            delta_ref[:, here] = jnp.sum(dout.astype(f32) * out_ref[:, here], axis=0, keepdims=True)
            dout_n_ref[here, :] = dout.astype(f32).T.astype(bf16)
        dq_ref[...] = jnp.zeros(dq_ref.shape, f32)
        sum_ref[...] = jnp.zeros(sum_ref.shape, f32)

    key_t, key, value = k_t_ref[...], k_ref[...], v_ref[...]
    id_col = widened(id_col_ref[...])

    def step(at, carry, diagonal):
        dkey, dvalue = carry
        rows = pl.ds(pl.multiple_of(at * SPAN, SPAN), SPAN)
        scores = dot(key, q_t_ref[:, rows]) * scale_log2 - lse_ref[:, rows]
        allowed = id_col == id_row_ref[:, rows]
        if diagonal:
            allowed = allowed & causal_tile()
        probs = jnp.exp2(jnp.where(allowed, scores, masked_score))
        dprobs = dot(value, dout_ref[at])
        dscores = (probs * (dprobs - delta_ref[:, rows])).astype(bf16)
        dvalue = dvalue + dot(probs.astype(bf16), dout_n_ref[rows, :])
        dkey = dkey + dot(dscores, q_ref[rows, :])
        dq_ref[at] += dot(key_t, dscores)
        return dkey, dvalue

    zero = jnp.zeros((SPAN, HEAD_SIZE), f32)
    carry = step(block, (zero, zero), True)
    dkey, dvalue = lax.fori_loop(block + 1, SPANS, lambda at, c: step(at, c, False), carry)
    cosine, sine = cos_ref[...], sin_ref[...]
    for number, grad in enumerate((dq_ref[block], dkey.T)):
        first = grad[:HALF] * scale
        second = grad[HALF:] * scale
        turned = jnp.concatenate(
            [first * cosine + second * sine, second * cosine - first * sine], axis=0
        )
        grad_ref[block, number * HEAD_SIZE:(number + 1) * HEAD_SIZE, :SPAN] = turned.astype(bf16)
    grad_ref[block, 2 * HEAD_SIZE:, :SPAN] = dvalue.T.astype(bf16)
    sum_ref[...] += dot(grad_ref[block, :, :SPAN], normed_ref[0])

    @pl.when(block == SPANS - 1)
    def _():
        part = sum_ref.shape[1] // SPANS
        shard = part // cubes
        for place in range(SPANS):
            pieces = [
                sum_ref[:, (cube * SPANS + place) * shard:(cube * SPANS + place + 1) * shard] for cube in range(cubes)
            ]
            grad_ref[place, :, SPAN:] = jnp.concatenate(pieces, axis=1).astype(bf16)


def attention_backward(q_t, q, k_t, k, v, dout, out, lse, id_row, id_col, cosine, sine, normed, cubes):
    tokens = k.shape[0]
    width = normed.shape[2]
    whole = lambda array: pl.BlockSpec(array.shape, lambda i: (0,) * array.ndim)
    wide = pl.BlockSpec((HEAD_SIZE, SPAN), lambda i: (0, i))
    tall = pl.BlockSpec((SPAN, HEAD_SIZE), lambda i: (i, 0))
    table = pl.BlockSpec((HALF, SPAN), lambda i: (0, i))
    return pl.pallas_call(
        functools.partial(backward_kernel, cubes),
        grid=(SPANS,),
        in_specs=[
            whole(q_t), whole(q), wide, tall, tall, whole(dout), whole(out), whole(lse), whole(id_row),
            pl.BlockSpec((SPAN, id_col.shape[1]), lambda i: (i, 0)), table, table,
            pl.BlockSpec((1, SPAN, width), lambda i: (i, 0, 0)),
        ],
        out_specs=pl.BlockSpec((SPANS, 3 * HEAD_SIZE, SPAN + width // SPANS), lambda i: (0, 0, 0)),
        out_shape=jax.ShapeDtypeStruct((SPANS, 3 * HEAD_SIZE, SPAN + width // SPANS), bf16),
        scratch_shapes=[
            pltpu.VMEM((1, tokens), f32),
            pltpu.VMEM((tokens, HEAD_SIZE), bf16),
            pltpu.VMEM((SPANS, HEAD_SIZE, SPAN), f32),
            pltpu.VMEM((3 * HEAD_SIZE, width), f32),
        ],
        compiler_params=pltpu.CompilerParams(vmem_limit_bytes=56 * 2**20),
        cost_estimate=pl.CostEstimate(
            flops=36 * SPAN * SPAN * 256 * 10 * 4, bytes_accessed=12 * 2**20, transcendentals=36 * SPAN * SPAN
        ),
        name="attention_backward",
    )(q_t, q, k_t, k, v, dout, out, lse, id_row, id_col, cosine, sine, normed)


def head_finish_kernel(*refs):
    sum_refs, (q_ref, k_ref, v_ref, q_out, k_out, v_out, product_ref) = refs[:-7], refs[-7:]
    total = sum_refs[0][...].astype(f32)
    for ref in sum_refs[1:]:
        total = total + ref[...].astype(f32)
    total = total.T
    product = jnp.zeros(product_ref.shape, f32)
    at = 0
    for ref, out in ((q_ref, q_out), (k_ref, k_out), (v_ref, v_out)):
        grad = total[:, at:at + out.shape[1]]
        at += out.shape[1]
        out[...] = grad
        product = product + jnp.sum(grad * ref[...].astype(f32), axis=1, keepdims=True)
    product_ref[...] = product


def head_finish(sums, q_weight, k_weight, v_weight):
    vmem = pl.BlockSpec(memory_space=pltpu.VMEM)
    return pl.pallas_call(
        head_finish_kernel,
        in_specs=[vmem] * (len(sums) + 3),
        out_specs=[vmem] * 4,
        out_shape=[jax.ShapeDtypeStruct(w.shape, f32) for w in (q_weight, k_weight, v_weight)]
        + [jax.ShapeDtypeStruct((q_weight.shape[0], 1), f32)],
        compiler_params=pltpu.CompilerParams(vmem_limit_bytes=32 * 2**20),
        name="head_finish",
    )(*sums, q_weight, k_weight, v_weight)


def unit_finish_kernel(place_ref, *refs):
    piece_refs, (gate_w_ref, up_w_ref, gate_out, up_out, down_out, product_ref) = refs[:PLANE], refs[PLANE:]
    units = gate_out.shape[1] // PLANE
    for link, piece_ref in enumerate(piece_refs):
        here = pl.ds(pl.multiple_of((place_ref[0] ^ link) * units, units), units)
        for number, out in enumerate((gate_out, up_out, down_out)):
            out[:, here] = piece_ref[:, number * units:(number + 1) * units].astype(f32)
    product_ref[...] = jnp.sum(
        gate_out[...] * gate_w_ref[...].astype(f32) + up_out[...] * up_w_ref[...].astype(f32), axis=1, keepdims=True
    )


def unit_finish(place, pieces, gate_weight, up_weight):
    vmem = pl.BlockSpec(memory_space=pltpu.VMEM)
    return pl.pallas_call(
        unit_finish_kernel,
        in_specs=[pl.BlockSpec(memory_space=pltpu.SMEM)] + [vmem] * (PLANE + 2),
        out_specs=[vmem] * 4,
        out_shape=[jax.ShapeDtypeStruct(gate_weight.shape, f32)] * 3
        + [jax.ShapeDtypeStruct((gate_weight.shape[0], 1), f32)],
        compiler_params=pltpu.CompilerParams(vmem_limit_bytes=32 * 2**20),
        name="unit_finish",
    )(place, *pieces, gate_weight, up_weight)


def unit_grad_kernel(*refs):
    tables, out_ref = (refs[:3 * PLANE], refs[3 * PLANE:6 * PLANE]), refs[6 * PLANE]
    column = 0
    for table in tables:
        total = None
        for k, right in enumerate(table[2 * PLANE:]):
            left = jnp.concatenate([table[2 * k][...], table[2 * k + 1][...]], axis=0)
            term = dot(left, right[...], 0, 0)
            total = term if total is None else total + term
        out_ref[:, column:column + total.shape[1]] = total.astype(bf16)
        column += total.shape[1]


def unit_grads(normed, dgate_up, dout, act):
    tokens, width = normed[0].shape
    rows = width // 4
    whole = lambda array: pl.BlockSpec(array.shape, lambda i: (0, 0))
    left = [pl.BlockSpec((tokens, rows), lambda i: (0, i))] * (2 * PLANE)
    columns = dgate_up[0].shape[1] + act[0].shape[1]
    return pl.pallas_call(
        unit_grad_kernel,
        grid=(width // rows,),
        in_specs=left + [whole(part) for part in dgate_up] + left + [whole(part) for part in act],
        out_specs=pl.BlockSpec((rows, columns), lambda i: (i, 0)),
        out_shape=jax.ShapeDtypeStruct((width, columns), bf16),
        compiler_params=pltpu.CompilerParams(vmem_limit_bytes=48 * 2**20),
        cost_estimate=pl.CostEstimate(
            flops=2 * 2 * tokens * PLANE * width * columns, bytes_accessed=24 * 2**20, transcendentals=0
        ),
        name="unit_grads",
    )(*normed, *dgate_up, *dout, *act)


def feed_kernel(pairs, *refs):
    ins, weight_ref, refs = refs[:4 * pairs], refs[4 * pairs], refs[4 * pairs + 1:]
    units = weight_ref.shape[1] // 3
    weight = weight_ref[:, :2 * units]
    down_weight = weight_ref[:, 2 * units:]
    for pair in range(pairs):
        own_ref, other_ref, d_own_ref, d_other_ref = ins[4 * pair:4 * pair + 4]
        kept_ref, sent_ref, out_kept_ref, out_sent_ref, dgate_up_ref, act_ref = refs[6 * pair:6 * pair + 6]
        rows = own_ref.shape[0]
        gate_up = dot(jnp.concatenate([own_ref[...], other_ref[...]], axis=0), weight)
        dact = dot(jnp.concatenate([d_own_ref[...], d_other_ref[...]], axis=0), down_weight)
        gate, up = gate_up[:, :units], gate_up[:, units:]
        sigma = 1.0 / (1.0 + jnp.exp(-gate))
        silu = gate * sigma
        dgate_up_ref[:, :units] = (dact * up * sigma * (1.0 + gate * (1.0 - sigma))).astype(bf16)
        dgate_up_ref[:, units:] = (dact * silu).astype(bf16)
        act_ref[...] = (silu * up).astype(bf16)
        dnormed = dot(dgate_up_ref[...], weight, 1, 1)
        kept_ref[...] = dnormed[:rows]
        sent_ref[...] = dnormed[rows:].astype(bf16)
        out = dot(act_ref[...], down_weight, 1, 1)
        out_kept_ref[...] = out[:rows]
        out_sent_ref[...] = out[rows:].astype(bf16)


def feed(rows_list, weight):
    pairs = len(rows_list)
    rows, width = rows_list[0][0].shape
    units = weight.shape[1] // 3
    vmem = pl.BlockSpec(memory_space=pltpu.VMEM)
    halves = [jax.ShapeDtypeStruct((rows, width), f32), jax.ShapeDtypeStruct((rows, width), bf16)]
    shapes = (
        halves * 2 + [jax.ShapeDtypeStruct((2 * rows, 2 * units), bf16), jax.ShapeDtypeStruct((2 * rows, units), bf16)]
    ) * pairs
    ins = [part for group in rows_list for part in group]
    outs = pl.pallas_call(
        functools.partial(feed_kernel, pairs),
        in_specs=[vmem] * (len(ins) + 1),
        out_specs=[vmem] * len(shapes),
        out_shape=shapes,
        compiler_params=pltpu.CompilerParams(vmem_limit_bytes=48 * 2**20),
        cost_estimate=pl.CostEstimate(
            flops=pairs * 2 * 2 * rows * width * units * 6, bytes_accessed=8 * 2**20, transcendentals=2 * rows * units
        ),
        name="feed",
    )(*ins, weight)
    return [outs[6 * pair:6 * pair + 6] for pair in range(pairs)]


def back_kernel(core_ref, back_ref, weight_ref, mine_ref, other_ref, head_ref, table_ref):
    heads = back_ref.shape[0]
    kv_heads = (table_ref.shape[0] // HEAD_SIZE - heads) // 2
    per_kv = heads // kv_heads
    cubes, _, shard = head_ref.shape

    def put(at, value):
        table_ref[at:at + HEAD_SIZE, :] = value[:, :SPAN]
        for cube in range(cubes):
            head_ref[cube, at:at + HEAD_SIZE, :] = value[:, SPAN + cube * shard:SPAN + (cube + 1) * shard]

    for head in range(heads):
        put(head * HEAD_SIZE, back_ref[head, :HEAD_SIZE, :])
    for number in range(2):
        here = slice((number + 1) * HEAD_SIZE, (number + 2) * HEAD_SIZE)
        for head in range(kv_heads):
            total = back_ref[head * per_kv, here, :].astype(f32)
            for copy in range(1, per_kv):
                total = total + back_ref[head * per_kv + copy, here, :].astype(f32)
            put((heads + number * kv_heads + head) * HEAD_SIZE, total.astype(bf16))
    rows = mine_ref.shape[0]
    both = dot(weight_ref[...], table_ref[...])
    low, high = both[:, :rows].T, both[:, rows:].T
    first = core_ref[0] == 0
    mine_ref[...] = jnp.where(first, low, high)
    other_ref[...] = jnp.where(first, high, low)


def input_terms(back, weight, core, cubes):
    vmem = pl.BlockSpec(memory_space=pltpu.VMEM)
    width, features = weight.shape
    rows = SPAN // 2
    shard = (back.shape[2] - SPAN) // cubes
    return pl.pallas_call(
        back_kernel,
        in_specs=[pl.BlockSpec(memory_space=pltpu.SMEM), vmem, vmem],
        out_specs=[vmem] * 3,
        out_shape=[jax.ShapeDtypeStruct((rows, width), f32)] * 2
        + [jax.ShapeDtypeStruct((cubes, features, shard), bf16)],
        scratch_shapes=[pltpu.VMEM((features, SPAN), bf16)],
        compiler_params=pltpu.CompilerParams(vmem_limit_bytes=40 * 2**20),
        cost_estimate=pl.CostEstimate(
            flops=4 * width * features * rows, bytes_accessed=12 * 2**20, transcendentals=0
        ),
        name="input_terms",
    )(core, back, weight)


tie = lax.optimization_barrier


def with_swapped(pieces):
    return [part for piece in pieces for part in (piece, swap(piece))]


def rms_factor(stream):
    return lax.rsqrt(jnp.mean(stream * stream, axis=-1, keepdims=True) + norm_eps)


def norm_backward(stream, factor, gain, dnormed):
    scaled = dnormed * gain
    return factor * scaled - stream * factor**3 * jnp.mean(scaled * stream, axis=-1, keepdims=True)


def body(
    hidden,
    document_index,
    attn_gain,
    q_weight,
    key_matrix,
    value_matrix,
    out_weight,
    mlp_gain,
    gate_weight,
    up_weight,
    down_weight,
    cotangent,
):
    count = lax.axis_size("fsdp")
    planes = count // PLANE
    f = lax.axis_index("fsdp")
    t = lax.axis_index("tp")
    place = f % SPANS
    plane_at = f // PLANE
    own, width = hidden.shape
    shard = q_weight.shape[1]
    q_heads = q_weight.shape[2] // HEAD_SIZE
    kv_heads = key_matrix.shape[2] // HEAD_SIZE
    per_kv = q_heads // kv_heads
    units = gate_weight.shape[2] // PLANE

    def by_head(weight, heads, copies):
        cut = weight[0].reshape(shard, heads, HEAD_SIZE).transpose(1, 0, 2)
        return jnp.repeat(cut, copies, axis=0)

    gains_own = jnp.stack([attn_gain[0], mlp_gain[0]], axis=-1)
    sent = jnp.concatenate(
        [
            by_head(q_weight, q_heads, 1),
            by_head(key_matrix, kv_heads, per_kv),
            by_head(value_matrix, kv_heads, per_kv),
            jnp.broadcast_to(gains_own[None], (SPANS, shard, 2)),
        ],
        axis=-1,
    )
    sent = jnp.tile(sent, (count // SPANS, 1, 1))

    plane_place = f % PLANE
    cubes = count // SPANS
    cube_at = f // SPANS
    half = own // 2
    unit_set = jnp.concatenate(
        [w[0].reshape(shard, PLANE, units).transpose(1, 0, 2) for w in (gate_weight, up_weight, down_weight)],
        axis=-1,
    )
    lines = [list(range(first, count, PLANE)) for first in range(PLANE)]
    p1, p2, p4 = hop(hidden, 1), hop(hidden, 2), hop(hidden, 4)
    out_0 = lax.all_to_all(
        jnp.broadcast_to(out_weight, (planes,) + out_weight.shape[1:]), "fsdp", 0, 0, axis_index_groups=lines
    )
    sent, unit_set, p1, p2, p4, out_0 = tie((sent, unit_set, p1, p2, p4, out_0))
    p3, p6, p5 = hop(p2, 1), hop(p4, 2), hop(p1, 4)
    out_1, out_2 = hop(out_0, 1), hop(out_0, 2)
    head_set = exchange(sent, count).reshape(width, -1)

    own_ids = lax.dynamic_slice_in_dim(document_index, f * SPAN + t * own, own)
    dstream = cotangent.astype(f32) * (own_ids != 0).astype(f32)[:, None]
    dmlp_own = dstream.astype(bf16)
    unit_set, head_set, p3, p6, p5, dmlp_own, out_1, out_2 = tie(
        (unit_set, head_set, p3, p6, p5, dmlp_own, out_1, out_2)
    )
    cut_a, cut_b = own // 128 * 48, own // 128 * 88
    p7 = [hop(p6[:cut_a], 1), hop(p5[cut_a:cut_b], 2), hop(p3[cut_b:], 4)]
    out_3 = hop(out_0, 3)
    unit_own = exchange(unit_set, PLANE).reshape(PLANE * shard, 3 * units)
    dmlp_own, p7, unit_own, out_3 = tie((dmlp_own, p7, unit_own, out_3))
    pieces = with_swapped([hidden, p1, p2, p3, p4, p5, p6, jnp.concatenate(p7, axis=0)])
    dmlp_1, dmlp_2 = hop(dmlp_own, 1), hop(dmlp_own, 2)
    unit_weight = lax.all_gather(unit_own, "fsdp", axis=0, tiled=True, axis_index_groups=lines)
    out_part = jnp.zeros((planes, PLANE, shard, out_0.shape[2]), bf16)
    for k, piece in enumerate((out_0, out_1, out_2, out_3)):
        out_part = lax.dynamic_update_slice_in_dim(out_part, piece[:, None], plane_place ^ k, 1)
    out_part = out_part.reshape(width, -1)
    in_shard = jnp.concatenate([q_weight[0], key_matrix[0], value_matrix[0]], axis=1)

    seq_ids = lax.dynamic_slice_in_dim(document_index, f // SPANS * PACKED_LENGTH, PACKED_LENGTH)
    seq_index = jnp.arange(PACKED_LENGTH, dtype=jnp.int32)
    before = jnp.concatenate([jnp.full((1,), -1, jnp.int32), seq_ids[:-1]])
    starts = lax.cummax(jnp.where(seq_ids != before, seq_index, 0), axis=0)
    positions = (seq_index - starts).astype(f32)
    freq = rope_base ** (-2.0 * jnp.arange(HALF, dtype=f32) / HEAD_SIZE)
    angle = freq[:, None] * positions[None, :]
    cosine, sine = jnp.cos(angle), jnp.sin(angle)
    id_row = seq_ids[None, :]
    id_col = jnp.broadcast_to(seq_ids[:, None], (PACKED_LENGTH, 128))
    places = jnp.stack([place, t]).astype(jnp.int32)

    normed, gains, q_t, k_t, v_t, q, key, v = project(pieces, head_set, places, cosine, sine)
    gain_a, gain_m = gains[0:1], gains[1:2]
    q_t, dmlp_1, dmlp_2 = tie((q_t, dmlp_1, dmlp_2))
    dmlp_3 = [hop(dmlp_2[:half], 1), hop(dmlp_1[half:], 2)]
    out_t, out_full, lse = attention_forward(q_t, key, v_t, id_row, id_col)
    out_t, dmlp_3 = tie((out_t, dmlp_3))
    dmlp = with_swapped([dmlp_own, dmlp_1, dmlp_2, jnp.concatenate(dmlp_3, axis=0)])
    attended = exchange(out_t, SPANS).reshape(q_heads * HEAD_SIZE, SPAN)

    stream = hidden.astype(f32)
    mine = lax.dynamic_slice_in_dim(attended, t * own, own, 1)
    other = lax.dynamic_slice_in_dim(attended, (1 - t) * own, own, 1)
    mid = stream + dot(mine, out_part, 0, 1) + swap(dot(other, out_part, 0, 1))

    factor_m = rms_factor(mid)
    normed_own = (mid * factor_m * gain_m).astype(bf16)
    n1, n2 = hop(normed_own, 1), hop(normed_own, 2)
    n1, n2, normed_late, in_shard = tie((n1, n2, normed_own, in_shard))
    in_part = lax.all_gather(in_shard, "fsdp", axis=0, tiled=True)
    n3 = hop(normed_late, 3)
    normed_m = with_swapped([normed_own, n1, n2])
    results = feed([normed_m[2 * k:2 * k + 2] + dmlp[2 * k:2 * k + 2] for k in range(3)], unit_weight)
    results, n3 = tie((results, n3))
    n3 = with_swapped([n3])
    dn_got = [swap(result[1]) for result in results]
    n3, dn_got = tie((n3, dn_got))
    normed_m += n3
    results += feed([n3 + dmlp[6:8]], unit_weight)
    dn_last, acts = tie((swap(results[3][1]), [result[5] for result in results]))
    dn_got += [dn_last]
    dn_pair = [result[0] + got.astype(f32) for result, got in zip(results, dn_got)]
    dn_far = [dn_pair[0]] + [hop(dn_pair[k].astype(bf16), k) for k in range(1, PLANE)]
    out_pair = [result[2] + swap(result[3]).astype(f32) for result in results]
    out_low = [out_pair[k].astype(bf16) for k in range(1, PLANE)]
    unit_term = unit_grads(normed_m, [result[4] for result in results], dmlp, acts)
    dn_far, out_low, unit_term = tie((dn_far, out_low, unit_term))
    unit_sum = lax.psum_scatter(unit_term, "fsdp", scatter_dimension=0, tiled=True, axis_index_groups=lines)

    dnormed_m = dn_far[0]
    for far in dn_far[1:]:
        dnormed_m = dnormed_m + far.astype(f32)
    dmid = dstream + norm_backward(mid, factor_m, gain_m, dnormed_m)

    dattn = dmid.astype(bf16)
    dattn_other = swap(dattn)
    dattn = jnp.where(
        t == 0,
        jnp.concatenate([dattn, dattn_other], axis=0),
        jnp.concatenate([dattn_other, dattn], axis=0),
    )
    dout = dot(out_part, dattn, 0, 1).astype(bf16)
    dout = exchange(dout.reshape(SPANS, HEAD_SIZE, SPAN), SPANS)
    out_term = dot(dattn, attended, 0, 1).astype(bf16).reshape(planes, PLANE, shard, -1).transpose(1, 0, 2, 3)
    dout, out_term, out_low = tie((dout, out_term, out_low))
    out_term = exchange(out_term.reshape(PLANE, planes * shard, -1), PLANE)
    out_far = [hop(out_low[2], 3)]
    grads = attention_backward(
        q_t, q, k_t, key, v, dout, out_full, lse, id_row, id_col, cosine, sine, normed, cubes
    )
    grads, out_term, out_far, out_low = tie((grads, out_term, out_far, out_low))

    back = exchange(grads, SPANS)
    out_term = out_term.astype(f32).sum(axis=0).reshape(planes, shard, -1)
    out_grad = lax.dynamic_index_in_dim(out_term, plane_at, 0, keepdims=False)
    out_sums = []
    for k in range(1, planes):
        far = lax.dynamic_index_in_dim(out_term, plane_at ^ k, 0, keepdims=False)
        out_sums.append(hop(far.astype(bf16), PLANE * k))
    back, out_low, unit_sum, in_part, out_sums = tie((back, out_low, unit_sum, in_part, out_sums))
    for far in out_sums:
        out_grad = out_grad + far.astype(f32)
    unit_sum = unit_sum.reshape(PLANE, shard, 3 * units)
    unit_back = [lax.dynamic_index_in_dim(unit_sum, plane_place ^ k, 0, keepdims=False) for k in range(PLANE)]
    unit_back = [piece if k == 0 else hop(piece, k) for k, piece in enumerate(unit_back)]
    out_far += [hop(low, k) for k, low in enumerate(out_low[:2], 1)]
    mine, other, head_terms = input_terms(back, in_part, t.reshape(1).astype(jnp.int32), cubes)
    head_sums = [lax.dynamic_index_in_dim(head_terms, cube_at ^ k, 0, keepdims=False) for k in range(cubes)]
    head_sums = [piece if k == 0 else hop(piece, SPANS * k) for k, piece in enumerate(head_sums)]
    dnormed_a = mine + swap(other)
    input_grad = dmid + norm_backward(stream, rms_factor(stream), gain_a, dnormed_a)

    q_grad, k_grad, v_grad, gain_a_part = head_finish(head_sums, q_weight[0], key_matrix[0], value_matrix[0])

    out_total = out_pair[0]
    for far in out_far:
        out_total = out_total + far.astype(f32)
    output = (mid + out_total).astype(bf16)
    gate_grad, up_grad, down_grad, gain_m_part = unit_finish(
        plane_place.reshape(1).astype(jnp.int32), unit_back, gate_weight[0], up_weight[0]
    )

    gain_parts = jnp.concatenate([gain_a_part, gain_m_part], axis=1).T
    gain_grads = (gain_parts + swap(gain_parts)) / jnp.stack([attn_gain[0], mlp_gain[0]]).astype(f32)
    return (
        output,
        input_grad,
        gain_grads[0:1],
        q_grad[None],
        k_grad[None],
        v_grad[None],
        out_grad[None],
        gain_grads[1:2],
        gate_grad[None],
        up_grad[None],
        down_grad[None],
    )


def solution(mesh):
    rows = P(("fsdp", "tp"), None)
    gain = P(None, "fsdp")
    weight = P(None, "fsdp", "tp")
    return jax.shard_map(
        body,
        mesh=mesh,
        in_specs=(rows, P(), gain, weight, weight, weight, weight, gain, weight, weight, weight, rows),
        out_specs=(rows, rows, gain, weight, weight, weight, weight, gain, weight, weight, weight),
        check_vma=False,
    )
```

```python
import functools
import math

import jax
import jax.numpy as jnp
from jax import lax
from jax.experimental import pallas as pl
from jax.experimental.pallas import tpu as pltpu
from jax.sharding import PartitionSpec as P

HEAD_SIZE = 96
HALF = HEAD_SIZE // 2
SPANS = 8
PLANE = 4
PACKED_LENGTH = 4096
SPAN = PACKED_LENGTH // SPANS

rope_base = 100000.0
norm_eps = 1e-05
masked_score = -1000000000.0
scale = HEAD_SIZE ** (-0.5)
scale_log2 = scale * math.log2(math.e)
bf16 = jnp.bfloat16
brief = pl.CostEstimate(flops=1024, bytes_accessed=1024, transcendentals=0)
f32 = jnp.float32


def dot(left, right, left_dim=1, right_dim=0):
    return lax.dot_general(
        left, right, (((left_dim,), (right_dim,)), ((), ())), preferred_element_type=f32
    )


def hop(value, distance):
    count = lax.axis_size("fsdp")
    return lax.ppermute(value, "fsdp", [(i, i ^ distance) for i in range(count)])


def swap(value):
    return lax.ppermute(value, "tp", [(0, 1), (1, 0)])


def groups_of(size):
    count = lax.axis_size("fsdp")
    return [list(range(first, first + size)) for first in range(0, count, size)]


def exchange(value, size):
    groups = None if size == lax.axis_size("fsdp") else groups_of(size)
    return lax.all_to_all(value, "fsdp", 0, 0, axis_index_groups=groups)


def project_kernel(*refs):
    pieces, (place_ref, head_ref, cos_ref, sin_ref) = refs[:2 * SPANS], refs[2 * SPANS:2 * SPANS + 4]
    normed_ref, gain_ref, q_t_ref, k_t_ref, v_t_ref, q_ref, k_ref, v_ref = refs[2 * SPANS + 4:2 * SPANS + 12]
    in_buf, out_buf, in_sem, out_sem = refs[2 * SPANS + 12:]
    rows = pieces[0].shape[0]
    place, core = place_ref[0], place_ref[1]

    def fetch(pair, part):
        return pltpu.make_async_copy(
            pieces[2 * pair + part],
            in_buf.at[pair % 3, pl.ds(pl.multiple_of((core ^ part) * rows, rows), rows)],
            in_sem.at[pair % 3, part],
        )

    def store(pair):
        return pltpu.make_async_copy(out_buf.at[pair % 2], normed_ref.at[place ^ pair], out_sem.at[pair % 2])

    for pair in range(2):
        for part in range(2):
            fetch(pair, part).start()
    row = lax.broadcasted_iota(jnp.int32, (8, head_ref.shape[1]), 0)
    column = lax.broadcasted_iota(jnp.int32, (8, head_ref.shape[1]), 1)
    pick = (column == row + 3 * HEAD_SIZE).astype(f32).astype(bf16)
    gains = dot(pick, head_ref[...], 1, 1)
    gain = gains[0:1]
    gain_ref[...] = gains
    for pair in range(SPANS):
        for part in range(2):
            fetch(pair, part).wait()
        if pair + 2 < SPANS:
            for part in range(2):
                fetch(pair + 2, part).start()
        if pair >= 2:
            store(pair - 2).wait()
        x = in_buf[pair % 3].astype(f32)
        factor = lax.rsqrt(jnp.mean(x * x, axis=-1, keepdims=True) + norm_eps)
        normed = (x * factor * gain).astype(bf16)
        out_buf[pair % 2] = normed
        store(pair).start()
        product = dot(normed, head_ref[:, :3 * HEAD_SIZE]).T
        here = pl.ds(pl.multiple_of((place ^ pair) * 2 * rows, 2 * rows), 2 * rows)
        cosine, sine = cos_ref[:, here], sin_ref[:, here]
        for number, (t_ref, n_ref) in enumerate(((q_t_ref, q_ref), (k_t_ref, k_ref))):
            first = product[number * HEAD_SIZE:number * HEAD_SIZE + HALF]
            second = product[number * HEAD_SIZE + HALF:(number + 1) * HEAD_SIZE]
            turned = jnp.concatenate(
                [first * cosine - second * sine, second * cosine + first * sine], axis=0
            )
            t_ref[:, here] = turned.astype(bf16)
            n_ref[here, :] = turned.T.astype(bf16)
        value = product[2 * HEAD_SIZE:3 * HEAD_SIZE]
        v_t_ref[:, here] = value.astype(bf16)
        v_ref[here, :] = value.T.astype(bf16)
    for pair in range(SPANS - 2, SPANS):
        store(pair).wait()


def project(pieces, head_set, places, cosine, sine):
    rows, width = pieces[0].shape
    tokens = 2 * SPANS * rows
    vmem = pl.BlockSpec(memory_space=pltpu.VMEM)
    anywhere = pl.BlockSpec(memory_space=pl.ANY)
    return pl.pallas_call(
        project_kernel,
        in_specs=[anywhere] * len(pieces) + [pl.BlockSpec(memory_space=pltpu.SMEM), vmem, vmem, vmem],
        out_specs=[anywhere] + [vmem] * 7,
        out_shape=[
            jax.ShapeDtypeStruct((SPANS, 2 * rows, width), bf16),
            jax.ShapeDtypeStruct((8, width), f32),
        ]
        + [jax.ShapeDtypeStruct((HEAD_SIZE, tokens), bf16)] * 3
        + [jax.ShapeDtypeStruct((tokens, HEAD_SIZE), bf16)] * 3,
        scratch_shapes=[
            pltpu.VMEM((3, 2 * rows, width), bf16),
            pltpu.VMEM((2, 2 * rows, width), bf16),
            pltpu.SemaphoreType.DMA((3, 2)),
            pltpu.SemaphoreType.DMA((2,)),
        ],
        compiler_params=pltpu.CompilerParams(vmem_limit_bytes=56 * 2**20),
        cost_estimate=brief,
        name="project",
    )(*pieces, places, head_set, cosine, sine)


def widened(column):
    return jnp.concatenate([column] * (SPAN // column.shape[1]), axis=1)


def causal_tile():
    key_at = lax.broadcasted_iota(jnp.int32, (SPAN, SPAN), 0)
    query_at = lax.broadcasted_iota(jnp.int32, (SPAN, SPAN), 1)
    return key_at <= query_at


def forward_kernel(q_t_ref, k_ref, v_t_ref, id_row_ref, id_col_ref, out_ref, out_full_ref, lse_ref):
    block = pl.program_id(0)
    query = q_t_ref[...]
    id_row = id_row_ref[...]

    def step(at, carry, diagonal):
        best, total, result = carry
        keys = pl.ds(pl.multiple_of(at * SPAN, SPAN), SPAN)
        scores = dot(k_ref[keys, :], query) * scale_log2
        allowed = widened(id_col_ref[keys, :]) == id_row
        if diagonal:
            allowed = allowed & causal_tile()
        scores = jnp.where(allowed, scores, masked_score)
        larger = jnp.maximum(best, jnp.max(scores, axis=0, keepdims=True))
        weights = jnp.exp2(scores - larger)
        faded = jnp.exp2(best - larger)
        total = total * faded + jnp.sum(weights, axis=0, keepdims=True)
        result = result * faded + dot(v_t_ref[:, keys], weights.astype(bf16))
        return larger, total, result

    carry = (
        jnp.full((1, SPAN), masked_score, f32),
        jnp.zeros((1, SPAN), f32),
        jnp.zeros((HEAD_SIZE, SPAN), f32),
    )
    carry = lax.fori_loop(0, block, lambda at, c: step(at, c, False), carry)
    best, total, result = step(block, carry, True)
    result = result / total
    out_full_ref[...] = result
    out_ref[0] = result.astype(bf16)
    lse_ref[...] = best + jnp.log2(total)


def attention_forward(q_t, k, v_t, id_row, id_col):
    tokens = k.shape[0]
    whole = lambda array: pl.BlockSpec(array.shape, lambda i: (0, 0))
    return pl.pallas_call(
        forward_kernel,
        grid=(SPANS,),
        in_specs=[
            pl.BlockSpec((HEAD_SIZE, SPAN), lambda i: (0, i)),
            whole(k),
            whole(v_t),
            pl.BlockSpec((1, SPAN), lambda i: (0, i)),
            whole(id_col),
        ],
        out_specs=[
            pl.BlockSpec((1, HEAD_SIZE, SPAN), lambda i: (i, 0, 0)),
            pl.BlockSpec((HEAD_SIZE, SPAN), lambda i: (0, i)),
            pl.BlockSpec((1, SPAN), lambda i: (0, i)),
        ],
        out_shape=[
            jax.ShapeDtypeStruct((SPANS, HEAD_SIZE, SPAN), bf16),
            jax.ShapeDtypeStruct((HEAD_SIZE, tokens), f32),
            jax.ShapeDtypeStruct((1, tokens), f32),
        ],
        compiler_params=pltpu.CompilerParams(vmem_limit_bytes=40 * 2**20),
        cost_estimate=brief,
        name="attention_forward",
    )(q_t, k, v_t, id_row, id_col)


def backward_kernel(cubes, q_t_ref, q_ref, k_t_ref, k_ref, v_ref, dout_ref, out_ref, lse_ref, id_row_ref, id_col_ref,
                    cos_ref, sin_ref, normed_ref, grad_ref, delta_ref, dout_n_ref, dq_ref, sum_ref):
    block = pl.program_id(0)

    @pl.when(block == 0)
    def _():
        for at in range(SPANS):
            dout = dout_ref[at]
            here = slice(at * SPAN, (at + 1) * SPAN)
            delta_ref[:, here] = jnp.sum(dout.astype(f32) * out_ref[:, here], axis=0, keepdims=True)
            dout_n_ref[here, :] = dout.astype(f32).T.astype(bf16)
        dq_ref[...] = jnp.zeros(dq_ref.shape, f32)
        sum_ref[...] = jnp.zeros(sum_ref.shape, f32)

    key_t, key, value = k_t_ref[...], k_ref[...], v_ref[...]
    id_col = widened(id_col_ref[...])

    def step(at, carry, diagonal):
        dkey, dvalue = carry
        rows = pl.ds(pl.multiple_of(at * SPAN, SPAN), SPAN)
        scores = dot(key, q_t_ref[:, rows]) * scale_log2 - lse_ref[:, rows]
        allowed = id_col == id_row_ref[:, rows]
        if diagonal:
            allowed = allowed & causal_tile()
        probs = jnp.exp2(jnp.where(allowed, scores, masked_score))
        dprobs = dot(value, dout_ref[at])
        dscores = (probs * (dprobs - delta_ref[:, rows])).astype(bf16)
        dvalue = dvalue + dot(probs.astype(bf16), dout_n_ref[rows, :])
        dkey = dkey + dot(dscores, q_ref[rows, :])
        dq_ref[at] += dot(key_t, dscores)
        return dkey, dvalue

    zero = jnp.zeros((SPAN, HEAD_SIZE), f32)
    carry = step(block, (zero, zero), True)
    dkey, dvalue = lax.fori_loop(block + 1, SPANS, lambda at, c: step(at, c, False), carry)
    cosine, sine = cos_ref[...], sin_ref[...]
    for number, grad in enumerate((dq_ref[block], dkey.T)):
        first = grad[:HALF] * scale
        second = grad[HALF:] * scale
        turned = jnp.concatenate(
            [first * cosine + second * sine, second * cosine - first * sine], axis=0
        )
        grad_ref[block, number * HEAD_SIZE:(number + 1) * HEAD_SIZE, :SPAN] = turned.astype(bf16)
    grad_ref[block, 2 * HEAD_SIZE:, :SPAN] = dvalue.T.astype(bf16)
    sum_ref[...] += dot(grad_ref[block, :, :SPAN], normed_ref[0])

    @pl.when(block == SPANS - 1)
    def _():
        part = sum_ref.shape[1] // SPANS
        shard = part // cubes
        for place in range(SPANS):
            pieces = [
                sum_ref[:, (cube * SPANS + place) * shard:(cube * SPANS + place + 1) * shard] for cube in range(cubes)
            ]
            grad_ref[place, :, SPAN:] = jnp.concatenate(pieces, axis=1).astype(bf16)


def attention_backward(q_t, q, k_t, k, v, dout, out, lse, id_row, id_col, cosine, sine, normed, cubes):
    tokens = k.shape[0]
    width = normed.shape[2]
    whole = lambda array: pl.BlockSpec(array.shape, lambda i: (0,) * array.ndim)
    wide = pl.BlockSpec((HEAD_SIZE, SPAN), lambda i: (0, i))
    tall = pl.BlockSpec((SPAN, HEAD_SIZE), lambda i: (i, 0))
    table = pl.BlockSpec((HALF, SPAN), lambda i: (0, i))
    return pl.pallas_call(
        functools.partial(backward_kernel, cubes),
        grid=(SPANS,),
        in_specs=[
            whole(q_t), whole(q), wide, tall, tall, whole(dout), whole(out), whole(lse), whole(id_row),
            pl.BlockSpec((SPAN, id_col.shape[1]), lambda i: (i, 0)), table, table,
            pl.BlockSpec((1, SPAN, width), lambda i: (i, 0, 0)),
        ],
        out_specs=pl.BlockSpec((SPANS, 3 * HEAD_SIZE, SPAN + width // SPANS), lambda i: (0, 0, 0)),
        out_shape=jax.ShapeDtypeStruct((SPANS, 3 * HEAD_SIZE, SPAN + width // SPANS), bf16),
        scratch_shapes=[
            pltpu.VMEM((1, tokens), f32),
            pltpu.VMEM((tokens, HEAD_SIZE), bf16),
            pltpu.VMEM((SPANS, HEAD_SIZE, SPAN), f32),
            pltpu.VMEM((3 * HEAD_SIZE, width), f32),
        ],
        compiler_params=pltpu.CompilerParams(vmem_limit_bytes=56 * 2**20),
        cost_estimate=brief,
        name="attention_backward",
    )(q_t, q, k_t, k, v, dout, out, lse, id_row, id_col, cosine, sine, normed)


def head_finish_kernel(*refs):
    sum_refs, (q_ref, k_ref, v_ref, q_out, k_out, v_out, product_ref) = refs[:-7], refs[-7:]
    total = sum_refs[0][...].astype(f32)
    for ref in sum_refs[1:]:
        total = total + ref[...].astype(f32)
    total = total.T
    product = jnp.zeros(product_ref.shape, f32)
    at = 0
    for ref, out in ((q_ref, q_out), (k_ref, k_out), (v_ref, v_out)):
        grad = total[:, at:at + out.shape[1]]
        at += out.shape[1]
        out[...] = grad
        product = product + jnp.sum(grad * ref[...].astype(f32), axis=1, keepdims=True)
    product_ref[...] = product


def head_finish(sums, q_weight, k_weight, v_weight):
    vmem = pl.BlockSpec(memory_space=pltpu.VMEM)
    return pl.pallas_call(
        head_finish_kernel,
        in_specs=[vmem] * (len(sums) + 3),
        out_specs=[vmem] * 4,
        out_shape=[jax.ShapeDtypeStruct(w.shape, f32) for w in (q_weight, k_weight, v_weight)]
        + [jax.ShapeDtypeStruct((q_weight.shape[0], 1), f32)],
        compiler_params=pltpu.CompilerParams(vmem_limit_bytes=32 * 2**20),
        name="head_finish",
    )(*sums, q_weight, k_weight, v_weight)


def unit_finish_kernel(place_ref, *refs):
    piece_refs, (gate_w_ref, up_w_ref, gate_out, up_out, down_out, product_ref) = refs[:PLANE], refs[PLANE:]
    units = gate_out.shape[1] // PLANE
    for link, piece_ref in enumerate(piece_refs):
        here = pl.ds(pl.multiple_of((place_ref[0] ^ link) * units, units), units)
        for number, out in enumerate((gate_out, up_out, down_out)):
            out[:, here] = piece_ref[:, number * units:(number + 1) * units].astype(f32)
    product_ref[...] = jnp.sum(
        gate_out[...] * gate_w_ref[...].astype(f32) + up_out[...] * up_w_ref[...].astype(f32), axis=1, keepdims=True
    )


def unit_finish(place, pieces, gate_weight, up_weight):
    vmem = pl.BlockSpec(memory_space=pltpu.VMEM)
    return pl.pallas_call(
        unit_finish_kernel,
        in_specs=[pl.BlockSpec(memory_space=pltpu.SMEM)] + [vmem] * (PLANE + 2),
        out_specs=[vmem] * 4,
        out_shape=[jax.ShapeDtypeStruct(gate_weight.shape, f32)] * 3
        + [jax.ShapeDtypeStruct((gate_weight.shape[0], 1), f32)],
        compiler_params=pltpu.CompilerParams(vmem_limit_bytes=32 * 2**20),
        name="unit_finish",
    )(place, *pieces, gate_weight, up_weight)


def unit_grad_kernel(*refs):
    tables, out_ref = (refs[:3 * PLANE], refs[3 * PLANE:6 * PLANE]), refs[6 * PLANE]
    column = 0
    for table in tables:
        total = None
        for k, right in enumerate(table[2 * PLANE:]):
            left = jnp.concatenate([table[2 * k][...], table[2 * k + 1][...]], axis=0)
            term = dot(left, right[...], 0, 0)
            total = term if total is None else total + term
        out_ref[:, column:column + total.shape[1]] = total.astype(bf16)
        column += total.shape[1]


def unit_grads(normed, dgate_up, dout, act):
    tokens, width = normed[0].shape
    rows = width // 4
    whole = lambda array: pl.BlockSpec(array.shape, lambda i: (0, 0))
    left = [pl.BlockSpec((tokens, rows), lambda i: (0, i))] * (2 * PLANE)
    columns = dgate_up[0].shape[1] + act[0].shape[1]
    return pl.pallas_call(
        unit_grad_kernel,
        grid=(width // rows,),
        in_specs=left + [whole(part) for part in dgate_up] + left + [whole(part) for part in act],
        out_specs=pl.BlockSpec((rows, columns), lambda i: (i, 0)),
        out_shape=jax.ShapeDtypeStruct((width, columns), bf16),
        compiler_params=pltpu.CompilerParams(vmem_limit_bytes=48 * 2**20),
        cost_estimate=brief,
        name="unit_grads",
    )(*normed, *dgate_up, *dout, *act)


def feed_kernel(pairs, *refs):
    ins, weight_ref, refs = refs[:4 * pairs], refs[4 * pairs], refs[4 * pairs + 1:]
    units = weight_ref.shape[1] // 3
    weight = weight_ref[:, :2 * units]
    down_weight = weight_ref[:, 2 * units:]
    for pair in range(pairs):
        own_ref, other_ref, d_own_ref, d_other_ref = ins[4 * pair:4 * pair + 4]
        kept_ref, sent_ref, out_kept_ref, out_sent_ref, dgate_up_ref, act_ref = refs[6 * pair:6 * pair + 6]
        rows = own_ref.shape[0]
        gate_up = dot(jnp.concatenate([own_ref[...], other_ref[...]], axis=0), weight)
        dact = dot(jnp.concatenate([d_own_ref[...], d_other_ref[...]], axis=0), down_weight)
        gate, up = gate_up[:, :units], gate_up[:, units:]
        sigma = 1.0 / (1.0 + jnp.exp(-gate))
        silu = gate * sigma
        dgate_up_ref[:, :units] = (dact * up * sigma * (1.0 + gate * (1.0 - sigma))).astype(bf16)
        dgate_up_ref[:, units:] = (dact * silu).astype(bf16)
        act_ref[...] = (silu * up).astype(bf16)
        dnormed = dot(dgate_up_ref[...], weight, 1, 1)
        kept_ref[...] = dnormed[:rows]
        sent_ref[...] = dnormed[rows:].astype(bf16)
        out = dot(act_ref[...], down_weight, 1, 1)
        out_kept_ref[...] = out[:rows]
        out_sent_ref[...] = out[rows:].astype(bf16)


def feed(rows_list, weight):
    pairs = len(rows_list)
    rows, width = rows_list[0][0].shape
    units = weight.shape[1] // 3
    vmem = pl.BlockSpec(memory_space=pltpu.VMEM)
    halves = [jax.ShapeDtypeStruct((rows, width), f32), jax.ShapeDtypeStruct((rows, width), bf16)]
    shapes = (
        halves * 2 + [jax.ShapeDtypeStruct((2 * rows, 2 * units), bf16), jax.ShapeDtypeStruct((2 * rows, units), bf16)]
    ) * pairs
    ins = [part for group in rows_list for part in group]
    outs = pl.pallas_call(
        functools.partial(feed_kernel, pairs),
        in_specs=[vmem] * (len(ins) + 1),
        out_specs=[vmem] * len(shapes),
        out_shape=shapes,
        compiler_params=pltpu.CompilerParams(vmem_limit_bytes=48 * 2**20),
        cost_estimate=brief,
        name="feed",
    )(*ins, weight)
    return [outs[6 * pair:6 * pair + 6] for pair in range(pairs)]


def back_kernel(core_ref, back_ref, weight_ref, mine_ref, other_ref, head_ref, table_ref):
    heads = back_ref.shape[0]
    kv_heads = (table_ref.shape[0] // HEAD_SIZE - heads) // 2
    per_kv = heads // kv_heads
    cubes, _, shard = head_ref.shape

    def put(at, value):
        table_ref[at:at + HEAD_SIZE, :] = value[:, :SPAN]
        for cube in range(cubes):
            head_ref[cube, at:at + HEAD_SIZE, :] = value[:, SPAN + cube * shard:SPAN + (cube + 1) * shard]

    for head in range(heads):
        put(head * HEAD_SIZE, back_ref[head, :HEAD_SIZE, :])
    for number in range(2):
        here = slice((number + 1) * HEAD_SIZE, (number + 2) * HEAD_SIZE)
        for head in range(kv_heads):
            total = back_ref[head * per_kv, here, :].astype(f32)
            for copy in range(1, per_kv):
                total = total + back_ref[head * per_kv + copy, here, :].astype(f32)
            put((heads + number * kv_heads + head) * HEAD_SIZE, total.astype(bf16))
    rows = mine_ref.shape[0]
    both = dot(weight_ref[...], table_ref[...])
    low, high = both[:, :rows].T, both[:, rows:].T
    first = core_ref[0] == 0
    mine_ref[...] = jnp.where(first, low, high)
    other_ref[...] = jnp.where(first, high, low)


def input_terms(back, weight, core, cubes):
    vmem = pl.BlockSpec(memory_space=pltpu.VMEM)
    width, features = weight.shape
    rows = SPAN // 2
    shard = (back.shape[2] - SPAN) // cubes
    return pl.pallas_call(
        back_kernel,
        in_specs=[pl.BlockSpec(memory_space=pltpu.SMEM), vmem, vmem],
        out_specs=[vmem] * 3,
        out_shape=[jax.ShapeDtypeStruct((rows, width), f32)] * 2
        + [jax.ShapeDtypeStruct((cubes, features, shard), bf16)],
        scratch_shapes=[pltpu.VMEM((features, SPAN), bf16)],
        compiler_params=pltpu.CompilerParams(vmem_limit_bytes=56 * 2**20),
        cost_estimate=brief,
        name="input_terms",
    )(core, back, weight)


tie = lax.optimization_barrier


def with_swapped(pieces):
    return [part for piece in pieces for part in (piece, swap(piece))]


def rms_factor(stream):
    return lax.rsqrt(jnp.mean(stream * stream, axis=-1, keepdims=True) + norm_eps)


def norm_backward(stream, factor, gain, dnormed):
    scaled = dnormed * gain
    return factor * scaled - stream * factor**3 * jnp.mean(scaled * stream, axis=-1, keepdims=True)


def body(
    hidden,
    document_index,
    attn_gain,
    q_weight,
    key_matrix,
    value_matrix,
    out_weight,
    mlp_gain,
    gate_weight,
    up_weight,
    down_weight,
    cotangent,
):
    count = lax.axis_size("fsdp")
    planes = count // PLANE
    f = lax.axis_index("fsdp")
    t = lax.axis_index("tp")
    place = f % SPANS
    plane_at = f // PLANE
    own, width = hidden.shape
    shard = q_weight.shape[1]
    q_heads = q_weight.shape[2] // HEAD_SIZE
    kv_heads = key_matrix.shape[2] // HEAD_SIZE
    per_kv = q_heads // kv_heads
    units = gate_weight.shape[2] // PLANE

    def by_head(weight, heads, copies):
        cut = weight[0].reshape(shard, heads, HEAD_SIZE).transpose(1, 0, 2)
        return jnp.repeat(cut, copies, axis=0)

    gains_own = jnp.stack([attn_gain[0], mlp_gain[0]], axis=-1)
    sent = jnp.concatenate(
        [
            by_head(q_weight, q_heads, 1),
            by_head(key_matrix, kv_heads, per_kv),
            by_head(value_matrix, kv_heads, per_kv),
            jnp.broadcast_to(gains_own[None], (SPANS, shard, 2)),
        ],
        axis=-1,
    )
    sent = jnp.tile(sent, (count // SPANS, 1, 1))

    plane_place = f % PLANE
    cubes = count // SPANS
    cube_at = f // SPANS
    half = own // 2
    unit_set = jnp.concatenate(
        [w[0].reshape(shard, PLANE, units).transpose(1, 0, 2) for w in (gate_weight, up_weight, down_weight)],
        axis=-1,
    )
    lines = [list(range(first, count, PLANE)) for first in range(PLANE)]
    lines = [list(range(first, count, PLANE)) for first in range(PLANE)]
    p1, p2, p4 = hop(hidden, 1), hop(hidden, 2), hop(hidden, 4)
    head_set = exchange(sent, count).reshape(width, -1)
    out_far = [hop(out_weight[0], PLANE * k) for k in range(1, planes)]
    p4, document_index, cotangent = tie((p4, document_index, cotangent))
    p5, p6 = hop(p4, 1), hop(p4, 2)
    p3 = [hop(p2[:half], 1), hop(p1[half:], 2)]
    p7 = [hop(p6[:half], 1), hop(p5[half:], 2)]
    p3, p7 = jnp.concatenate(p3, axis=0), jnp.concatenate(p7, axis=0)
    unit_set, head_set = tie((unit_set, head_set))
    unit_own = exchange(unit_set, PLANE).reshape(PLANE * shard, 3 * units)

    seq_ids = lax.dynamic_slice_in_dim(document_index, f // SPANS * PACKED_LENGTH, PACKED_LENGTH)
    seq_index = jnp.arange(PACKED_LENGTH, dtype=jnp.int32)
    before = jnp.concatenate([jnp.full((1,), -1, jnp.int32), seq_ids[:-1]])
    starts = lax.cummax(jnp.where(seq_ids != before, seq_index, 0), axis=0)
    positions = (seq_index - starts).astype(f32)
    freq = rope_base ** (-2.0 * jnp.arange(HALF, dtype=f32) / HEAD_SIZE)
    angle = freq[:, None] * positions[None, :]
    cosine, sine = jnp.cos(angle), jnp.sin(angle)
    id_row = seq_ids[None, :]
    id_col = jnp.broadcast_to(seq_ids[:, None], (PACKED_LENGTH, 128))

    own_ids = lax.dynamic_slice_in_dim(document_index, f * SPAN + t * own, own)
    dstream = cotangent.astype(f32) * (own_ids != 0).astype(f32)[:, None]
    dmlp_own = dstream.astype(bf16)
    head_set, dmlp_own, cosine, sine, id_col, p3, out_far = tie(
        (head_set, dmlp_own, cosine, sine, id_col, p3, out_far)
    )
    pieces = with_swapped([hidden, p1, p2, p3, p4, p5, p6, p7])
    out_0 = jnp.zeros((planes,) + out_weight.shape[1:], bf16)
    for k, piece in enumerate([out_weight[0]] + out_far):
        out_0 = lax.dynamic_update_slice_in_dim(out_0, piece[None], plane_at ^ k, 0)
    out_1, out_2 = hop(out_0, 1), hop(out_0, 2)
    in_shard = jnp.concatenate([q_weight[0], key_matrix[0], value_matrix[0]], axis=1)

    places = jnp.stack([place, t]).astype(jnp.int32)

    normed, gains, q_t, k_t, v_t, q, key, v = project(pieces, head_set, places, cosine, sine)
    gain_a, gain_m = gains[0:1], gains[1:2]
    q_t, out_0, out_1, out_2, dmlp_own, unit_own = tie((q_t, out_0, out_1, out_2, dmlp_own, unit_own))
    unit_weight = lax.all_gather(unit_own, "fsdp", axis=0, tiled=True, axis_index_groups=lines)
    out_3 = hop(out_0, 3)
    dmlp_1, dmlp_2 = hop(dmlp_own, 1), hop(dmlp_own, 2)
    out_t, out_full, lse = attention_forward(q_t, key, v_t, id_row, id_col)
    out_t, dmlp_1, dmlp_2, out_3, dmlp_late = tie((out_t, dmlp_1, dmlp_2, out_3, dmlp_own))
    dmlp_3 = hop(dmlp_late, 3)
    attended = exchange(out_t, SPANS)
    attended, dmlp_3, in_shard = tie((attended, dmlp_3, in_shard))
    in_part = lax.all_gather(in_shard, "fsdp", axis=0, tiled=True)
    attended = attended.reshape(q_heads * HEAD_SIZE, SPAN)
    out_part = jnp.zeros((planes, PLANE, shard, out_0.shape[2]), bf16)
    for k, piece in enumerate((out_0, out_1, out_2, out_3)):
        out_part = lax.dynamic_update_slice_in_dim(out_part, piece[:, None], plane_place ^ k, 1)
    out_part = out_part.reshape(width, -1)

    stream = hidden.astype(f32)
    mine = lax.dynamic_slice_in_dim(attended, t * own, own, 1)
    other = lax.dynamic_slice_in_dim(attended, (1 - t) * own, own, 1)
    mid = stream + dot(mine, out_part, 0, 1) + swap(dot(other, out_part, 0, 1))

    factor_m = rms_factor(mid)
    normed_own = (mid * factor_m * gain_m).astype(bf16)
    dmlp = with_swapped([dmlp_own, dmlp_1, dmlp_2, dmlp_3])
    n1, n2 = hop(normed_own, 1), hop(normed_own, 2)
    n1, n2, normed_late = tie((n1, n2, normed_own))
    n3 = hop(normed_late, 3)
    normed_m = with_swapped([normed_own, n1, n2])
    second, third = feed([normed_m[2 * k:2 * k + 2] + dmlp[2 * k:2 * k + 2] for k in (1, 2)], unit_weight)
    second, third, n3 = tie((second, third, n3))
    normed_m += with_swapped([n3])
    dn_got = [swap(second[1]), swap(third[1])]
    first, fourth = feed([normed_m[2 * k:2 * k + 2] + dmlp[2 * k:2 * k + 2] for k in (0, 3)], unit_weight)
    first, fourth, dn_got = tie((first, fourth, dn_got))
    results = [first, second, third, fourth]
    dn_got = [swap(first[1])] + dn_got + [swap(fourth[1])]
    dn_pair = [result[0] + got.astype(f32) for result, got in zip(results, dn_got)]
    dn_far = [dn_pair[0]] + [hop(dn_pair[k].astype(bf16), k) for k in range(1, PLANE)]
    out_pair = [result[2] + swap(result[3]).astype(f32) for result in results]
    out_low = [out_pair[k].astype(bf16) for k in range(1, PLANE)]
    unit_term = unit_grads(normed_m, [result[4] for result in results], dmlp, [result[5] for result in results])
    dn_far, out_low, in_part, unit_term = tie((dn_far, out_low, in_part, unit_term))
    unit_sum = lax.psum_scatter(unit_term, "fsdp", scatter_dimension=0, tiled=True, axis_index_groups=lines)
    out_far = [hop(low, k) for k, low in enumerate(out_low[:2], 1)]

    dnormed_m = dn_far[0]
    for far in dn_far[1:]:
        dnormed_m = dnormed_m + far.astype(f32)
    dmid = dstream + norm_backward(mid, factor_m, gain_m, dnormed_m)

    dattn = dmid.astype(bf16)
    dattn_other = swap(dattn)
    dattn = jnp.where(
        t == 0,
        jnp.concatenate([dattn, dattn_other], axis=0),
        jnp.concatenate([dattn_other, dattn], axis=0),
    )
    dout = dot(out_part, dattn, 0, 1).astype(bf16)
    dout = exchange(dout.reshape(SPANS, HEAD_SIZE, SPAN), SPANS)
    out_term = dot(dattn, attended, 0, 1).astype(bf16).reshape(planes, PLANE, shard, -1).transpose(1, 0, 2, 3)
    dout, out_term, out_low, out_far = tie((dout, out_term, out_low, out_far))
    out_term = exchange(out_term.reshape(PLANE, planes * shard, -1), PLANE)
    out_far += [hop(out_low[2], 3)]
    grads = attention_backward(
        q_t, q, k_t, key, v, dout, out_full, lse, id_row, id_col, cosine, sine, normed, cubes
    )
    grads, out_term, out_far, unit_sum = tie((grads, out_term, out_far, unit_sum))

    back = exchange(grads, SPANS)
    unit_sum = unit_sum.reshape(PLANE, shard, 3 * units)
    unit_back = [lax.dynamic_index_in_dim(unit_sum, plane_place ^ k, 0, keepdims=False) for k in range(PLANE)]
    unit_back = [piece if k == 0 else hop(piece, k) for k, piece in enumerate(unit_back)]
    out_term = out_term.astype(f32).sum(axis=0).reshape(planes, shard, -1)
    out_grad = lax.dynamic_index_in_dim(out_term, plane_at, 0, keepdims=False)
    out_sums = []
    for k in range(1, planes):
        far = lax.dynamic_index_in_dim(out_term, plane_at ^ k, 0, keepdims=False)
        out_sums.append(hop(far.astype(bf16), PLANE * k))
    back, out_sums, unit_back = tie((back, out_sums, unit_back))
    for far in out_sums:
        out_grad = out_grad + far.astype(f32)
    mine, other, head_terms = input_terms(back, in_part, t.reshape(1).astype(jnp.int32), cubes)
    head_sums = [lax.dynamic_index_in_dim(head_terms, cube_at ^ k, 0, keepdims=False) for k in range(cubes)]
    head_sums = [piece if k == 0 else hop(piece, SPANS * k) for k, piece in enumerate(head_sums)]
    dnormed_a = mine + swap(other)
    input_grad = dmid + norm_backward(stream, rms_factor(stream), gain_a, dnormed_a)
    input_grad, head_sums = tie((input_grad, head_sums))

    q_grad, k_grad, v_grad, gain_a_part = head_finish(head_sums, q_weight[0], key_matrix[0], value_matrix[0])

    out_total = out_pair[0]
    for far in out_far:
        out_total = out_total + far.astype(f32)
    output = (mid + out_total).astype(bf16)
    gate_grad, up_grad, down_grad, gain_m_part = unit_finish(
        plane_place.reshape(1).astype(jnp.int32), unit_back, gate_weight[0], up_weight[0]
    )

    gain_parts = jnp.concatenate([gain_a_part, gain_m_part], axis=1).T
    gain_grads = (gain_parts + swap(gain_parts)) / jnp.stack([attn_gain[0], mlp_gain[0]]).astype(f32)
    return (
        output,
        input_grad,
        gain_grads[0:1],
        q_grad[None],
        k_grad[None],
        v_grad[None],
        out_grad[None],
        gain_grads[1:2],
        gate_grad[None],
        up_grad[None],
        down_grad[None],
    )


def solution(mesh):
    rows = P(("fsdp", "tp"), None)
    gain = P(None, "fsdp")
    weight = P(None, "fsdp", "tp")
    return jax.shard_map(
        body,
        mesh=mesh,
        in_specs=(rows, P(), gain, weight, weight, weight, weight, gain, weight, weight, weight, rows),
        out_specs=(rows, rows, gain, weight, weight, weight, weight, gain, weight, weight, weight),
        check_vma=False,
    )
```

```python
import functools
import math

import jax
import jax.numpy as jnp
from jax import lax
from jax.experimental import pallas as pl
from jax.experimental.pallas import tpu as pltpu
from jax.sharding import PartitionSpec as P

HEAD_SIZE = 96
HALF = HEAD_SIZE // 2
SPANS = 8
KV_HEADS = SPANS // 2
PLANE = 4
PACKED_LENGTH = 4096
SPAN = PACKED_LENGTH // SPANS

rope_base = 100000.0
norm_eps = 1e-05
masked_score = -1000000000.0
scale = HEAD_SIZE ** (-0.5)
scale_log2 = scale * math.log2(math.e)
bf16 = jnp.bfloat16
brief = pl.CostEstimate(flops=1024, bytes_accessed=1024, transcendentals=0)
f32 = jnp.float32


def dot(left, right, left_dim=1, right_dim=0):
    return lax.dot_general(
        left, right, (((left_dim,), (right_dim,)), ((), ())), preferred_element_type=f32
    )


def hop(value, distance):
    count = lax.axis_size("fsdp")
    return lax.ppermute(value, "fsdp", [(i, i ^ distance) for i in range(count)])


def swap(value):
    return lax.ppermute(value, "tp", [(0, 1), (1, 0)])


def groups_of(size):
    count = lax.axis_size("fsdp")
    return [list(range(first, first + size)) for first in range(0, count, size)]


def exchange(value, size):
    groups = None if size == lax.axis_size("fsdp") else groups_of(size)
    return lax.all_to_all(value, "fsdp", 0, 0, axis_index_groups=groups)


def head_cut_kernel(q_ref, k_ref, v_ref, gain_ref, out_ref):
    gains = gain_ref[...].astype(f32)
    for place in range(SPANS):
        parts = []
        for ref in (q_ref, k_ref, v_ref):
            head = place * ref.shape[1] // (SPANS * HEAD_SIZE)
            parts.append(ref[:, head * HEAD_SIZE:(head + 1) * HEAD_SIZE].astype(f32))
        cut = jnp.concatenate(parts + [gains], axis=1).astype(bf16)
        for first in range(0, out_ref.shape[0], SPANS):
            out_ref[first + place] = cut


def head_cut(count, q_weight, k_weight, v_weight, gains):
    vmem = pl.BlockSpec(memory_space=pltpu.VMEM)
    shard = q_weight.shape[0]
    return pl.pallas_call(
        head_cut_kernel,
        in_specs=[vmem] * 4,
        out_specs=vmem,
        out_shape=jax.ShapeDtypeStruct((count, shard, 3 * HEAD_SIZE + 2), bf16),
        compiler_params=pltpu.CompilerParams(vmem_limit_bytes=32 * 2**20),
        cost_estimate=brief,
        name="head_cut",
    )(q_weight, k_weight, v_weight, gains)


def project_kernel(*refs):
    pieces, (place_ref, head_ref, cos_ref, sin_ref) = refs[:2 * SPANS], refs[2 * SPANS:2 * SPANS + 4]
    normed_ref, gain_ref, q_t_ref, k_t_ref, v_t_ref, q_ref, k_ref, v_ref = refs[2 * SPANS + 4:2 * SPANS + 12]
    in_buf, out_buf, in_sem, out_sem = refs[2 * SPANS + 12:]
    rows = pieces[0].shape[0]
    place, core = place_ref[0], place_ref[1]

    def fetch(pair, part):
        return pltpu.make_async_copy(
            pieces[2 * pair + part],
            in_buf.at[pair % 3, pl.ds(pl.multiple_of((core ^ part) * rows, rows), rows)],
            in_sem.at[pair % 3, part],
        )

    def store(pair):
        return pltpu.make_async_copy(out_buf.at[pair % 2], normed_ref.at[place ^ pair], out_sem.at[pair % 2])

    for pair in range(2):
        for part in range(2):
            fetch(pair, part).start()
    row = lax.broadcasted_iota(jnp.int32, (8, head_ref.shape[1]), 0)
    column = lax.broadcasted_iota(jnp.int32, (8, head_ref.shape[1]), 1)
    pick = (column == row + 3 * HEAD_SIZE).astype(f32).astype(bf16)
    gains = dot(pick, head_ref[...], 1, 1)
    gain = gains[0:1]
    gain_ref[...] = gains
    for pair in range(SPANS):
        for part in range(2):
            fetch(pair, part).wait()
        if pair + 2 < SPANS:
            for part in range(2):
                fetch(pair + 2, part).start()
        if pair >= 2:
            store(pair - 2).wait()
        x = in_buf[pair % 3].astype(f32)
        factor = lax.rsqrt(jnp.mean(x * x, axis=-1, keepdims=True) + norm_eps)
        normed = (x * factor * gain).astype(bf16)
        out_buf[pair % 2] = normed
        store(pair).start()
        product = dot(normed, head_ref[:, :3 * HEAD_SIZE]).T
        here = pl.ds(pl.multiple_of((place ^ pair) * 2 * rows, 2 * rows), 2 * rows)
        cosine, sine = cos_ref[:, here], sin_ref[:, here]
        for number, (t_ref, n_ref) in enumerate(((q_t_ref, q_ref), (k_t_ref, k_ref))):
            first = product[number * HEAD_SIZE:number * HEAD_SIZE + HALF]
            second = product[number * HEAD_SIZE + HALF:(number + 1) * HEAD_SIZE]
            turned = jnp.concatenate(
                [first * cosine - second * sine, second * cosine + first * sine], axis=0
            )
            t_ref[:, here] = turned.astype(bf16)
            n_ref[here, :] = turned.T.astype(bf16)
        value = product[2 * HEAD_SIZE:3 * HEAD_SIZE]
        v_t_ref[:, here] = value.astype(bf16)
        v_ref[here, :] = value.T.astype(bf16)
    for pair in range(SPANS - 2, SPANS):
        store(pair).wait()


def project(pieces, head_set, places, cosine, sine):
    rows, width = pieces[0].shape
    tokens = 2 * SPANS * rows
    vmem = pl.BlockSpec(memory_space=pltpu.VMEM)
    anywhere = pl.BlockSpec(memory_space=pl.ANY)
    return pl.pallas_call(
        project_kernel,
        in_specs=[anywhere] * len(pieces) + [pl.BlockSpec(memory_space=pltpu.SMEM), vmem, vmem, vmem],
        out_specs=[anywhere] + [vmem] * 7,
        out_shape=[
            jax.ShapeDtypeStruct((SPANS, 2 * rows, width), bf16),
            jax.ShapeDtypeStruct((8, width), f32),
        ]
        + [jax.ShapeDtypeStruct((HEAD_SIZE, tokens), bf16)] * 3
        + [jax.ShapeDtypeStruct((tokens, HEAD_SIZE), bf16)] * 3,
        scratch_shapes=[
            pltpu.VMEM((3, 2 * rows, width), bf16),
            pltpu.VMEM((2, 2 * rows, width), bf16),
            pltpu.SemaphoreType.DMA((3, 2)),
            pltpu.SemaphoreType.DMA((2,)),
        ],
        compiler_params=pltpu.CompilerParams(vmem_limit_bytes=56 * 2**20),
        cost_estimate=brief,
        name="project",
    )(*pieces, places, head_set, cosine, sine)


def widened(column):
    return jnp.concatenate([column] * (SPAN // column.shape[1]), axis=1)


def causal_tile():
    key_at = lax.broadcasted_iota(jnp.int32, (SPAN, SPAN), 0)
    query_at = lax.broadcasted_iota(jnp.int32, (SPAN, SPAN), 1)
    return key_at <= query_at


def forward_kernel(q_t_ref, k_ref, v_t_ref, id_row_ref, id_col_ref, out_ref, out_full_ref, lse_ref):
    block = pl.program_id(0)
    query = q_t_ref[...]
    id_row = id_row_ref[...]

    def step(at, carry, diagonal):
        best, total, result = carry
        keys = pl.ds(pl.multiple_of(at * SPAN, SPAN), SPAN)
        scores = dot(k_ref[keys, :], query) * scale_log2
        allowed = widened(id_col_ref[keys, :]) == id_row
        if diagonal:
            allowed = allowed & causal_tile()
        scores = jnp.where(allowed, scores, masked_score)
        larger = jnp.maximum(best, jnp.max(scores, axis=0, keepdims=True))
        weights = jnp.exp2(scores - larger)
        faded = jnp.exp2(best - larger)
        total = total * faded + jnp.sum(weights, axis=0, keepdims=True)
        result = result * faded + dot(v_t_ref[:, keys], weights.astype(bf16))
        return larger, total, result

    carry = (
        jnp.full((1, SPAN), masked_score, f32),
        jnp.zeros((1, SPAN), f32),
        jnp.zeros((HEAD_SIZE, SPAN), f32),
    )
    carry = lax.fori_loop(0, block, lambda at, c: step(at, c, False), carry)
    best, total, result = step(block, carry, True)
    result = result / total
    out_full_ref[...] = result
    out_ref[0] = result.astype(bf16)
    lse_ref[...] = best + jnp.log2(total)


def attention_forward(q_t, k, v_t, id_row, id_col):
    tokens = k.shape[0]
    whole = lambda array: pl.BlockSpec(array.shape, lambda i: (0, 0))
    return pl.pallas_call(
        forward_kernel,
        grid=(SPANS,),
        in_specs=[
            pl.BlockSpec((HEAD_SIZE, SPAN), lambda i: (0, i)),
            whole(k),
            whole(v_t),
            pl.BlockSpec((1, SPAN), lambda i: (0, i)),
            whole(id_col),
        ],
        out_specs=[
            pl.BlockSpec((1, HEAD_SIZE, SPAN), lambda i: (i, 0, 0)),
            pl.BlockSpec((HEAD_SIZE, SPAN), lambda i: (0, i)),
            pl.BlockSpec((1, SPAN), lambda i: (0, i)),
        ],
        out_shape=[
            jax.ShapeDtypeStruct((SPANS, HEAD_SIZE, SPAN), bf16),
            jax.ShapeDtypeStruct((HEAD_SIZE, tokens), f32),
            jax.ShapeDtypeStruct((1, tokens), f32),
        ],
        compiler_params=pltpu.CompilerParams(vmem_limit_bytes=40 * 2**20),
        cost_estimate=brief,
        name="attention_forward",
    )(q_t, k, v_t, id_row, id_col)


def backward_kernel(q_t_ref, q_ref, k_t_ref, k_ref, v_ref, dout_ref, out_ref, lse_ref, id_row_ref, id_col_ref,
                    cos_ref, sin_ref, normed_ref, grad_ref, weight_grad_ref, delta_ref, dout_n_ref, dq_ref, sum_ref):
    block = pl.program_id(0)

    @pl.when(block == 0)
    def _():
        for at in range(SPANS):
            dout = dout_ref[at]
            here = slice(at * SPAN, (at + 1) * SPAN)
            delta_ref[:, here] = jnp.sum(dout.astype(f32) * out_ref[:, here], axis=0, keepdims=True)
            dout_n_ref[here, :] = dout.astype(f32).T.astype(bf16)
        dq_ref[...] = jnp.zeros(dq_ref.shape, f32)
        sum_ref[...] = jnp.zeros(sum_ref.shape, f32)

    key_t, key, value = k_t_ref[...], k_ref[...], v_ref[...]
    id_col = widened(id_col_ref[...])

    def step(at, carry, diagonal):
        dkey, dvalue = carry
        rows = pl.ds(pl.multiple_of(at * SPAN, SPAN), SPAN)
        scores = dot(key, q_t_ref[:, rows]) * scale_log2 - lse_ref[:, rows]
        allowed = id_col == id_row_ref[:, rows]
        if diagonal:
            allowed = allowed & causal_tile()
        probs = jnp.exp2(jnp.where(allowed, scores, masked_score))
        dprobs = dot(value, dout_ref[at])
        dscores = (probs * (dprobs - delta_ref[:, rows])).astype(bf16)
        dvalue = dvalue + dot(probs.astype(bf16), dout_n_ref[rows, :])
        dkey = dkey + dot(dscores, q_ref[rows, :])
        dq_ref[at] += dot(key_t, dscores)
        return dkey, dvalue

    zero = jnp.zeros((SPAN, HEAD_SIZE), f32)
    carry = step(block, (zero, zero), True)
    dkey, dvalue = lax.fori_loop(block + 1, SPANS, lambda at, c: step(at, c, False), carry)
    cosine, sine = cos_ref[...], sin_ref[...]
    for number, grad in enumerate((dq_ref[block], dkey.T)):
        first = grad[:HALF] * scale
        second = grad[HALF:] * scale
        turned = jnp.concatenate(
            [first * cosine + second * sine, second * cosine - first * sine], axis=0
        )
        grad_ref[0, number * HEAD_SIZE:(number + 1) * HEAD_SIZE, :] = turned.astype(bf16)
    grad_ref[0, 2 * HEAD_SIZE:, :] = dvalue.T.astype(bf16)
    sum_ref[...] += dot(grad_ref[0], normed_ref[0])

    @pl.when(block == SPANS - 1)
    def _():
        weight_grad_ref[...] = sum_ref[...].T.astype(bf16)


def attention_backward(q_t, q, k_t, k, v, dout, out, lse, id_row, id_col, cosine, sine, normed):
    tokens = k.shape[0]
    width = normed.shape[2]
    whole = lambda array: pl.BlockSpec(array.shape, lambda i: (0,) * array.ndim)
    wide = pl.BlockSpec((HEAD_SIZE, SPAN), lambda i: (0, i))
    tall = pl.BlockSpec((SPAN, HEAD_SIZE), lambda i: (i, 0))
    table = pl.BlockSpec((HALF, SPAN), lambda i: (0, i))
    return pl.pallas_call(
        backward_kernel,
        grid=(SPANS,),
        in_specs=[
            whole(q_t), whole(q), wide, tall, tall, whole(dout), whole(out), whole(lse), whole(id_row),
            pl.BlockSpec((SPAN, id_col.shape[1]), lambda i: (i, 0)), table, table,
            pl.BlockSpec((1, SPAN, width), lambda i: (i, 0, 0)),
        ],
        out_specs=[
            pl.BlockSpec((1, 3 * HEAD_SIZE, SPAN), lambda i: (i, 0, 0)),
            pl.BlockSpec((width, 3 * HEAD_SIZE), lambda i: (0, 0)),
        ],
        out_shape=[
            jax.ShapeDtypeStruct((SPANS, 3 * HEAD_SIZE, SPAN), bf16),
            jax.ShapeDtypeStruct((width, 3 * HEAD_SIZE), bf16),
        ],
        scratch_shapes=[
            pltpu.VMEM((1, tokens), f32),
            pltpu.VMEM((tokens, HEAD_SIZE), bf16),
            pltpu.VMEM((SPANS, HEAD_SIZE, SPAN), f32),
            pltpu.VMEM((3 * HEAD_SIZE, width), f32),
        ],
        compiler_params=pltpu.CompilerParams(vmem_limit_bytes=56 * 2**20),
        cost_estimate=brief,
        name="attention_backward",
    )(q_t, q, k_t, k, v, dout, out, lse, id_row, id_col, cosine, sine, normed)


def head_finish_kernel(sum_ref, q_ref, k_ref, v_ref, q_out, k_out, v_out, product_ref):
    product = jnp.zeros(product_ref.shape, f32)
    for number, (ref, out) in enumerate(((q_ref, q_out), (k_ref, k_out), (v_ref, v_out))):
        heads = out.shape[1] // HEAD_SIZE
        copies = SPANS // heads
        grads = []
        for head in range(heads):
            grad = sum_ref[head * copies].astype(f32)
            for other in range(1, copies):
                grad = grad + sum_ref[head * copies + other].astype(f32)
            grads.append(grad[:, number * HEAD_SIZE:(number + 1) * HEAD_SIZE])
        grad = jnp.concatenate(grads, axis=1)
        out[...] = grad
        product = product + jnp.sum(grad * ref[...].astype(f32), axis=1, keepdims=True)
    product_ref[...] = product


def head_finish(sums, q_weight, k_weight, v_weight):
    vmem = pl.BlockSpec(memory_space=pltpu.VMEM)
    return pl.pallas_call(
        head_finish_kernel,
        in_specs=[vmem] * 4,
        out_specs=[vmem] * 4,
        out_shape=[jax.ShapeDtypeStruct(w.shape, f32) for w in (q_weight, k_weight, v_weight)]
        + [jax.ShapeDtypeStruct((q_weight.shape[0], 1), f32)],
        compiler_params=pltpu.CompilerParams(vmem_limit_bytes=32 * 2**20),
        cost_estimate=brief,
        name="head_finish",
    )(sums, q_weight, k_weight, v_weight)


def unit_finish_kernel(place_ref, *refs):
    piece_refs, (gate_w_ref, up_w_ref, gate_out, up_out, down_out, product_ref) = refs[:PLANE], refs[PLANE:]
    units = gate_out.shape[1] // PLANE
    for link, piece_ref in enumerate(piece_refs):
        here = pl.ds(pl.multiple_of((place_ref[0] ^ link) * units, units), units)
        for number, out in enumerate((gate_out, up_out, down_out)):
            out[:, here] = piece_ref[:, number * units:(number + 1) * units].astype(f32)
    product_ref[...] = jnp.sum(
        gate_out[...] * gate_w_ref[...].astype(f32) + up_out[...] * up_w_ref[...].astype(f32), axis=1, keepdims=True
    )


def unit_finish(place, pieces, gate_weight, up_weight):
    vmem = pl.BlockSpec(memory_space=pltpu.VMEM)
    return pl.pallas_call(
        unit_finish_kernel,
        in_specs=[pl.BlockSpec(memory_space=pltpu.SMEM)] + [vmem] * (PLANE + 2),
        out_specs=[vmem] * 4,
        out_shape=[jax.ShapeDtypeStruct(gate_weight.shape, f32)] * 3
        + [jax.ShapeDtypeStruct((gate_weight.shape[0], 1), f32)],
        compiler_params=pltpu.CompilerParams(vmem_limit_bytes=32 * 2**20),
        name="unit_finish",
    )(place, *pieces, gate_weight, up_weight)


def unit_grad_kernel(*refs):
    tables, out_ref = (refs[:3 * PLANE], refs[3 * PLANE:6 * PLANE]), refs[6 * PLANE]
    column = 0
    for table in tables:
        total = None
        for k, right in enumerate(table[2 * PLANE:]):
            left = jnp.concatenate([table[2 * k][...], table[2 * k + 1][...]], axis=0)
            term = dot(left, right[...], 0, 0)
            total = term if total is None else total + term
        out_ref[:, column:column + total.shape[1]] = total.astype(bf16)
        column += total.shape[1]


def unit_grads(normed, dgate_up, dout, act):
    tokens, width = normed[0].shape
    rows = width // 4
    whole = lambda array: pl.BlockSpec(array.shape, lambda i: (0, 0))
    left = [pl.BlockSpec((tokens, rows), lambda i: (0, i))] * (2 * PLANE)
    columns = dgate_up[0].shape[1] + act[0].shape[1]
    return pl.pallas_call(
        unit_grad_kernel,
        grid=(width // rows,),
        in_specs=left + [whole(part) for part in dgate_up] + left + [whole(part) for part in act],
        out_specs=pl.BlockSpec((rows, columns), lambda i: (i, 0)),
        out_shape=jax.ShapeDtypeStruct((width, columns), bf16),
        compiler_params=pltpu.CompilerParams(vmem_limit_bytes=48 * 2**20),
        cost_estimate=brief,
        name="unit_grads",
    )(*normed, *dgate_up, *dout, *act)


def feed_kernel(pairs, *refs):
    ins, weight_ref, refs = refs[:4 * pairs], refs[4 * pairs], refs[4 * pairs + 1:]
    units = weight_ref.shape[1] // 3
    weight = weight_ref[:, :2 * units]
    down_weight = weight_ref[:, 2 * units:]
    for pair in range(pairs):
        own_ref, other_ref, d_own_ref, d_other_ref = ins[4 * pair:4 * pair + 4]
        kept_ref, sent_ref, out_kept_ref, out_sent_ref, dgate_up_ref, act_ref = refs[6 * pair:6 * pair + 6]
        rows = own_ref.shape[0]
        gate_up = dot(jnp.concatenate([own_ref[...], other_ref[...]], axis=0), weight)
        dact = dot(jnp.concatenate([d_own_ref[...], d_other_ref[...]], axis=0), down_weight)
        gate, up = gate_up[:, :units], gate_up[:, units:]
        sigma = 1.0 / (1.0 + jnp.exp(-gate))
        silu = gate * sigma
        dgate_up_ref[:, :units] = (dact * up * sigma * (1.0 + gate * (1.0 - sigma))).astype(bf16)
        dgate_up_ref[:, units:] = (dact * silu).astype(bf16)
        act_ref[...] = (silu * up).astype(bf16)
        dnormed = dot(dgate_up_ref[...], weight, 1, 1)
        kept_ref[...] = dnormed[:rows]
        sent_ref[...] = dnormed[rows:].astype(bf16)
        out = dot(act_ref[...], down_weight, 1, 1)
        out_kept_ref[...] = out[:rows]
        out_sent_ref[...] = out[rows:].astype(bf16)


def feed(rows_list, weight):
    pairs = len(rows_list)
    rows, width = rows_list[0][0].shape
    units = weight.shape[1] // 3
    vmem = pl.BlockSpec(memory_space=pltpu.VMEM)
    halves = [jax.ShapeDtypeStruct((rows, width), f32), jax.ShapeDtypeStruct((rows, width), bf16)]
    shapes = (
        halves * 2 + [jax.ShapeDtypeStruct((2 * rows, 2 * units), bf16), jax.ShapeDtypeStruct((2 * rows, units), bf16)]
    ) * pairs
    ins = [part for group in rows_list for part in group]
    outs = pl.pallas_call(
        functools.partial(feed_kernel, pairs),
        in_specs=[vmem] * (len(ins) + 1),
        out_specs=[vmem] * len(shapes),
        out_shape=shapes,
        compiler_params=pltpu.CompilerParams(vmem_limit_bytes=48 * 2**20),
        cost_estimate=brief,
        name="feed",
    )(*ins, weight)
    return [outs[6 * pair:6 * pair + 6] for pair in range(pairs)]


def merged_heads(back_ref):
    heads = back_ref.shape[0]
    per_kv = heads // KV_HEADS
    rows = [back_ref[head, :HEAD_SIZE, :] for head in range(heads)]
    for number in (1, 2):
        here = slice(number * HEAD_SIZE, (number + 1) * HEAD_SIZE)
        for head in range(KV_HEADS):
            total = back_ref[head * per_kv, here, :].astype(f32)
            for copy in range(1, per_kv):
                total = total + back_ref[head * per_kv + copy, here, :].astype(f32)
            rows.append(total.astype(bf16))
    return rows


def back_kernel(core_ref, back_ref, weight_ref, mine_ref, other_ref, table_ref):
    for at, value in enumerate(merged_heads(back_ref)):
        table_ref[at * HEAD_SIZE:(at + 1) * HEAD_SIZE, :] = value
    rows = mine_ref.shape[0]
    both = dot(weight_ref[...], table_ref[...])
    low, high = both[:, :rows].T, both[:, rows:].T
    first = core_ref[0] == 0
    mine_ref[...] = jnp.where(first, low, high)
    other_ref[...] = jnp.where(first, high, low)


def input_terms(back, weight, core):
    vmem = pl.BlockSpec(memory_space=pltpu.VMEM)
    width, features = weight.shape
    rows = SPAN // 2
    return pl.pallas_call(
        back_kernel,
        in_specs=[pl.BlockSpec(memory_space=pltpu.SMEM), vmem, vmem],
        out_specs=[vmem] * 2,
        out_shape=[jax.ShapeDtypeStruct((rows, width), f32)] * 2,
        scratch_shapes=[pltpu.VMEM((features, SPAN), bf16)],
        compiler_params=pltpu.CompilerParams(vmem_limit_bytes=40 * 2**20),
        cost_estimate=brief,
        name="input_terms",
    )(core, back, weight)


tie = lax.optimization_barrier


def with_swapped(pieces):
    return [part for piece in pieces for part in (piece, swap(piece))]


def rms_factor(stream):
    return lax.rsqrt(jnp.mean(stream * stream, axis=-1, keepdims=True) + norm_eps)


def norm_backward(stream, factor, gain, dnormed):
    scaled = dnormed * gain
    return factor * scaled - stream * factor**3 * jnp.mean(scaled * stream, axis=-1, keepdims=True)


def body(
    hidden,
    document_index,
    attn_gain,
    q_weight,
    key_matrix,
    value_matrix,
    out_weight,
    mlp_gain,
    gate_weight,
    up_weight,
    down_weight,
    cotangent,
):
    count = lax.axis_size("fsdp")
    planes = count // PLANE
    f = lax.axis_index("fsdp")
    t = lax.axis_index("tp")
    place = f % SPANS
    plane_at = f // PLANE
    own, width = hidden.shape
    shard = q_weight.shape[1]
    q_heads = q_weight.shape[2] // HEAD_SIZE
    kv_heads = key_matrix.shape[2] // HEAD_SIZE
    per_kv = q_heads // kv_heads
    units = gate_weight.shape[2] // PLANE

    gains_own = jnp.stack([attn_gain[0], mlp_gain[0]], axis=-1)
    sent = head_cut(count, q_weight[0], key_matrix[0], value_matrix[0], gains_own)

    plane_place = f % PLANE
    cubes = count // SPANS
    cube_at = f // SPANS
    half = own // 2
    unit_set = jnp.concatenate(
        [w[0].reshape(shard, PLANE, units).transpose(1, 0, 2) for w in (gate_weight, up_weight, down_weight)],
        axis=-1,
    )
    lines = [list(range(first, count, PLANE)) for first in range(PLANE)]
    lines = [list(range(first, count, PLANE)) for first in range(PLANE)]
    p1, p2, p4 = hop(hidden, 1), hop(hidden, 2), hop(hidden, 4)
    head_set = exchange(sent, count).reshape(width, -1)
    out_far = [hop(out_weight[0], PLANE * k) for k in range(1, planes)]
    p4, document_index, cotangent = tie((p4, document_index, cotangent))
    p5, p6 = hop(p4, 1), hop(p4, 2)
    p3 = [hop(p2[:half], 1), hop(p1[half:], 2)]
    p7 = [hop(p6[:half], 1), hop(p5[half:], 2)]
    p3, p7 = jnp.concatenate(p3, axis=0), jnp.concatenate(p7, axis=0)
    unit_set, head_set = tie((unit_set, head_set))
    unit_own = exchange(unit_set, PLANE).reshape(PLANE * shard, 3 * units)

    seq_ids = lax.dynamic_slice_in_dim(document_index, f // SPANS * PACKED_LENGTH, PACKED_LENGTH)
    seq_index = jnp.arange(PACKED_LENGTH, dtype=jnp.int32)
    before = jnp.concatenate([jnp.full((1,), -1, jnp.int32), seq_ids[:-1]])
    starts = lax.cummax(jnp.where(seq_ids != before, seq_index, 0), axis=0)
    positions = (seq_index - starts).astype(f32)
    freq = rope_base ** (-2.0 * jnp.arange(HALF, dtype=f32) / HEAD_SIZE)
    angle = freq[:, None] * positions[None, :]
    cosine, sine = jnp.cos(angle), jnp.sin(angle)
    id_row = seq_ids[None, :]
    id_col = jnp.broadcast_to(seq_ids[:, None], (PACKED_LENGTH, 128))

    own_ids = lax.dynamic_slice_in_dim(document_index, f * SPAN + t * own, own)
    dstream = cotangent.astype(f32) * (own_ids != 0).astype(f32)[:, None]
    dmlp_own = dstream.astype(bf16)
    head_set, dmlp_own, cosine, sine, id_col, p3, out_far = tie(
        (head_set, dmlp_own, cosine, sine, id_col, p3, out_far)
    )
    pieces = with_swapped([hidden, p1, p2, p3, p4, p5, p6, p7])
    out_0 = jnp.zeros((planes,) + out_weight.shape[1:], bf16)
    for k, piece in enumerate([out_weight[0]] + out_far):
        out_0 = lax.dynamic_update_slice_in_dim(out_0, piece[None], plane_at ^ k, 0)
    out_1, out_2 = hop(out_0, 1), hop(out_0, 2)
    in_shard = jnp.concatenate([q_weight[0], key_matrix[0], value_matrix[0]], axis=1)

    places = jnp.stack([place, t]).astype(jnp.int32)

    normed, gains, q_t, k_t, v_t, q, key, v = project(pieces, head_set, places, cosine, sine)
    gain_a, gain_m = gains[0:1], gains[1:2]
    q_t, out_0, out_1, out_2, dmlp_own, unit_own = tie((q_t, out_0, out_1, out_2, dmlp_own, unit_own))
    unit_weight = lax.all_gather(unit_own, "fsdp", axis=0, tiled=True, axis_index_groups=lines)
    out_3 = hop(out_0, 3)
    dmlp_1, dmlp_2 = hop(dmlp_own, 1), hop(dmlp_own, 2)
    out_t, out_full, lse = attention_forward(q_t, key, v_t, id_row, id_col)
    out_t, dmlp_1, dmlp_2, out_3, dmlp_late = tie((out_t, dmlp_1, dmlp_2, out_3, dmlp_own))
    dmlp_3 = hop(dmlp_late, 3)
    attended = exchange(out_t, SPANS)
    attended, dmlp_3, in_shard = tie((attended, dmlp_3, in_shard))
    in_part = lax.all_gather(in_shard, "fsdp", axis=0, tiled=True)
    attended = attended.reshape(q_heads * HEAD_SIZE, SPAN)
    out_part = jnp.zeros((planes, PLANE, shard, out_0.shape[2]), bf16)
    for k, piece in enumerate((out_0, out_1, out_2, out_3)):
        out_part = lax.dynamic_update_slice_in_dim(out_part, piece[:, None], plane_place ^ k, 1)
    out_part = out_part.reshape(width, -1)

    stream = hidden.astype(f32)
    mine = lax.dynamic_slice_in_dim(attended, t * own, own, 1)
    other = lax.dynamic_slice_in_dim(attended, (1 - t) * own, own, 1)
    mid = stream + dot(mine, out_part, 0, 1) + swap(dot(other, out_part, 0, 1))

    factor_m = rms_factor(mid)
    normed_own = (mid * factor_m * gain_m).astype(bf16)
    dmlp = with_swapped([dmlp_own, dmlp_1, dmlp_2, dmlp_3])
    n1, n2 = hop(normed_own, 1), hop(normed_own, 2)
    n1, n2, normed_late = tie((n1, n2, normed_own))
    n3 = hop(normed_late, 3)
    normed_m = with_swapped([normed_own, n1, n2])
    second, third = feed([normed_m[2 * k:2 * k + 2] + dmlp[2 * k:2 * k + 2] for k in (1, 2)], unit_weight)
    second, third, n3 = tie((second, third, n3))
    normed_m += with_swapped([n3])
    dn_got = [swap(second[1]), swap(third[1])]
    first, fourth = feed([normed_m[2 * k:2 * k + 2] + dmlp[2 * k:2 * k + 2] for k in (0, 3)], unit_weight)
    first, fourth, dn_got = tie((first, fourth, dn_got))
    results = [first, second, third, fourth]
    dn_got = [swap(first[1])] + dn_got + [swap(fourth[1])]
    dn_pair = [result[0] + got.astype(f32) for result, got in zip(results, dn_got)]
    dn_low = [dn_pair[k].astype(bf16) for k in range(1, PLANE)]
    dn_low[2], acts = tie((dn_low[2], [result[5] for result in results]))
    dn_far = [dn_pair[0]] + [hop(low, k) for k, low in enumerate(dn_low, 1)]
    out_pair = [result[2] + swap(result[3]).astype(f32) for result in results]
    out_low = [out_pair[k].astype(bf16) for k in range(1, PLANE)]
    unit_term = unit_grads(normed_m, [result[4] for result in results], dmlp, acts)
    dn_far, out_low, in_part, unit_term = tie((dn_far, out_low, in_part, unit_term))
    unit_sum = lax.psum_scatter(unit_term, "fsdp", scatter_dimension=0, tiled=True, axis_index_groups=lines)
    out_far = [hop(low, k) for k, low in enumerate(out_low[:2], 1)]

    dnormed_m = dn_far[0]
    for far in dn_far[1:]:
        dnormed_m = dnormed_m + far.astype(f32)
    dmid = dstream + norm_backward(mid, factor_m, gain_m, dnormed_m)

    dattn = dmid.astype(bf16)
    dattn_other = swap(dattn)
    dattn = jnp.where(
        t == 0,
        jnp.concatenate([dattn, dattn_other], axis=0),
        jnp.concatenate([dattn_other, dattn], axis=0),
    )
    dout = dot(out_part, dattn, 0, 1).astype(bf16)
    dout = exchange(dout.reshape(SPANS, HEAD_SIZE, SPAN), SPANS)
    out_term = dot(dattn, attended, 0, 1).astype(bf16).reshape(planes, PLANE, shard, -1).transpose(1, 0, 2, 3)
    dout, out_term, out_low, out_far = tie((dout, out_term, out_low, out_far))
    out_term = exchange(out_term.reshape(PLANE, planes * shard, -1), PLANE)
    out_far += [hop(out_low[2], 3)]
    grads, head_low = attention_backward(
        q_t, q, k_t, key, v, dout, out_full, lse, id_row, id_col, cosine, sine, normed
    )
    grads, head_low, out_term, out_far, unit_sum = tie((grads, head_low, out_term, out_far, unit_sum))
    head_low = head_low.reshape(cubes, SPANS * shard, 3 * HEAD_SIZE)
    head_sum = lax.dynamic_index_in_dim(head_low, cube_at, 0, keepdims=False).astype(f32)
    for k in range(1, cubes):
        far = lax.dynamic_index_in_dim(head_low, cube_at ^ k, 0, keepdims=False)
        head_sum = head_sum + hop(far, SPANS * k).astype(f32)
    head_sum = head_sum.astype(bf16).reshape(SPANS, shard, 3 * HEAD_SIZE)

    back = exchange(grads, SPANS)
    unit_sum = unit_sum.reshape(PLANE, shard, 3 * units)
    unit_back = [lax.dynamic_index_in_dim(unit_sum, plane_place ^ k, 0, keepdims=False) for k in range(PLANE)]
    unit_back = [piece if k == 0 else hop(piece, k) for k, piece in enumerate(unit_back)]
    out_term = out_term.astype(f32).sum(axis=0).reshape(planes, shard, -1)
    out_grad = lax.dynamic_index_in_dim(out_term, plane_at, 0, keepdims=False)
    out_sums = []
    for k in range(1, planes):
        far = lax.dynamic_index_in_dim(out_term, plane_at ^ k, 0, keepdims=False)
        out_sums.append(hop(far.astype(bf16), PLANE * k))
    out_total = out_pair[0]
    for far in out_far:
        out_total = out_total + far.astype(f32)
    output = (mid + out_total).astype(bf16)
    back, out_sums, unit_back, output, head_sum = tie((back, out_sums, unit_back, output, head_sum))
    head_sums = exchange(head_sum, SPANS)
    for far in out_sums:
        out_grad = out_grad + far.astype(f32)
    mine, other = input_terms(back, in_part, t.reshape(1).astype(jnp.int32))
    dnormed_a = mine + swap(other)
    input_grad = dmid + norm_backward(stream, rms_factor(stream), gain_a, dnormed_a)
    input_grad, head_sums = tie((input_grad, head_sums))

    q_grad, k_grad, v_grad, gain_a_part = head_finish(head_sums, q_weight[0], key_matrix[0], value_matrix[0])

    gate_grad, up_grad, down_grad, gain_m_part = unit_finish(
        plane_place.reshape(1).astype(jnp.int32), unit_back, gate_weight[0], up_weight[0]
    )

    gain_parts = jnp.concatenate([gain_a_part, gain_m_part], axis=1).T
    gain_grads = (gain_parts + swap(gain_parts)) / jnp.stack([attn_gain[0], mlp_gain[0]]).astype(f32)
    return (
        output,
        input_grad,
        gain_grads[0:1],
        q_grad[None],
        k_grad[None],
        v_grad[None],
        out_grad[None],
        gain_grads[1:2],
        gate_grad[None],
        up_grad[None],
        down_grad[None],
    )


def solution(mesh):
    rows = P(("fsdp", "tp"), None)
    gain = P(None, "fsdp")
    weight = P(None, "fsdp", "tp")
    return jax.shard_map(
        body,
        mesh=mesh,
        in_specs=(rows, P(), gain, weight, weight, weight, weight, gain, weight, weight, weight, rows),
        out_specs=(rows, rows, gain, weight, weight, weight, weight, gain, weight, weight, weight),
        check_vma=False,
    )
```

```python
import functools
import math

import jax
import jax.numpy as jnp
from jax import lax
from jax.experimental import pallas as pl
from jax.experimental.pallas import tpu as pltpu
from jax.sharding import PartitionSpec as P

HEAD_SIZE = 96
HALF = HEAD_SIZE // 2
SPANS = 8
KV_HEADS = SPANS // 2
PLANE = 4
PACKED_LENGTH = 4096
SPAN = PACKED_LENGTH // SPANS

rope_base = 100000.0
norm_eps = 1e-05
masked_score = -1000000000.0
scale = HEAD_SIZE ** (-0.5)
scale_log2 = scale * math.log2(math.e)
bf16 = jnp.bfloat16
brief = pl.CostEstimate(flops=1024, bytes_accessed=1024, transcendentals=0)
f32 = jnp.float32


def dot(left, right, left_dim=1, right_dim=0):
    return lax.dot_general(
        left, right, (((left_dim,), (right_dim,)), ((), ())), preferred_element_type=f32
    )


def hop(value, distance):
    count = lax.axis_size("fsdp")
    return lax.ppermute(value, "fsdp", [(i, i ^ distance) for i in range(count)])


def swap(value):
    return lax.ppermute(value, "tp", [(0, 1), (1, 0)])


def groups_of(size):
    count = lax.axis_size("fsdp")
    return [list(range(first, first + size)) for first in range(0, count, size)]


def exchange(value, size):
    groups = None if size == lax.axis_size("fsdp") else groups_of(size)
    return lax.all_to_all(value, "fsdp", 0, 0, axis_index_groups=groups)


def head_cut_kernel(q_ref, k_ref, v_ref, gain_ref, out_ref):
    gains = gain_ref[...].astype(f32)
    for place in range(SPANS):
        parts = []
        for ref in (q_ref, k_ref, v_ref):
            head = place * ref.shape[1] // (SPANS * HEAD_SIZE)
            parts.append(ref[:, head * HEAD_SIZE:(head + 1) * HEAD_SIZE].astype(f32))
        cut = jnp.concatenate(parts + [gains], axis=1).astype(bf16)
        for first in range(0, out_ref.shape[0], SPANS):
            out_ref[first + place] = cut


def head_cut(count, q_weight, k_weight, v_weight, gains):
    vmem = pl.BlockSpec(memory_space=pltpu.VMEM)
    shard = q_weight.shape[0]
    return pl.pallas_call(
        head_cut_kernel,
        in_specs=[vmem] * 4,
        out_specs=vmem,
        out_shape=jax.ShapeDtypeStruct((count, shard, 3 * HEAD_SIZE + 2), bf16),
        compiler_params=pltpu.CompilerParams(vmem_limit_bytes=32 * 2**20),
        cost_estimate=brief,
        name="head_cut",
    )(q_weight, k_weight, v_weight, gains)


def project_kernel(*refs):
    pieces, (place_ref, head_ref, cos_ref, sin_ref) = refs[:2 * SPANS], refs[2 * SPANS:2 * SPANS + 4]
    normed_ref, gain_ref, q_t_ref, k_t_ref, v_t_ref, q_ref, k_ref, v_ref = refs[2 * SPANS + 4:2 * SPANS + 12]
    in_buf, out_buf, in_sem, out_sem = refs[2 * SPANS + 12:]
    rows = pieces[0].shape[0]
    place, core = place_ref[0], place_ref[1]

    def fetch(pair, part):
        return pltpu.make_async_copy(
            pieces[2 * pair + part],
            in_buf.at[pair % 3, pl.ds(pl.multiple_of((core ^ part) * rows, rows), rows)],
            in_sem.at[pair % 3, part],
        )

    def store(pair):
        return pltpu.make_async_copy(out_buf.at[pair % 2], normed_ref.at[place ^ pair], out_sem.at[pair % 2])

    for pair in range(2):
        for part in range(2):
            fetch(pair, part).start()
    row = lax.broadcasted_iota(jnp.int32, (8, head_ref.shape[1]), 0)
    column = lax.broadcasted_iota(jnp.int32, (8, head_ref.shape[1]), 1)
    pick = (column == row + 3 * HEAD_SIZE).astype(f32).astype(bf16)
    gains = dot(pick, head_ref[...], 1, 1)
    gain = gains[0:1]
    gain_ref[...] = gains
    for pair in range(SPANS):
        for part in range(2):
            fetch(pair, part).wait()
        if pair + 2 < SPANS:
            for part in range(2):
                fetch(pair + 2, part).start()
        if pair >= 2:
            store(pair - 2).wait()
        x = in_buf[pair % 3].astype(f32)
        factor = lax.rsqrt(jnp.mean(x * x, axis=-1, keepdims=True) + norm_eps)
        normed = (x * factor * gain).astype(bf16)
        out_buf[pair % 2] = normed
        store(pair).start()
        product = dot(normed, head_ref[:, :3 * HEAD_SIZE]).T
        here = pl.ds(pl.multiple_of((place ^ pair) * 2 * rows, 2 * rows), 2 * rows)
        cosine, sine = cos_ref[:, here], sin_ref[:, here]
        for number, (t_ref, n_ref) in enumerate(((q_t_ref, q_ref), (k_t_ref, k_ref))):
            first = product[number * HEAD_SIZE:number * HEAD_SIZE + HALF]
            second = product[number * HEAD_SIZE + HALF:(number + 1) * HEAD_SIZE]
            turned = jnp.concatenate(
                [first * cosine - second * sine, second * cosine + first * sine], axis=0
            )
            t_ref[:, here] = turned.astype(bf16)
            n_ref[here, :] = turned.T.astype(bf16)
        value = product[2 * HEAD_SIZE:3 * HEAD_SIZE]
        v_t_ref[:, here] = value.astype(bf16)
        v_ref[here, :] = value.T.astype(bf16)
    for pair in range(SPANS - 2, SPANS):
        store(pair).wait()


def project(pieces, head_set, places, cosine, sine):
    rows, width = pieces[0].shape
    tokens = 2 * SPANS * rows
    vmem = pl.BlockSpec(memory_space=pltpu.VMEM)
    anywhere = pl.BlockSpec(memory_space=pl.ANY)
    return pl.pallas_call(
        project_kernel,
        in_specs=[anywhere] * len(pieces) + [pl.BlockSpec(memory_space=pltpu.SMEM), vmem, vmem, vmem],
        out_specs=[anywhere] + [vmem] * 7,
        out_shape=[
            jax.ShapeDtypeStruct((SPANS, 2 * rows, width), bf16),
            jax.ShapeDtypeStruct((8, width), f32),
        ]
        + [jax.ShapeDtypeStruct((HEAD_SIZE, tokens), bf16)] * 3
        + [jax.ShapeDtypeStruct((tokens, HEAD_SIZE), bf16)] * 3,
        scratch_shapes=[
            pltpu.VMEM((3, 2 * rows, width), bf16),
            pltpu.VMEM((2, 2 * rows, width), bf16),
            pltpu.SemaphoreType.DMA((3, 2)),
            pltpu.SemaphoreType.DMA((2,)),
        ],
        compiler_params=pltpu.CompilerParams(vmem_limit_bytes=56 * 2**20),
        cost_estimate=brief,
        name="project",
    )(*pieces, places, head_set, cosine, sine)


def widened(column):
    return jnp.concatenate([column] * (SPAN // column.shape[1]), axis=1)


def causal_tile():
    key_at = lax.broadcasted_iota(jnp.int32, (SPAN, SPAN), 0)
    query_at = lax.broadcasted_iota(jnp.int32, (SPAN, SPAN), 1)
    return key_at <= query_at


def forward_kernel(q_t_ref, k_ref, v_t_ref, id_row_ref, id_col_ref, out_ref, out_full_ref, lse_ref):
    block = pl.program_id(0)
    query = q_t_ref[...]
    id_row = id_row_ref[...]

    def step(at, carry, diagonal):
        best, total, result = carry
        keys = pl.ds(pl.multiple_of(at * SPAN, SPAN), SPAN)
        scores = dot(k_ref[keys, :], query) * scale_log2
        allowed = widened(id_col_ref[keys, :]) == id_row
        if diagonal:
            allowed = allowed & causal_tile()
        scores = jnp.where(allowed, scores, masked_score)
        larger = jnp.maximum(best, jnp.max(scores, axis=0, keepdims=True))
        weights = jnp.exp2(scores - larger)
        faded = jnp.exp2(best - larger)
        total = total * faded + jnp.sum(weights, axis=0, keepdims=True)
        result = result * faded + dot(v_t_ref[:, keys], weights.astype(bf16))
        return larger, total, result

    carry = (
        jnp.full((1, SPAN), masked_score, f32),
        jnp.zeros((1, SPAN), f32),
        jnp.zeros((HEAD_SIZE, SPAN), f32),
    )
    carry = lax.fori_loop(0, block, lambda at, c: step(at, c, False), carry)
    best, total, result = step(block, carry, True)
    result = result / total
    out_full_ref[...] = result
    out_ref[0] = result.astype(bf16)
    lse_ref[...] = best + jnp.log2(total)


def attention_forward(q_t, k, v_t, id_row, id_col):
    tokens = k.shape[0]
    whole = lambda array: pl.BlockSpec(array.shape, lambda i: (0, 0))
    return pl.pallas_call(
        forward_kernel,
        grid=(SPANS,),
        in_specs=[
            pl.BlockSpec((HEAD_SIZE, SPAN), lambda i: (0, i)),
            whole(k),
            whole(v_t),
            pl.BlockSpec((1, SPAN), lambda i: (0, i)),
            whole(id_col),
        ],
        out_specs=[
            pl.BlockSpec((1, HEAD_SIZE, SPAN), lambda i: (i, 0, 0)),
            pl.BlockSpec((HEAD_SIZE, SPAN), lambda i: (0, i)),
            pl.BlockSpec((1, SPAN), lambda i: (0, i)),
        ],
        out_shape=[
            jax.ShapeDtypeStruct((SPANS, HEAD_SIZE, SPAN), bf16),
            jax.ShapeDtypeStruct((HEAD_SIZE, tokens), f32),
            jax.ShapeDtypeStruct((1, tokens), f32),
        ],
        compiler_params=pltpu.CompilerParams(vmem_limit_bytes=40 * 2**20),
        cost_estimate=brief,
        name="attention_forward",
    )(q_t, k, v_t, id_row, id_col)


def backward_kernel(q_t_ref, q_ref, k_t_ref, k_ref, v_ref, dout_ref, out_ref, lse_ref, id_row_ref, id_col_ref,
                    cos_ref, sin_ref, normed_ref, grad_ref, weight_grad_ref, delta_ref, dout_n_ref, dq_ref, sum_ref):
    block = pl.program_id(0)

    @pl.when(block == 0)
    def _():
        for at in range(SPANS):
            dout = dout_ref[at]
            here = slice(at * SPAN, (at + 1) * SPAN)
            delta_ref[:, here] = jnp.sum(dout.astype(f32) * out_ref[:, here], axis=0, keepdims=True)
            dout_n_ref[here, :] = dout.astype(f32).T.astype(bf16)
        dq_ref[...] = jnp.zeros(dq_ref.shape, f32)
        sum_ref[...] = jnp.zeros(sum_ref.shape, f32)

    key_t, key, value = k_t_ref[...], k_ref[...], v_ref[...]
    id_col = widened(id_col_ref[...])

    def step(at, carry, diagonal):
        dkey, dvalue = carry
        rows = pl.ds(pl.multiple_of(at * SPAN, SPAN), SPAN)
        scores = dot(key, q_t_ref[:, rows]) * scale_log2 - lse_ref[:, rows]
        allowed = id_col == id_row_ref[:, rows]
        if diagonal:
            allowed = allowed & causal_tile()
        probs = jnp.exp2(jnp.where(allowed, scores, masked_score))
        dprobs = dot(value, dout_ref[at])
        dscores = (probs * (dprobs - delta_ref[:, rows])).astype(bf16)
        dvalue = dvalue + dot(probs.astype(bf16), dout_n_ref[rows, :])
        dkey = dkey + dot(dscores, q_ref[rows, :])
        dq_ref[at] += dot(key_t, dscores)
        return dkey, dvalue

    zero = jnp.zeros((SPAN, HEAD_SIZE), f32)
    carry = step(block, (zero, zero), True)
    dkey, dvalue = lax.fori_loop(block + 1, SPANS, lambda at, c: step(at, c, False), carry)
    cosine, sine = cos_ref[...], sin_ref[...]
    for number, grad in enumerate((dq_ref[block], dkey.T)):
        first = grad[:HALF] * scale
        second = grad[HALF:] * scale
        turned = jnp.concatenate(
            [first * cosine + second * sine, second * cosine - first * sine], axis=0
        )
        grad_ref[0, number * HEAD_SIZE:(number + 1) * HEAD_SIZE, :] = turned.astype(bf16)
    grad_ref[0, 2 * HEAD_SIZE:, :] = dvalue.T.astype(bf16)
    sum_ref[...] += dot(grad_ref[0], normed_ref[0])

    @pl.when(block == SPANS - 1)
    def _():
        weight_grad_ref[...] = sum_ref[...].T.astype(bf16)


def attention_backward(q_t, q, k_t, k, v, dout, out, lse, id_row, id_col, cosine, sine, normed):
    tokens = k.shape[0]
    width = normed.shape[2]
    whole = lambda array: pl.BlockSpec(array.shape, lambda i: (0,) * array.ndim)
    wide = pl.BlockSpec((HEAD_SIZE, SPAN), lambda i: (0, i))
    tall = pl.BlockSpec((SPAN, HEAD_SIZE), lambda i: (i, 0))
    table = pl.BlockSpec((HALF, SPAN), lambda i: (0, i))
    return pl.pallas_call(
        backward_kernel,
        grid=(SPANS,),
        in_specs=[
            whole(q_t), whole(q), wide, tall, tall, whole(dout), whole(out), whole(lse), whole(id_row),
            pl.BlockSpec((SPAN, id_col.shape[1]), lambda i: (i, 0)), table, table,
            pl.BlockSpec((1, SPAN, width), lambda i: (i, 0, 0)),
        ],
        out_specs=[
            pl.BlockSpec((1, 3 * HEAD_SIZE, SPAN), lambda i: (i, 0, 0)),
            pl.BlockSpec((width, 3 * HEAD_SIZE), lambda i: (0, 0)),
        ],
        out_shape=[
            jax.ShapeDtypeStruct((SPANS, 3 * HEAD_SIZE, SPAN), bf16),
            jax.ShapeDtypeStruct((width, 3 * HEAD_SIZE), bf16),
        ],
        scratch_shapes=[
            pltpu.VMEM((1, tokens), f32),
            pltpu.VMEM((tokens, HEAD_SIZE), bf16),
            pltpu.VMEM((SPANS, HEAD_SIZE, SPAN), f32),
            pltpu.VMEM((3 * HEAD_SIZE, width), f32),
        ],
        compiler_params=pltpu.CompilerParams(vmem_limit_bytes=56 * 2**20),
        cost_estimate=brief,
        name="attention_backward",
    )(q_t, q, k_t, k, v, dout, out, lse, id_row, id_col, cosine, sine, normed)


def head_finish_kernel(sum_ref, q_ref, k_ref, v_ref, q_out, k_out, v_out, product_ref):
    product = jnp.zeros(product_ref.shape, f32)
    for number, (ref, out) in enumerate(((q_ref, q_out), (k_ref, k_out), (v_ref, v_out))):
        heads = out.shape[1] // HEAD_SIZE
        copies = SPANS // heads
        grads = []
        for head in range(heads):
            grad = sum_ref[head * copies].astype(f32)
            for other in range(1, copies):
                grad = grad + sum_ref[head * copies + other].astype(f32)
            grads.append(grad[:, number * HEAD_SIZE:(number + 1) * HEAD_SIZE])
        grad = jnp.concatenate(grads, axis=1)
        out[...] = grad
        product = product + jnp.sum(grad * ref[...].astype(f32), axis=1, keepdims=True)
    product_ref[...] = product


def head_finish(sums, q_weight, k_weight, v_weight):
    vmem = pl.BlockSpec(memory_space=pltpu.VMEM)
    return pl.pallas_call(
        head_finish_kernel,
        in_specs=[vmem] * 4,
        out_specs=[vmem] * 4,
        out_shape=[jax.ShapeDtypeStruct(w.shape, f32) for w in (q_weight, k_weight, v_weight)]
        + [jax.ShapeDtypeStruct((q_weight.shape[0], 1), f32)],
        compiler_params=pltpu.CompilerParams(vmem_limit_bytes=32 * 2**20),
        cost_estimate=brief,
        name="head_finish",
    )(sums, q_weight, k_weight, v_weight)


def unit_finish_kernel(place_ref, *refs):
    piece_refs, (gate_w_ref, up_w_ref, gate_out, up_out, down_out, product_ref) = refs[:PLANE], refs[PLANE:]
    units = gate_out.shape[1] // PLANE
    for link, piece_ref in enumerate(piece_refs):
        here = pl.ds(pl.multiple_of((place_ref[0] ^ link) * units, units), units)
        for number, out in enumerate((gate_out, up_out, down_out)):
            out[:, here] = piece_ref[:, number * units:(number + 1) * units].astype(f32)
    product_ref[...] = jnp.sum(
        gate_out[...] * gate_w_ref[...].astype(f32) + up_out[...] * up_w_ref[...].astype(f32), axis=1, keepdims=True
    )


def unit_finish(place, pieces, gate_weight, up_weight):
    vmem = pl.BlockSpec(memory_space=pltpu.VMEM)
    return pl.pallas_call(
        unit_finish_kernel,
        in_specs=[pl.BlockSpec(memory_space=pltpu.SMEM)] + [vmem] * (PLANE + 2),
        out_specs=[vmem] * 4,
        out_shape=[jax.ShapeDtypeStruct(gate_weight.shape, f32)] * 3
        + [jax.ShapeDtypeStruct((gate_weight.shape[0], 1), f32)],
        compiler_params=pltpu.CompilerParams(vmem_limit_bytes=32 * 2**20),
        name="unit_finish",
    )(place, *pieces, gate_weight, up_weight)


def unit_grad_kernel(*refs):
    tables, out_ref = (refs[:3 * PLANE], refs[3 * PLANE:6 * PLANE]), refs[6 * PLANE]
    column = 0
    for table in tables:
        total = None
        for k, right in enumerate(table[2 * PLANE:]):
            left = jnp.concatenate([table[2 * k][...], table[2 * k + 1][...]], axis=0)
            term = dot(left, right[...], 0, 0)
            total = term if total is None else total + term
        out_ref[:, column:column + total.shape[1]] = total.astype(bf16)
        column += total.shape[1]


def unit_grads(normed, dgate_up, dout, act):
    tokens, width = normed[0].shape
    rows = width // 4
    whole = lambda array: pl.BlockSpec(array.shape, lambda i: (0, 0))
    left = [pl.BlockSpec((tokens, rows), lambda i: (0, i))] * (2 * PLANE)
    columns = dgate_up[0].shape[1] + act[0].shape[1]
    return pl.pallas_call(
        unit_grad_kernel,
        grid=(width // rows,),
        in_specs=left + [whole(part) for part in dgate_up] + left + [whole(part) for part in act],
        out_specs=pl.BlockSpec((rows, columns), lambda i: (i, 0)),
        out_shape=jax.ShapeDtypeStruct((width, columns), bf16),
        compiler_params=pltpu.CompilerParams(vmem_limit_bytes=48 * 2**20),
        cost_estimate=brief,
        name="unit_grads",
    )(*normed, *dgate_up, *dout, *act)


def feed_kernel(pairs, *refs):
    ins, weight_ref, refs = refs[:4 * pairs], refs[4 * pairs], refs[4 * pairs + 1:]
    units = weight_ref.shape[1] // 3
    weight = weight_ref[:, :2 * units]
    down_weight = weight_ref[:, 2 * units:]
    for pair in range(pairs):
        own_ref, other_ref, d_own_ref, d_other_ref = ins[4 * pair:4 * pair + 4]
        kept_ref, sent_ref, out_kept_ref, out_sent_ref, dgate_up_ref, act_ref = refs[6 * pair:6 * pair + 6]
        rows = own_ref.shape[0]
        gate_up = dot(jnp.concatenate([own_ref[...], other_ref[...]], axis=0), weight)
        dact = dot(jnp.concatenate([d_own_ref[...], d_other_ref[...]], axis=0), down_weight)
        gate, up = gate_up[:, :units], gate_up[:, units:]
        sigma = 1.0 / (1.0 + jnp.exp(-gate))
        silu = gate * sigma
        dgate_up_ref[:, :units] = (dact * up * sigma * (1.0 + gate * (1.0 - sigma))).astype(bf16)
        dgate_up_ref[:, units:] = (dact * silu).astype(bf16)
        act_ref[...] = (silu * up).astype(bf16)
        dnormed = dot(dgate_up_ref[...], weight, 1, 1)
        kept_ref[...] = dnormed[:rows]
        sent_ref[...] = dnormed[rows:].astype(bf16)
        out = dot(act_ref[...], down_weight, 1, 1)
        out_kept_ref[...] = out[:rows]
        out_sent_ref[...] = out[rows:].astype(bf16)


def feed(rows_list, weight):
    pairs = len(rows_list)
    rows, width = rows_list[0][0].shape
    units = weight.shape[1] // 3
    vmem = pl.BlockSpec(memory_space=pltpu.VMEM)
    halves = [jax.ShapeDtypeStruct((rows, width), f32), jax.ShapeDtypeStruct((rows, width), bf16)]
    shapes = (
        halves * 2 + [jax.ShapeDtypeStruct((2 * rows, 2 * units), bf16), jax.ShapeDtypeStruct((2 * rows, units), bf16)]
    ) * pairs
    ins = [part for group in rows_list for part in group]
    outs = pl.pallas_call(
        functools.partial(feed_kernel, pairs),
        in_specs=[vmem] * (len(ins) + 1),
        out_specs=[vmem] * len(shapes),
        out_shape=shapes,
        compiler_params=pltpu.CompilerParams(vmem_limit_bytes=48 * 2**20),
        cost_estimate=brief,
        name="feed",
    )(*ins, weight)
    return [outs[6 * pair:6 * pair + 6] for pair in range(pairs)]


def merged_heads(back_ref):
    heads = back_ref.shape[0]
    per_kv = heads // KV_HEADS
    rows = [back_ref[head, :HEAD_SIZE, :] for head in range(heads)]
    for number in (1, 2):
        here = slice(number * HEAD_SIZE, (number + 1) * HEAD_SIZE)
        for head in range(KV_HEADS):
            total = back_ref[head * per_kv, here, :].astype(f32)
            for copy in range(1, per_kv):
                total = total + back_ref[head * per_kv + copy, here, :].astype(f32)
            rows.append(total.astype(bf16))
    return rows


def back_kernel(core_ref, back_ref, weight_ref, mine_ref, other_ref, table_ref):
    for at, value in enumerate(merged_heads(back_ref)):
        table_ref[at * HEAD_SIZE:(at + 1) * HEAD_SIZE, :] = value
    rows = mine_ref.shape[0]
    both = dot(weight_ref[...], table_ref[...])
    low, high = both[:, :rows].T, both[:, rows:].T
    first = core_ref[0] == 0
    mine_ref[...] = jnp.where(first, low, high)
    other_ref[...] = jnp.where(first, high, low)


def input_terms(back, weight, core):
    vmem = pl.BlockSpec(memory_space=pltpu.VMEM)
    width, features = weight.shape
    rows = SPAN // 2
    return pl.pallas_call(
        back_kernel,
        in_specs=[pl.BlockSpec(memory_space=pltpu.SMEM), vmem, vmem],
        out_specs=[vmem] * 2,
        out_shape=[jax.ShapeDtypeStruct((rows, width), f32)] * 2,
        scratch_shapes=[pltpu.VMEM((features, SPAN), bf16)],
        compiler_params=pltpu.CompilerParams(vmem_limit_bytes=40 * 2**20),
        cost_estimate=brief,
        name="input_terms",
    )(core, back, weight)


tie = lax.optimization_barrier


def with_swapped(pieces):
    return [part for piece in pieces for part in (piece, swap(piece))]


def rms_factor(stream):
    return lax.rsqrt(jnp.mean(stream * stream, axis=-1, keepdims=True) + norm_eps)


def norm_backward(stream, factor, gain, dnormed):
    scaled = dnormed * gain
    return factor * scaled - stream * factor**3 * jnp.mean(scaled * stream, axis=-1, keepdims=True)


def body(
    hidden,
    document_index,
    attn_gain,
    q_weight,
    key_matrix,
    value_matrix,
    out_weight,
    mlp_gain,
    gate_weight,
    up_weight,
    down_weight,
    cotangent,
):
    count = lax.axis_size("fsdp")
    planes = count // PLANE
    f = lax.axis_index("fsdp")
    t = lax.axis_index("tp")
    place = f % SPANS
    plane_at = f // PLANE
    own, width = hidden.shape
    shard = q_weight.shape[1]
    q_heads = q_weight.shape[2] // HEAD_SIZE
    kv_heads = key_matrix.shape[2] // HEAD_SIZE
    per_kv = q_heads // kv_heads
    units = gate_weight.shape[2] // PLANE

    gains_own = jnp.stack([attn_gain[0], mlp_gain[0]], axis=-1)
    sent = head_cut(count, q_weight[0], key_matrix[0], value_matrix[0], gains_own)

    plane_place = f % PLANE
    cubes = count // SPANS
    cube_at = f // SPANS
    half = own // 2
    unit_set = jnp.concatenate(
        [w[0].reshape(shard, PLANE, units).transpose(1, 0, 2) for w in (gate_weight, up_weight, down_weight)],
        axis=-1,
    )
    lines = [list(range(first, count, PLANE)) for first in range(PLANE)]
    lines = [list(range(first, count, PLANE)) for first in range(PLANE)]
    p1, p2, p4 = hop(hidden, 1), hop(hidden, 2), hop(hidden, 4)
    head_set = exchange(sent, count).reshape(width, -1)
    out_far = [hop(out_weight[0], PLANE * k) for k in range(1, planes)]
    p4, document_index, cotangent = tie((p4, document_index, cotangent))
    p5, p6 = hop(p4, 1), hop(p4, 2)
    p3 = [hop(p2[:half], 1), hop(p1[half:], 2)]
    p7 = [hop(p6[:half], 1), hop(p5[half:], 2)]
    p3, p7 = jnp.concatenate(p3, axis=0), jnp.concatenate(p7, axis=0)
    unit_set, head_set = tie((unit_set, head_set))
    unit_own = exchange(unit_set, PLANE).reshape(PLANE * shard, 3 * units)

    seq_ids = lax.dynamic_slice_in_dim(document_index, f // SPANS * PACKED_LENGTH, PACKED_LENGTH)
    seq_index = jnp.arange(PACKED_LENGTH, dtype=jnp.int32)
    before = jnp.concatenate([jnp.full((1,), -1, jnp.int32), seq_ids[:-1]])
    starts = lax.cummax(jnp.where(seq_ids != before, seq_index, 0), axis=0)
    positions = (seq_index - starts).astype(f32)
    freq = rope_base ** (-2.0 * jnp.arange(HALF, dtype=f32) / HEAD_SIZE)
    angle = freq[:, None] * positions[None, :]
    cosine, sine = jnp.cos(angle), jnp.sin(angle)
    id_row = seq_ids[None, :]
    id_col = jnp.broadcast_to(seq_ids[:, None], (PACKED_LENGTH, 128))

    own_ids = lax.dynamic_slice_in_dim(document_index, f * SPAN + t * own, own)
    dstream = cotangent.astype(f32) * (own_ids != 0).astype(f32)[:, None]
    dmlp_own = dstream.astype(bf16)
    head_set, dmlp_own, cosine, sine, id_col, p3, out_far = tie(
        (head_set, dmlp_own, cosine, sine, id_col, p3, out_far)
    )
    pieces = with_swapped([hidden, p1, p2, p3, p4, p5, p6, p7])
    out_0 = jnp.zeros((planes,) + out_weight.shape[1:], bf16)
    for k, piece in enumerate([out_weight[0]] + out_far):
        out_0 = lax.dynamic_update_slice_in_dim(out_0, piece[None], plane_at ^ k, 0)
    out_1, out_2 = hop(out_0, 1), hop(out_0, 2)
    in_shard = jnp.concatenate([q_weight[0], key_matrix[0], value_matrix[0]], axis=1)

    places = jnp.stack([place, t]).astype(jnp.int32)

    normed, gains, q_t, k_t, v_t, q, key, v = project(pieces, head_set, places, cosine, sine)
    gain_a, gain_m = gains[0:1], gains[1:2]
    q_t, out_0, out_1, out_2, dmlp_own, unit_own = tie((q_t, out_0, out_1, out_2, dmlp_own, unit_own))
    unit_weight = lax.all_gather(unit_own, "fsdp", axis=0, tiled=True, axis_index_groups=lines)
    out_3 = hop(out_0, 3)
    dmlp_1, dmlp_2 = hop(dmlp_own, 1), hop(dmlp_own, 2)
    out_t, out_full, lse = attention_forward(q_t, key, v_t, id_row, id_col)
    out_t, dmlp_1, dmlp_2, out_3, dmlp_late = tie((out_t, dmlp_1, dmlp_2, out_3, dmlp_own))
    dmlp_3 = hop(dmlp_late, 3)
    attended = exchange(out_t, SPANS)
    attended, dmlp_3, in_shard = tie((attended, dmlp_3, in_shard))
    in_part = lax.all_gather(in_shard, "fsdp", axis=0, tiled=True)
    attended = attended.reshape(q_heads * HEAD_SIZE, SPAN)
    out_part = jnp.zeros((planes, PLANE, shard, out_0.shape[2]), bf16)
    for k, piece in enumerate((out_0, out_1, out_2, out_3)):
        out_part = lax.dynamic_update_slice_in_dim(out_part, piece[:, None], plane_place ^ k, 1)
    out_part = out_part.reshape(width, -1)

    stream = hidden.astype(f32)
    mine = lax.dynamic_slice_in_dim(attended, t * own, own, 1)
    other = lax.dynamic_slice_in_dim(attended, (1 - t) * own, own, 1)
    mid = stream + dot(mine, out_part, 0, 1) + swap(dot(other, out_part, 0, 1))

    factor_m = rms_factor(mid)
    normed_own = (mid * factor_m * gain_m).astype(bf16)
    dmlp = with_swapped([dmlp_own, dmlp_1, dmlp_2, dmlp_3])
    n1, n2 = hop(normed_own, 1), hop(normed_own, 2)
    n1, n2, normed_late = tie((n1, n2, normed_own))
    n3 = hop(normed_late, 3)
    normed_m = with_swapped([normed_own, n1, n2])
    second, third = feed([normed_m[2 * k:2 * k + 2] + dmlp[2 * k:2 * k + 2] for k in (1, 2)], unit_weight)
    second, third, n3 = tie((second, third, n3))
    normed_m += with_swapped([n3])
    dn_got = [swap(second[1]), swap(third[1])]
    first, fourth = feed([normed_m[2 * k:2 * k + 2] + dmlp[2 * k:2 * k + 2] for k in (0, 3)], unit_weight)
    first, fourth, dn_got = tie((first, fourth, dn_got))
    results = [first, second, third, fourth]
    dn_got = [swap(first[1])] + dn_got + [swap(fourth[1])]
    dn_pair = [result[0] + got.astype(f32) for result, got in zip(results, dn_got)]
    dn_low = [dn_pair[k].astype(bf16) for k in range(1, PLANE)]
    dn_low[2], acts = tie((dn_low[2], [result[5] for result in results]))
    dn_far = [dn_pair[0]] + [hop(low, k) for k, low in enumerate(dn_low, 1)]
    out_pair = [result[2] + swap(result[3]).astype(f32) for result in results]
    out_low = [out_pair[k].astype(bf16) for k in range(1, PLANE)]
    unit_term = unit_grads(normed_m, [result[4] for result in results], dmlp, acts)
    dn_far, out_low, in_part, unit_term = tie((dn_far, out_low, in_part, unit_term))
    unit_sum = lax.psum_scatter(unit_term, "fsdp", scatter_dimension=0, tiled=True, axis_index_groups=lines)
    out_far = [hop(low, k) for k, low in enumerate(out_low[:2], 1)]

    dnormed_m = dn_far[0]
    for far in dn_far[1:]:
        dnormed_m = dnormed_m + far.astype(f32)
    dmid = dstream + norm_backward(mid, factor_m, gain_m, dnormed_m)

    dattn = dmid.astype(bf16)
    dattn_other = swap(dattn)
    dattn = jnp.where(
        t == 0,
        jnp.concatenate([dattn, dattn_other], axis=0),
        jnp.concatenate([dattn_other, dattn], axis=0),
    )
    dout = dot(out_part, dattn, 0, 1).astype(bf16)
    dout = exchange(dout.reshape(SPANS, HEAD_SIZE, SPAN), SPANS)
    out_term = dot(dattn, attended, 0, 1).astype(bf16).reshape(planes, PLANE, shard, -1).transpose(1, 0, 2, 3)
    dout, out_term, out_low, out_far = tie((dout, out_term, out_low, out_far))
    out_term = exchange(out_term.reshape(PLANE, planes * shard, -1), PLANE)
    out_far += [hop(out_low[2], 3)]
    grads, head_low = attention_backward(
        q_t, q, k_t, key, v, dout, out_full, lse, id_row, id_col, cosine, sine, normed
    )
    grads, head_low, out_term, out_far, unit_sum = tie((grads, head_low, out_term, out_far, unit_sum))
    head_low = head_low.reshape(cubes, SPANS * shard, 3 * HEAD_SIZE)
    head_sum = lax.dynamic_index_in_dim(head_low, cube_at, 0, keepdims=False).astype(f32)
    for k in range(1, cubes):
        far = lax.dynamic_index_in_dim(head_low, cube_at ^ k, 0, keepdims=False)
        head_sum = head_sum + hop(far, SPANS * k).astype(f32)
    head_sum = head_sum.astype(bf16).reshape(SPANS, shard, 3 * HEAD_SIZE)

    back = exchange(grads, SPANS)
    unit_sum = unit_sum.reshape(PLANE, shard, 3 * units)
    unit_back = [lax.dynamic_index_in_dim(unit_sum, plane_place ^ k, 0, keepdims=False) for k in range(PLANE)]
    unit_back = [piece if k == 0 else hop(piece, k) for k, piece in enumerate(unit_back)]
    out_term = out_term.astype(f32).sum(axis=0).reshape(planes, shard, -1)
    out_grad = lax.dynamic_index_in_dim(out_term, plane_at, 0, keepdims=False)
    out_sums = []
    for k in range(1, planes):
        far = lax.dynamic_index_in_dim(out_term, plane_at ^ k, 0, keepdims=False)
        out_sums.append(far.astype(bf16))
    out_total = out_pair[0]
    for far in out_far:
        out_total = out_total + far.astype(f32)
    output = (mid + out_total).astype(bf16)
    back, _, unit_back, output, head_sum, first_sum = tie(
        (back, out_sums, unit_back, output, head_sum, hop(out_sums[0], PLANE))
    )
    out_sums = [first_sum] + [hop(far, PLANE * k) for k, far in enumerate(out_sums[1:], 2)]
    head_sums = exchange(head_sum, SPANS)
    for far in out_sums:
        out_grad = out_grad + far.astype(f32)
    mine, other = input_terms(back, in_part, t.reshape(1).astype(jnp.int32))
    dnormed_a = mine + swap(other)
    input_grad = dmid + norm_backward(stream, rms_factor(stream), gain_a, dnormed_a)
    input_grad, head_sums = tie((input_grad, head_sums))

    q_grad, k_grad, v_grad, gain_a_part = head_finish(head_sums, q_weight[0], key_matrix[0], value_matrix[0])

    gate_grad, up_grad, down_grad, gain_m_part = unit_finish(
        plane_place.reshape(1).astype(jnp.int32), unit_back, gate_weight[0], up_weight[0]
    )

    gain_parts = jnp.concatenate([gain_a_part, gain_m_part], axis=1).T
    gain_grads = (gain_parts + swap(gain_parts)) / jnp.stack([attn_gain[0], mlp_gain[0]]).astype(f32)
    return (
        output,
        input_grad,
        gain_grads[0:1],
        q_grad[None],
        k_grad[None],
        v_grad[None],
        out_grad[None],
        gain_grads[1:2],
        gate_grad[None],
        up_grad[None],
        down_grad[None],
    )


def solution(mesh):
    rows = P(("fsdp", "tp"), None)
    gain = P(None, "fsdp")
    weight = P(None, "fsdp", "tp")
    return jax.shard_map(
        body,
        mesh=mesh,
        in_specs=(rows, P(), gain, weight, weight, weight, weight, gain, weight, weight, weight, rows),
        out_specs=(rows, rows, gain, weight, weight, weight, weight, gain, weight, weight, weight),
        check_vma=False,
    )
```

```python
import functools
import math

import jax
import jax.numpy as jnp
from jax import lax
from jax.experimental import pallas as pl
from jax.experimental.pallas import tpu as pltpu
from jax.sharding import PartitionSpec as P

HEAD_SIZE = 96
HALF = HEAD_SIZE // 2
SPANS = 8
KV_HEADS = SPANS // 2
PLANE = 4
PACKED_LENGTH = 4096
SPAN = PACKED_LENGTH // SPANS

rope_base = 100000.0
norm_eps = 1e-05
masked_score = -1000000000.0
scale = HEAD_SIZE ** (-0.5)
scale_log2 = scale * math.log2(math.e)
bf16 = jnp.bfloat16
brief = pl.CostEstimate(flops=1024, bytes_accessed=1024, transcendentals=0)
f32 = jnp.float32


def dot(left, right, left_dim=1, right_dim=0):
    return lax.dot_general(
        left, right, (((left_dim,), (right_dim,)), ((), ())), preferred_element_type=f32
    )


def hop(value, distance):
    count = lax.axis_size("fsdp")
    return lax.ppermute(value, "fsdp", [(i, i ^ distance) for i in range(count)])


def swap(value):
    return lax.ppermute(value, "tp", [(0, 1), (1, 0)])


def groups_of(size):
    count = lax.axis_size("fsdp")
    return [list(range(first, first + size)) for first in range(0, count, size)]


def exchange(value, size):
    groups = None if size == lax.axis_size("fsdp") else groups_of(size)
    return lax.all_to_all(value, "fsdp", 0, 0, axis_index_groups=groups)


def head_cut_kernel(q_ref, k_ref, v_ref, gain_ref, out_ref):
    gains = gain_ref[...].astype(f32)
    for place in range(SPANS):
        parts = []
        for ref in (q_ref, k_ref, v_ref):
            head = place * ref.shape[1] // (SPANS * HEAD_SIZE)
            parts.append(ref[:, head * HEAD_SIZE:(head + 1) * HEAD_SIZE].astype(f32))
        cut = jnp.concatenate(parts + [gains], axis=1).astype(bf16)
        for first in range(0, out_ref.shape[0], SPANS):
            out_ref[first + place] = cut


def head_cut(count, q_weight, k_weight, v_weight, gains):
    vmem = pl.BlockSpec(memory_space=pltpu.VMEM)
    shard = q_weight.shape[0]
    return pl.pallas_call(
        head_cut_kernel,
        in_specs=[vmem] * 4,
        out_specs=vmem,
        out_shape=jax.ShapeDtypeStruct((count, shard, 3 * HEAD_SIZE + 2), bf16),
        compiler_params=pltpu.CompilerParams(vmem_limit_bytes=32 * 2**20),
        cost_estimate=brief,
        name="head_cut",
    )(q_weight, k_weight, v_weight, gains)


def project_kernel(*refs):
    pieces, (place_ref, head_ref, cos_ref, sin_ref) = refs[:2 * SPANS], refs[2 * SPANS:2 * SPANS + 4]
    normed_ref, gain_ref, q_t_ref, k_t_ref, v_t_ref, k_ref, v_ref = refs[2 * SPANS + 4:2 * SPANS + 11]
    in_buf, out_buf, in_sem, out_sem = refs[2 * SPANS + 11:]
    rows = pieces[0].shape[0]
    place, core = place_ref[0], place_ref[1]

    def fetch(pair, part):
        return pltpu.make_async_copy(
            pieces[2 * pair + part],
            in_buf.at[pair % 3, pl.ds(pl.multiple_of((core ^ part) * rows, rows), rows)],
            in_sem.at[pair % 3, part],
        )

    def store(pair):
        return pltpu.make_async_copy(out_buf.at[pair % 2], normed_ref.at[place ^ pair], out_sem.at[pair % 2])

    for pair in range(2):
        for part in range(2):
            fetch(pair, part).start()
    row = lax.broadcasted_iota(jnp.int32, (8, head_ref.shape[1]), 0)
    column = lax.broadcasted_iota(jnp.int32, (8, head_ref.shape[1]), 1)
    pick = (column == row + 3 * HEAD_SIZE).astype(f32).astype(bf16)
    gains = dot(pick, head_ref[...], 1, 1)
    gain = gains[0:1]
    gain_ref[...] = gains
    for pair in range(SPANS):
        for part in range(2):
            fetch(pair, part).wait()
        if pair + 2 < SPANS:
            for part in range(2):
                fetch(pair + 2, part).start()
        if pair >= 2:
            store(pair - 2).wait()
        x = in_buf[pair % 3].astype(f32)
        factor = lax.rsqrt(jnp.mean(x * x, axis=-1, keepdims=True) + norm_eps)
        normed = (x * factor * gain).astype(bf16)
        out_buf[pair % 2] = normed
        store(pair).start()
        product = dot(normed, head_ref[:, :3 * HEAD_SIZE]).T
        here = pl.ds(pl.multiple_of((place ^ pair) * 2 * rows, 2 * rows), 2 * rows)
        cosine, sine = cos_ref[:, here], sin_ref[:, here]
        for number, (t_ref, n_ref) in enumerate(((q_t_ref, None), (k_t_ref, k_ref))):
            first = product[number * HEAD_SIZE:number * HEAD_SIZE + HALF]
            second = product[number * HEAD_SIZE + HALF:(number + 1) * HEAD_SIZE]
            turned = jnp.concatenate(
                [first * cosine - second * sine, second * cosine + first * sine], axis=0
            )
            t_ref[:, here] = turned.astype(bf16)
            if n_ref is not None:
                n_ref[here, :] = turned.T.astype(bf16)
        value = product[2 * HEAD_SIZE:3 * HEAD_SIZE]
        v_t_ref[:, here] = value.astype(bf16)
        v_ref[here, :] = value.T.astype(bf16)
    for pair in range(SPANS - 2, SPANS):
        store(pair).wait()


def project(pieces, head_set, places, cosine, sine):
    rows, width = pieces[0].shape
    tokens = 2 * SPANS * rows
    vmem = pl.BlockSpec(memory_space=pltpu.VMEM)
    anywhere = pl.BlockSpec(memory_space=pl.ANY)
    return pl.pallas_call(
        project_kernel,
        in_specs=[anywhere] * len(pieces) + [pl.BlockSpec(memory_space=pltpu.SMEM), vmem, vmem, vmem],
        out_specs=[anywhere] + [vmem] * 6,
        out_shape=[
            jax.ShapeDtypeStruct((SPANS, 2 * rows, width), bf16),
            jax.ShapeDtypeStruct((8, width), f32),
        ]
        + [jax.ShapeDtypeStruct((HEAD_SIZE, tokens), bf16)] * 3
        + [jax.ShapeDtypeStruct((tokens, HEAD_SIZE), bf16)] * 2,
        scratch_shapes=[
            pltpu.VMEM((3, 2 * rows, width), bf16),
            pltpu.VMEM((2, 2 * rows, width), bf16),
            pltpu.SemaphoreType.DMA((3, 2)),
            pltpu.SemaphoreType.DMA((2,)),
        ],
        compiler_params=pltpu.CompilerParams(vmem_limit_bytes=56 * 2**20),
        cost_estimate=brief,
        name="project",
    )(*pieces, places, head_set, cosine, sine)


def widened(column):
    return jnp.concatenate([column] * (SPAN // column.shape[1]), axis=1)


def causal_tile():
    key_at = lax.broadcasted_iota(jnp.int32, (SPAN, SPAN), 0)
    query_at = lax.broadcasted_iota(jnp.int32, (SPAN, SPAN), 1)
    return key_at <= query_at


def forward_kernel(q_t_ref, k_ref, v_t_ref, id_row_ref, id_col_ref, out_ref, out_full_ref, lse_ref):
    block = pl.program_id(0)
    query = q_t_ref[...]
    id_row = id_row_ref[...]

    def step(at, carry, diagonal):
        best, total, result = carry
        keys = pl.ds(pl.multiple_of(at * SPAN, SPAN), SPAN)
        scores = dot(k_ref[keys, :], query) * scale_log2
        allowed = widened(id_col_ref[keys, :]) == id_row
        if diagonal:
            allowed = allowed & causal_tile()
        scores = jnp.where(allowed, scores, masked_score)
        larger = jnp.maximum(best, jnp.max(scores, axis=0, keepdims=True))
        weights = jnp.exp2(scores - larger)
        faded = jnp.exp2(best - larger)
        total = total * faded + jnp.sum(weights, axis=0, keepdims=True)
        result = result * faded + dot(v_t_ref[:, keys], weights.astype(bf16))
        return larger, total, result

    carry = (
        jnp.full((1, SPAN), masked_score, f32),
        jnp.zeros((1, SPAN), f32),
        jnp.zeros((HEAD_SIZE, SPAN), f32),
    )
    carry = lax.fori_loop(0, block, lambda at, c: step(at, c, False), carry)
    best, total, result = step(block, carry, True)
    result = result / total
    out_full_ref[...] = result
    out_ref[0] = result.astype(bf16)
    lse_ref[...] = best + jnp.log2(total)


def attention_forward(q_t, k, v_t, id_row, id_col):
    tokens = k.shape[0]
    whole = lambda array: pl.BlockSpec(array.shape, lambda i: (0, 0))
    return pl.pallas_call(
        forward_kernel,
        grid=(SPANS,),
        in_specs=[
            pl.BlockSpec((HEAD_SIZE, SPAN), lambda i: (0, i)),
            whole(k),
            whole(v_t),
            pl.BlockSpec((1, SPAN), lambda i: (0, i)),
            whole(id_col),
        ],
        out_specs=[
            pl.BlockSpec((1, HEAD_SIZE, SPAN), lambda i: (i, 0, 0)),
            pl.BlockSpec((HEAD_SIZE, SPAN), lambda i: (0, i)),
            pl.BlockSpec((1, SPAN), lambda i: (0, i)),
        ],
        out_shape=[
            jax.ShapeDtypeStruct((SPANS, HEAD_SIZE, SPAN), bf16),
            jax.ShapeDtypeStruct((HEAD_SIZE, tokens), f32),
            jax.ShapeDtypeStruct((1, tokens), f32),
        ],
        compiler_params=pltpu.CompilerParams(vmem_limit_bytes=40 * 2**20),
        cost_estimate=brief,
        name="attention_forward",
    )(q_t, k, v_t, id_row, id_col)


def backward_kernel(q_t_ref, k_t_ref, k_ref, v_ref, dout_ref, out_ref, lse_ref, id_row_ref, id_col_ref,
                    cos_ref, sin_ref, normed_ref, grad_ref, weight_grad_ref, delta_ref, dq_ref, sum_ref):
    block = pl.program_id(0)

    @pl.when(block == 0)
    def _():
        for at in range(SPANS):
            dout = dout_ref[at]
            here = slice(at * SPAN, (at + 1) * SPAN)
            delta_ref[:, here] = jnp.sum(dout.astype(f32) * out_ref[:, here], axis=0, keepdims=True)
        dq_ref[...] = jnp.zeros(dq_ref.shape, f32)
        sum_ref[...] = jnp.zeros(sum_ref.shape, f32)

    key_t, key, value = k_t_ref[...], k_ref[...], v_ref[...]
    id_col = widened(id_col_ref[...])

    def step(at, carry, diagonal):
        dkey, dvalue = carry
        rows = pl.ds(pl.multiple_of(at * SPAN, SPAN), SPAN)
        scores = dot(key, q_t_ref[:, rows]) * scale_log2 - lse_ref[:, rows]
        allowed = id_col == id_row_ref[:, rows]
        if diagonal:
            allowed = allowed & causal_tile()
        probs = jnp.exp2(jnp.where(allowed, scores, masked_score))
        dprobs = dot(value, dout_ref[at])
        dscores = (probs * (dprobs - delta_ref[:, rows])).astype(bf16)
        dvalue = dvalue + dot(dout_ref[at], probs.astype(bf16), 1, 1)
        dkey = dkey + dot(q_t_ref[:, rows], dscores, 1, 1)
        dq_ref[at] += dot(key_t, dscores)
        return dkey, dvalue

    zero = jnp.zeros((HEAD_SIZE, SPAN), f32)
    carry = step(block, (zero, zero), True)
    dkey, dvalue = lax.fori_loop(block + 1, SPANS, lambda at, c: step(at, c, False), carry)
    cosine, sine = cos_ref[...], sin_ref[...]
    for number, grad in enumerate((dq_ref[block], dkey)):
        first = grad[:HALF] * scale
        second = grad[HALF:] * scale
        turned = jnp.concatenate(
            [first * cosine + second * sine, second * cosine - first * sine], axis=0
        )
        grad_ref[0, number * HEAD_SIZE:(number + 1) * HEAD_SIZE, :] = turned.astype(bf16)
    grad_ref[0, 2 * HEAD_SIZE:, :] = dvalue.astype(bf16)
    sum_ref[...] += dot(grad_ref[0], normed_ref[0])

    @pl.when(block == SPANS - 1)
    def _():
        weight_grad_ref[...] = sum_ref[...].T.astype(bf16)


def attention_backward(q_t, k_t, k, v, dout, out, lse, id_row, id_col, cosine, sine, normed):
    tokens = k.shape[0]
    width = normed.shape[2]
    whole = lambda array: pl.BlockSpec(array.shape, lambda i: (0,) * array.ndim)
    wide = pl.BlockSpec((HEAD_SIZE, SPAN), lambda i: (0, i))
    tall = pl.BlockSpec((SPAN, HEAD_SIZE), lambda i: (i, 0))
    table = pl.BlockSpec((HALF, SPAN), lambda i: (0, i))
    return pl.pallas_call(
        backward_kernel,
        grid=(SPANS,),
        in_specs=[
            whole(q_t), wide, tall, tall, whole(dout), whole(out), whole(lse), whole(id_row),
            pl.BlockSpec((SPAN, id_col.shape[1]), lambda i: (i, 0)), table, table,
            pl.BlockSpec((1, SPAN, width), lambda i: (i, 0, 0)),
        ],
        out_specs=[
            pl.BlockSpec((1, 3 * HEAD_SIZE, SPAN), lambda i: (i, 0, 0)),
            pl.BlockSpec((width, 3 * HEAD_SIZE), lambda i: (0, 0)),
        ],
        out_shape=[
            jax.ShapeDtypeStruct((SPANS, 3 * HEAD_SIZE, SPAN), bf16),
            jax.ShapeDtypeStruct((width, 3 * HEAD_SIZE), bf16),
        ],
        scratch_shapes=[
            pltpu.VMEM((1, tokens), f32),
            pltpu.VMEM((SPANS, HEAD_SIZE, SPAN), f32),
            pltpu.VMEM((3 * HEAD_SIZE, width), f32),
        ],
        compiler_params=pltpu.CompilerParams(vmem_limit_bytes=56 * 2**20),
        cost_estimate=brief,
        name="attention_backward",
    )(q_t, k_t, k, v, dout, out, lse, id_row, id_col, cosine, sine, normed)


def head_finish_kernel(sum_ref, q_ref, k_ref, v_ref, q_out, k_out, v_out, product_ref):
    product = jnp.zeros(product_ref.shape, f32)
    for number, (ref, out) in enumerate(((q_ref, q_out), (k_ref, k_out), (v_ref, v_out))):
        heads = out.shape[1] // HEAD_SIZE
        copies = SPANS // heads
        grads = []
        for head in range(heads):
            grad = sum_ref[head * copies].astype(f32)
            for other in range(1, copies):
                grad = grad + sum_ref[head * copies + other].astype(f32)
            grads.append(grad[:, number * HEAD_SIZE:(number + 1) * HEAD_SIZE])
        grad = jnp.concatenate(grads, axis=1)
        out[...] = grad
        product = product + jnp.sum(grad * ref[...].astype(f32), axis=1, keepdims=True)
    product_ref[...] = product


def head_finish(sums, q_weight, k_weight, v_weight):
    vmem = pl.BlockSpec(memory_space=pltpu.VMEM)
    return pl.pallas_call(
        head_finish_kernel,
        in_specs=[vmem] * 4,
        out_specs=[vmem] * 4,
        out_shape=[jax.ShapeDtypeStruct(w.shape, f32) for w in (q_weight, k_weight, v_weight)]
        + [jax.ShapeDtypeStruct((q_weight.shape[0], 1), f32)],
        compiler_params=pltpu.CompilerParams(vmem_limit_bytes=32 * 2**20),
        cost_estimate=brief,
        name="head_finish",
    )(sums, q_weight, k_weight, v_weight)


def unit_finish_kernel(place_ref, *refs):
    piece_refs, (gate_w_ref, up_w_ref, gate_out, up_out, down_out, product_ref) = refs[:PLANE], refs[PLANE:]
    units = gate_out.shape[1] // PLANE
    for link, piece_ref in enumerate(piece_refs):
        here = pl.ds(pl.multiple_of((place_ref[0] ^ link) * units, units), units)
        for number, out in enumerate((gate_out, up_out, down_out)):
            out[:, here] = piece_ref[:, number * units:(number + 1) * units].astype(f32)
    product_ref[...] = jnp.sum(
        gate_out[...] * gate_w_ref[...].astype(f32) + up_out[...] * up_w_ref[...].astype(f32), axis=1, keepdims=True
    )


def unit_finish(place, pieces, gate_weight, up_weight):
    vmem = pl.BlockSpec(memory_space=pltpu.VMEM)
    return pl.pallas_call(
        unit_finish_kernel,
        in_specs=[pl.BlockSpec(memory_space=pltpu.SMEM)] + [vmem] * (PLANE + 2),
        out_specs=[vmem] * 4,
        out_shape=[jax.ShapeDtypeStruct(gate_weight.shape, f32)] * 3
        + [jax.ShapeDtypeStruct((gate_weight.shape[0], 1), f32)],
        compiler_params=pltpu.CompilerParams(vmem_limit_bytes=32 * 2**20),
        name="unit_finish",
    )(place, *pieces, gate_weight, up_weight)


def unit_grad_kernel(*refs):
    tables, out_ref = (refs[:3 * PLANE], refs[3 * PLANE:6 * PLANE]), refs[6 * PLANE]
    column = 0
    for table in tables:
        total = None
        for k, right in enumerate(table[2 * PLANE:]):
            left = jnp.concatenate([table[2 * k][...], table[2 * k + 1][...]], axis=0)
            term = dot(left, right[...], 0, 0)
            total = term if total is None else total + term
        out_ref[:, column:column + total.shape[1]] = total.astype(bf16)
        column += total.shape[1]


def unit_grads(normed, dgate_up, dout, act):
    tokens, width = normed[0].shape
    rows = width // 4
    whole = lambda array: pl.BlockSpec(array.shape, lambda i: (0, 0))
    left = [pl.BlockSpec((tokens, rows), lambda i: (0, i))] * (2 * PLANE)
    columns = dgate_up[0].shape[1] + act[0].shape[1]
    return pl.pallas_call(
        unit_grad_kernel,
        grid=(width // rows,),
        in_specs=left + [whole(part) for part in dgate_up] + left + [whole(part) for part in act],
        out_specs=pl.BlockSpec((rows, columns), lambda i: (i, 0)),
        out_shape=jax.ShapeDtypeStruct((width, columns), bf16),
        compiler_params=pltpu.CompilerParams(vmem_limit_bytes=48 * 2**20),
        cost_estimate=brief,
        name="unit_grads",
    )(*normed, *dgate_up, *dout, *act)


def feed_kernel(pairs, *refs):
    ins, weight_ref, refs = refs[:4 * pairs], refs[4 * pairs], refs[4 * pairs + 1:]
    units = weight_ref.shape[1] // 3
    weight = weight_ref[:, :2 * units]
    down_weight = weight_ref[:, 2 * units:]
    for pair in range(pairs):
        own_ref, other_ref, d_own_ref, d_other_ref = ins[4 * pair:4 * pair + 4]
        kept_ref, sent_ref, out_kept_ref, out_sent_ref, dgate_up_ref, act_ref = refs[6 * pair:6 * pair + 6]
        rows = own_ref.shape[0]
        gate_up = dot(jnp.concatenate([own_ref[...], other_ref[...]], axis=0), weight)
        dact = dot(jnp.concatenate([d_own_ref[...], d_other_ref[...]], axis=0), down_weight)
        gate, up = gate_up[:, :units], gate_up[:, units:]
        sigma = 1.0 / (1.0 + jnp.exp(-gate))
        silu = gate * sigma
        dgate_up_ref[:, :units] = (dact * up * sigma * (1.0 + gate * (1.0 - sigma))).astype(bf16)
        dgate_up_ref[:, units:] = (dact * silu).astype(bf16)
        act_ref[...] = (silu * up).astype(bf16)
        dnormed = dot(dgate_up_ref[...], weight, 1, 1)
        kept_ref[...] = dnormed[:rows]
        sent_ref[...] = dnormed[rows:].astype(bf16)
        out = dot(act_ref[...], down_weight, 1, 1)
        out_kept_ref[...] = out[:rows]
        out_sent_ref[...] = out[rows:].astype(bf16)


def feed(rows_list, weight):
    pairs = len(rows_list)
    rows, width = rows_list[0][0].shape
    units = weight.shape[1] // 3
    vmem = pl.BlockSpec(memory_space=pltpu.VMEM)
    halves = [jax.ShapeDtypeStruct((rows, width), f32), jax.ShapeDtypeStruct((rows, width), bf16)]
    shapes = (
        halves * 2 + [jax.ShapeDtypeStruct((2 * rows, 2 * units), bf16), jax.ShapeDtypeStruct((2 * rows, units), bf16)]
    ) * pairs
    ins = [part for group in rows_list for part in group]
    outs = pl.pallas_call(
        functools.partial(feed_kernel, pairs),
        in_specs=[vmem] * (len(ins) + 1),
        out_specs=[vmem] * len(shapes),
        out_shape=shapes,
        compiler_params=pltpu.CompilerParams(vmem_limit_bytes=48 * 2**20),
        cost_estimate=brief,
        name="feed",
    )(*ins, weight)
    return [outs[6 * pair:6 * pair + 6] for pair in range(pairs)]


def merged_heads(back_ref):
    heads = back_ref.shape[0]
    per_kv = heads // KV_HEADS
    rows = [back_ref[head, :HEAD_SIZE, :] for head in range(heads)]
    for number in (1, 2):
        here = slice(number * HEAD_SIZE, (number + 1) * HEAD_SIZE)
        for head in range(KV_HEADS):
            total = back_ref[head * per_kv, here, :].astype(f32)
            for copy in range(1, per_kv):
                total = total + back_ref[head * per_kv + copy, here, :].astype(f32)
            rows.append(total.astype(bf16))
    return rows


def back_kernel(core_ref, back_ref, weight_ref, mine_ref, other_ref, table_ref):
    for at, value in enumerate(merged_heads(back_ref)):
        table_ref[at * HEAD_SIZE:(at + 1) * HEAD_SIZE, :] = value
    rows = mine_ref.shape[0]
    both = dot(weight_ref[...], table_ref[...])
    low, high = both[:, :rows].T, both[:, rows:].T
    first = core_ref[0] == 0
    mine_ref[...] = jnp.where(first, low, high)
    other_ref[...] = jnp.where(first, high, low)


def input_terms(back, weight, core):
    vmem = pl.BlockSpec(memory_space=pltpu.VMEM)
    width, features = weight.shape
    rows = SPAN // 2
    return pl.pallas_call(
        back_kernel,
        in_specs=[pl.BlockSpec(memory_space=pltpu.SMEM), vmem, vmem],
        out_specs=[vmem] * 2,
        out_shape=[jax.ShapeDtypeStruct((rows, width), f32)] * 2,
        scratch_shapes=[pltpu.VMEM((features, SPAN), bf16)],
        compiler_params=pltpu.CompilerParams(vmem_limit_bytes=40 * 2**20),
        cost_estimate=brief,
        name="input_terms",
    )(core, back, weight)


tie = lax.optimization_barrier


def with_swapped(pieces):
    return [part for piece in pieces for part in (piece, swap(piece))]


def rms_factor(stream):
    return lax.rsqrt(jnp.mean(stream * stream, axis=-1, keepdims=True) + norm_eps)


def norm_backward(stream, factor, gain, dnormed):
    scaled = dnormed * gain
    return factor * scaled - stream * factor**3 * jnp.mean(scaled * stream, axis=-1, keepdims=True)


def body(
    hidden,
    document_index,
    attn_gain,
    q_weight,
    key_matrix,
    value_matrix,
    out_weight,
    mlp_gain,
    gate_weight,
    up_weight,
    down_weight,
    cotangent,
):
    count = lax.axis_size("fsdp")
    planes = count // PLANE
    f = lax.axis_index("fsdp")
    t = lax.axis_index("tp")
    place = f % SPANS
    plane_at = f // PLANE
    own, width = hidden.shape
    shard = q_weight.shape[1]
    q_heads = q_weight.shape[2] // HEAD_SIZE
    kv_heads = key_matrix.shape[2] // HEAD_SIZE
    per_kv = q_heads // kv_heads
    units = gate_weight.shape[2] // PLANE

    gains_own = jnp.stack([attn_gain[0], mlp_gain[0]], axis=-1)
    sent = head_cut(count, q_weight[0], key_matrix[0], value_matrix[0], gains_own)

    plane_place = f % PLANE
    cubes = count // SPANS
    cube_at = f // SPANS
    half = own // 2
    unit_set = jnp.concatenate(
        [w[0].reshape(shard, PLANE, units).transpose(1, 0, 2) for w in (gate_weight, up_weight, down_weight)],
        axis=-1,
    )
    lines = [list(range(first, count, PLANE)) for first in range(PLANE)]
    lines = [list(range(first, count, PLANE)) for first in range(PLANE)]
    p1, p2, p4 = hop(hidden, 1), hop(hidden, 2), hop(hidden, 4)
    head_set = exchange(sent, count).reshape(width, -1)
    out_far = [hop(out_weight[0], PLANE * k) for k in range(1, planes)]
    p4, document_index, cotangent = tie((p4, document_index, cotangent))
    p5, p6 = hop(p4, 1), hop(p4, 2)
    p3 = [hop(p2[:half], 1), hop(p1[half:], 2)]
    p7 = [hop(p6[:half], 1), hop(p5[half:], 2)]
    p3, p7 = jnp.concatenate(p3, axis=0), jnp.concatenate(p7, axis=0)
    unit_set, head_set = tie((unit_set, head_set))
    unit_own = exchange(unit_set, PLANE).reshape(PLANE * shard, 3 * units)

    seq_ids = lax.dynamic_slice_in_dim(document_index, f // SPANS * PACKED_LENGTH, PACKED_LENGTH)
    seq_index = jnp.arange(PACKED_LENGTH, dtype=jnp.int32)
    before = jnp.concatenate([jnp.full((1,), -1, jnp.int32), seq_ids[:-1]])
    starts = lax.cummax(jnp.where(seq_ids != before, seq_index, 0), axis=0)
    positions = (seq_index - starts).astype(f32)
    freq = rope_base ** (-2.0 * jnp.arange(HALF, dtype=f32) / HEAD_SIZE)
    angle = freq[:, None] * positions[None, :]
    cosine, sine = jnp.cos(angle), jnp.sin(angle)
    id_row = seq_ids[None, :]
    id_col = jnp.broadcast_to(seq_ids[:, None], (PACKED_LENGTH, 128))

    own_ids = lax.dynamic_slice_in_dim(document_index, f * SPAN + t * own, own)
    dstream = cotangent.astype(f32) * (own_ids != 0).astype(f32)[:, None]
    dmlp_own = dstream.astype(bf16)
    head_set, dmlp_own, cosine, sine, id_col, p3, out_far = tie(
        (head_set, dmlp_own, cosine, sine, id_col, p3, out_far)
    )
    pieces = with_swapped([hidden, p1, p2, p3, p4, p5, p6, p7])
    out_0 = jnp.zeros((planes,) + out_weight.shape[1:], bf16)
    for k, piece in enumerate([out_weight[0]] + out_far):
        out_0 = lax.dynamic_update_slice_in_dim(out_0, piece[None], plane_at ^ k, 0)
    out_1, out_2 = hop(out_0, 1), hop(out_0, 2)
    in_shard = jnp.concatenate([q_weight[0], key_matrix[0], value_matrix[0]], axis=1)

    places = jnp.stack([place, t]).astype(jnp.int32)

    normed, gains, q_t, k_t, v_t, key, v = project(pieces, head_set, places, cosine, sine)
    gain_a, gain_m = gains[0:1], gains[1:2]
    q_t, out_0, out_1, out_2, dmlp_own, unit_own = tie((q_t, out_0, out_1, out_2, dmlp_own, unit_own))
    unit_weight = lax.all_gather(unit_own, "fsdp", axis=0, tiled=True, axis_index_groups=lines)
    out_3 = hop(out_0, 3)
    dmlp_1, dmlp_2 = hop(dmlp_own, 1), hop(dmlp_own, 2)
    out_t, out_full, lse = attention_forward(q_t, key, v_t, id_row, id_col)
    out_t, dmlp_1, dmlp_2, out_3, dmlp_late = tie((out_t, dmlp_1, dmlp_2, out_3, dmlp_own))
    dmlp_3 = hop(dmlp_late, 3)
    attended = exchange(out_t, SPANS)
    attended, dmlp_3, in_shard = tie((attended, dmlp_3, in_shard))
    in_part = lax.all_gather(in_shard, "fsdp", axis=0, tiled=True)
    attended = attended.reshape(q_heads * HEAD_SIZE, SPAN)
    out_part = jnp.zeros((planes, PLANE, shard, out_0.shape[2]), bf16)
    for k, piece in enumerate((out_0, out_1, out_2, out_3)):
        out_part = lax.dynamic_update_slice_in_dim(out_part, piece[:, None], plane_place ^ k, 1)
    out_part = out_part.reshape(width, -1)

    stream = hidden.astype(f32)
    mine = lax.dynamic_slice_in_dim(attended, t * own, own, 1)
    other = lax.dynamic_slice_in_dim(attended, (1 - t) * own, own, 1)
    mid = stream + dot(mine, out_part, 0, 1) + swap(dot(other, out_part, 0, 1))

    factor_m = rms_factor(mid)
    normed_own = (mid * factor_m * gain_m).astype(bf16)
    dmlp = with_swapped([dmlp_own, dmlp_1, dmlp_2, dmlp_3])
    n1, n2 = hop(normed_own, 1), hop(normed_own, 2)
    n1, n2, normed_late = tie((n1, n2, normed_own))
    n3 = hop(normed_late, 3)
    normed_m = with_swapped([normed_own, n1, n2])
    second, third = feed([normed_m[2 * k:2 * k + 2] + dmlp[2 * k:2 * k + 2] for k in (1, 2)], unit_weight)
    second, third, n3 = tie((second, third, n3))
    normed_m += with_swapped([n3])
    dn_got = [swap(second[1]), swap(third[1])]
    first, fourth = feed([normed_m[2 * k:2 * k + 2] + dmlp[2 * k:2 * k + 2] for k in (0, 3)], unit_weight)
    first, fourth, dn_got = tie((first, fourth, dn_got))
    results = [first, second, third, fourth]
    dn_got = [swap(first[1])] + dn_got + [swap(fourth[1])]
    dn_pair = [result[0] + got.astype(f32) for result, got in zip(results, dn_got)]
    dn_low = [dn_pair[k].astype(bf16) for k in range(1, PLANE)]
    dn_low[2], acts = tie((dn_low[2], [result[5] for result in results]))
    dn_far = [dn_pair[0]] + [hop(low, k) for k, low in enumerate(dn_low, 1)]
    out_pair = [result[2] + swap(result[3]).astype(f32) for result in results]
    out_low = [out_pair[k].astype(bf16) for k in range(1, PLANE)]
    unit_term = unit_grads(normed_m, [result[4] for result in results], dmlp, acts)
    dn_far, out_low, in_part, unit_term = tie((dn_far, out_low, in_part, unit_term))
    unit_sum = lax.psum_scatter(unit_term, "fsdp", scatter_dimension=0, tiled=True, axis_index_groups=lines)
    out_far = [hop(low, k) for k, low in enumerate(out_low[:2], 1)]

    dnormed_m = dn_far[0]
    for far in dn_far[1:]:
        dnormed_m = dnormed_m + far.astype(f32)
    dmid = dstream + norm_backward(mid, factor_m, gain_m, dnormed_m)

    dattn = dmid.astype(bf16)
    dattn_other = swap(dattn)
    dattn = jnp.where(
        t == 0,
        jnp.concatenate([dattn, dattn_other], axis=0),
        jnp.concatenate([dattn_other, dattn], axis=0),
    )
    dout = dot(out_part, dattn, 0, 1).astype(bf16)
    dout = exchange(dout.reshape(SPANS, HEAD_SIZE, SPAN), SPANS)
    out_term = dot(dattn, attended, 0, 1).astype(bf16).reshape(planes, PLANE, shard, -1).transpose(1, 0, 2, 3)
    dout, out_term, out_low, out_far = tie((dout, out_term, out_low, out_far))
    out_term = exchange(out_term.reshape(PLANE, planes * shard, -1), PLANE)
    out_far += [hop(out_low[2], 3)]
    grads, head_low = attention_backward(
        q_t, k_t, key, v, dout, out_full, lse, id_row, id_col, cosine, sine, normed
    )
    grads, head_low, out_term, out_far, unit_sum = tie((grads, head_low, out_term, out_far, unit_sum))
    head_low = head_low.reshape(cubes, SPANS * shard, 3 * HEAD_SIZE)
    head_sum = lax.dynamic_index_in_dim(head_low, cube_at, 0, keepdims=False).astype(f32)
    for k in range(1, cubes):
        far = lax.dynamic_index_in_dim(head_low, cube_at ^ k, 0, keepdims=False)
        head_sum = head_sum + hop(far, SPANS * k).astype(f32)
    head_sum = head_sum.astype(bf16).reshape(SPANS, shard, 3 * HEAD_SIZE)

    back = exchange(grads, SPANS)
    unit_sum = unit_sum.reshape(PLANE, shard, 3 * units)
    unit_back = [lax.dynamic_index_in_dim(unit_sum, plane_place ^ k, 0, keepdims=False) for k in range(PLANE)]
    unit_back = [piece if k == 0 else hop(piece, k) for k, piece in enumerate(unit_back)]
    out_term = out_term.astype(f32).sum(axis=0).reshape(planes, shard, -1)
    out_grad = lax.dynamic_index_in_dim(out_term, plane_at, 0, keepdims=False)
    out_sums = []
    for k in range(1, planes):
        far = lax.dynamic_index_in_dim(out_term, plane_at ^ k, 0, keepdims=False)
        out_sums.append(far.astype(bf16))
    out_total = out_pair[0]
    for far in out_far:
        out_total = out_total + far.astype(f32)
    output = (mid + out_total).astype(bf16)
    back, _, unit_back, output, head_sum, first_sum = tie(
        (back, out_sums, unit_back, output, head_sum, hop(out_sums[0], PLANE))
    )
    out_sums = [first_sum] + [hop(far, PLANE * k) for k, far in enumerate(out_sums[1:], 2)]
    head_sums = exchange(head_sum, SPANS)
    for far in out_sums:
        out_grad = out_grad + far.astype(f32)
    mine, other = input_terms(back, in_part, t.reshape(1).astype(jnp.int32))
    dnormed_a = mine + swap(other)
    input_grad = dmid + norm_backward(stream, rms_factor(stream), gain_a, dnormed_a)
    input_grad, head_sums = tie((input_grad, head_sums))

    q_grad, k_grad, v_grad, gain_a_part = head_finish(head_sums, q_weight[0], key_matrix[0], value_matrix[0])

    gate_grad, up_grad, down_grad, gain_m_part = unit_finish(
        plane_place.reshape(1).astype(jnp.int32), unit_back, gate_weight[0], up_weight[0]
    )

    gain_parts = jnp.concatenate([gain_a_part, gain_m_part], axis=1).T
    gain_grads = (gain_parts + swap(gain_parts)) / jnp.stack([attn_gain[0], mlp_gain[0]]).astype(f32)
    return (
        output,
        input_grad,
        gain_grads[0:1],
        q_grad[None],
        k_grad[None],
        v_grad[None],
        out_grad[None],
        gain_grads[1:2],
        gate_grad[None],
        up_grad[None],
        down_grad[None],
    )


def solution(mesh):
    rows = P(("fsdp", "tp"), None)
    gain = P(None, "fsdp")
    weight = P(None, "fsdp", "tp")
    return jax.shard_map(
        body,
        mesh=mesh,
        in_specs=(rows, P(), gain, weight, weight, weight, weight, gain, weight, weight, weight, rows),
        out_specs=(rows, rows, gain, weight, weight, weight, weight, gain, weight, weight, weight),
        check_vma=False,
    )
```
